32 devices in a mesh: rows: 8 (over z, core), cols: 4 (over y, x).
Axes of the slice: x: 2, y: 2, z: 4, core: 2. Of those that a mesh axis runs over, the one named last changes fastest.
Arguments:
- matrix: float32 [32768, 4096], P('rows', 'cols'), may hold values from -80 to 80
- mixers: float32 [8, 128, 128], replicated, may hold values from -0.001953125 to 0.001953125
- bucket_pair: int32 [256, 2], P('rows'), may hold values from 0 to 63, all different within a row; in each aligned block of 32 rows (0 to 31, 32 to 63, ...) at most 2 rows name the same one
- mixer_index: int32 [256], P('rows'), may hold values from 0 to 7
- sign_seed: int32 [256], P('rows'), may hold values from 0 to 1073741823
Outputs:
- projected: float32 [256, 4096], P('rows', 'cols')
The draws below stay inside these ranges and needn't reach their ends.
Inputs may be any that keep to these rules, and one draw needn't show every extreme that they name: `bucket_pair`: the two buckets of a tile differ; among the 32 tiles of one device no bucket is named more than 2 times, a bound that some block reaches.
All inputs are finite; a program needn't handle non-finite values.
Results may differ from the reference program's by a relative error of at most 0.0012.
Values may be sent and summed in bfloat16 or wider, within the bound.
No kernel may reach another device: no remote copies, remote signals or barrier semaphores. Data moves between devices by JAX's collectives and lax.ppermute only.
A program may use at most 128 MiB of HBM per device.

```python
import math
import jax
import jax.numpy as jnp
import numpy as np
from jax import lax

NCOL = 4096
SKETCH = 8192
TILE = 128
P_SIZE = 256
MIXERS = 8
MOST = 2
TILES_DEV = 32
NB = 64
NT = 256
ROWS_ALL = 32768


def draw_matrix(key, part):
    base_key = jax.random.fold_in(key, 11)
    first_key = jax.random.fold_in(base_key, 0)
    base = jax.random.normal(first_key, (ROWS_ALL, NCOL), jnp.float32)
    echo = jnp.tile(base[:, :P_SIZE], (1, NCOL // P_SIZE))
    column = jnp.arange(NCOL, dtype=jnp.int32)
    keep_mask = (column >= P_SIZE).astype(jnp.float32)
    result = base + 0.8 * echo * keep_mask[None, :]
    return jnp.clip(result, -80.0, 80.0)


def set_ends(array, rng, smallest, largest):
    longest = array.shape.index(max(array.shape))
    spots = []
    for shift in (0, 1):
        where = [jax.random.randint(jax.random.fold_in(rng, axis), (), 0, length) for axis, length in enumerate(array.shape)]
        where[longest] = (where[longest] + shift) % array.shape[longest]
        spots.append(tuple(where))
    return array.at[spots[0]].set(smallest).at[spots[1]].set(largest)


def shared_out(key, own, number, rows, amount, top, bound, skew):
    order = jax.random.permutation(key, amount)
    crowded, usual = portions_of(amount, rows * top, bound, skew, True), portions_of(amount, rows * top, bound, skew, False)
    places = jnp.arange(amount)

    def named(lengths, rotation):
        used = int((lengths > 0).sum())
        fixed = max(1, used // 4)
        passed = fixed + (places - fixed + rotation * (used - fixed)) % max(1, amount - fixed)
        return jnp.zeros((amount,), jnp.int32).at[order[jnp.where(places < fixed, places, passed)]].set(jnp.asarray(lengths, jnp.int32))

    lengths = jnp.where(number % 4 == 0, named(crowded, number // 4), named(usual, number - number // 4 - 1))
    mixed = jax.random.permutation(jax.random.fold_in(own, 3), amount)
    source_of, receiver = mixed[0:amount // 2 * 2:2], mixed[1:amount // 2 * 2:2]
    margin = jnp.minimum(lengths[source_of] - 1, bound - lengths[receiver]) // 2
    margin = jnp.where((source_of == order[0]) | (receiver == order[0]) | (lengths[receiver] == 0), 0, jnp.maximum(margin, 0))
    passed = jax.random.randint(jax.random.fold_in(own, 4), (amount // 2,), 0, 1 << 20) % (margin + 1)
    lengths = lengths.at[source_of].add(-passed).at[receiver].add(passed)
    items = jnp.searchsorted(jnp.cumsum(lengths), jnp.arange(rows * top), side="right").astype(jnp.int32)
    listing = items.reshape(top, rows).T
    listing = listing[jax.random.permutation(jax.random.fold_in(own, 1), rows)]
    rotation = jax.random.randint(jax.random.fold_in(own, 2), (rows, 1), 0, top)
    return jnp.take_along_axis(listing, (jnp.arange(top)[None, :] + rotation) % top, axis=1)


def portions_of(count, total, limit, skew, full):
    portions = [(1 << 20) // math.isqrt(standing ** skew) + 1 for standing in range(1, count + 1)]
    largest = limit if full else min(limit, max(-(-total // count), total * portions[0] // sum(portions)))
    least = 1 if total - largest >= count - 1 else 0
    given, spare = [largest] + [least] * (count - 1), total - largest - least * (count - 1)
    while spare > 0:
        free = [i for i in range(1, count) if given[i] < largest] or [i for i in range(1, count) if given[i] < limit]
        mass, remaining = sum([portions[i] for i in free]), spare
        for i in free:
            extra = min(limit - given[i], max(1, remaining * portions[i] // mass), spare)
            given[i] = given[i] + extra
            spare = spare - extra
    return np.array(given)


def bell_draw(key, dims, spread, reach, held_as=jnp.bfloat16):
    return jnp.clip(spread * jax.random.normal(key, dims, jnp.float32), -reach, reach).astype(held_as)


def setup_inputs(seed: int = 0) -> dict:
    key_of = jax.random.split(jax.random.key(seed), 6)
    matrix = draw_matrix(jax.random.fold_in(key_of[5], 71), 0)
    mixers = bell_draw(key_of[1], (MIXERS, TILE, TILE), (TILE * TILE * 2 * NT) ** -0.5, 0.001953125, jnp.float32)
    bucket_pair_keys = jax.random.split(jax.random.fold_in(key_of[2], 1), NT // TILES_DEV)
    bucket_pair_turns = jax.random.permutation(jax.random.fold_in(key_of[2], 3), NT // TILES_DEV)
    bucket_pair = jax.vmap(lambda own, number: shared_out(jax.random.fold_in(key_of[2], 2), own, number, TILES_DEV, NB, 2, MOST, 2))(bucket_pair_keys, bucket_pair_turns).reshape((NT, 2))
    mixer_index = set_ends(jax.random.randint(key_of[3], (NT,), 0, MIXERS), jax.random.fold_in(key_of[3], 1), 0, MIXERS - 1).astype(jnp.int32)
    sign_seed = set_ends(jax.random.randint(key_of[4], (NT,), 0, 1073741824), jax.random.fold_in(key_of[4], 1), 0, 1073741823).astype(jnp.int32)
    return dict(matrix=matrix, mixers=mixers, bucket_pair=bucket_pair, mixer_index=mixer_index, sign_seed=sign_seed)


def row_signs(seed_vals):
    position = jnp.arange(TILE, dtype=jnp.int32)
    hashed = (seed_vals[:, None] ^ position[None, :] * 40503) * 69069
    hashed_bit = hashed >> 16 & 1
    return (1 - 2 * hashed_bit).astype(jnp.float32)

def tile_flips(seed_vals):
    return (1 - 2 * (seed_vals >> 29 & 1)).astype(jnp.float32)

def reference(matrix, mixers, bucket_pair, mixer_index, sign_seed):
    blocks = matrix.reshape(NT, TILE, NCOL)
    row_sign = row_signs(sign_seed)
    tile_flip = tile_flips(sign_seed)

    def add_tile(totals, per_tile):
        block, signs_here, which, pair, flip = per_tile
        mixed_tile = jnp.dot(mixers[which].astype(jnp.float32), (signs_here[:, None] * block).astype(jnp.float32), precision=lax.Precision.HIGHEST, preferred_element_type=jnp.float32).astype(jnp.bfloat16)
        widened = mixed_tile.astype(jnp.float32)
        totals = totals.at[pair[0]].add(widened)
        totals = totals.at[pair[1]].add(flip * widened)
        return (totals, None)
    start = jnp.zeros((NB, TILE, NCOL), jnp.float32)
    totals, unused = lax.scan(add_tile, start, (blocks, row_sign, mixer_index, bucket_pair, tile_flip))
    sketch = totals.reshape(SKETCH, NCOL)
    panel_cols = sketch[:, :P_SIZE]
    gram_total = jnp.dot(panel_cols.T.astype(jnp.float32), panel_cols.astype(jnp.float32), precision=lax.Precision.HIGHEST, preferred_element_type=jnp.float32)
    factor = jnp.linalg.cholesky(gram_total)
    basis_rows = lax.linalg.triangular_solve(factor, panel_cols.T, left_side=True, lower=True).T
    return jnp.dot(basis_rows.T.astype(jnp.float32), sketch.astype(jnp.float32), precision=lax.Precision.HIGHEST, preferred_element_type=jnp.float32)
```

```python
import functools
import jax
import jax.numpy as jnp
from jax import lax
from jax.experimental import pallas as pl
from jax.experimental.pallas import tpu as pltpu
from jax.sharding import PartitionSpec as P

TILE = 128
P_SIZE = 256
NB = 64
CHUNKS = 1
F32, BF16, F16 = jnp.float32, jnp.bfloat16, jnp.float16
HI = lax.Precision.HIGHEST
MIB = 1 << 20


def vmem():
    return pl.BlockSpec(memory_space=pltpu.VMEM)


def smem():
    return pl.BlockSpec(memory_space=pltpu.SMEM)


def params(mib):
    return pltpu.CompilerParams(vmem_limit_bytes=mib * MIB)


def cost(flops, bytes_accessed):
    return pl.CostEstimate(flops=flops, bytes_accessed=bytes_accessed, transcendentals=0)


def signed_mixer(mixers_ref, index_ref, seed_ref, tile):
    position = lax.broadcasted_iota(jnp.int32, (1, TILE), 1)
    hashed = (seed_ref[tile] ^ position * 40503) * 69069
    sign = (1 - 2 * (hashed >> 16 & 1)).astype(F32)
    return mixers_ref[index_ref[tile]] * sign


def panel_kernel(per_step, parts, width, index_ref, seed_ref, core_ref, matrix_ref, mixers_ref, *refs):
    outs, turned = refs[:-1], refs[-1]
    core = core_ref[0]
    chunk_cols = P_SIZE // CHUNKS
    for u in range(per_step):
        mixer = signed_mixer(mixers_ref, index_ref, seed_ref, pl.program_id(0) * per_step + u)
        block = matrix_ref[u * TILE : (u + 1) * TILE, :]
        turned[...] = jnp.dot(mixer, block, precision=HI, preferred_element_type=F32).T
        for h in range(CHUNKS):
            for c in range(parts):
                for s in range(2):
                    who = core if s == 0 else 1 - core
                    start = pl.multiple_of(h * chunk_cols + c * width + who * (chunk_cols // 2), width)
                    outs[h * parts + c][s, u] = turned[pl.ds(start, width), :].astype(BF16)


def mix_panel(matrix, mixers, mixer_index, sign_seed, core, parts, width):
    tiles = mixer_index.shape[0]
    per_step = 4
    spec = pl.BlockSpec((2, per_step, width, TILE), lambda i, *_: (0, i, 0, 0))
    return pl.pallas_call(
        functools.partial(panel_kernel, per_step, parts, width),
        grid_spec=pltpu.PrefetchScalarGridSpec(
            num_scalar_prefetch=3,
            grid=(tiles // per_step,),
            in_specs=[
                pl.BlockSpec((per_step * TILE, P_SIZE), lambda i, *_: (i, 0)),
                pl.BlockSpec(mixers.shape, lambda i, *_: (0, 0, 0)),
            ],
            out_specs=[spec] * (CHUNKS * parts),
            scratch_shapes=[pltpu.VMEM((P_SIZE, TILE), F32)],
        ),
        out_shape=[jax.ShapeDtypeStruct((2, tiles, width, TILE), BF16)] * (CHUNKS * parts),
        compiler_params=params(24),
        cost_estimate=cost(12 * tiles * TILE * TILE * P_SIZE, 6 * tiles * TILE * P_SIZE),
        name="mix_panel",
    )(mixer_index, sign_seed, core, matrix, mixers)


def mix_kernel(per_step, index_ref, seed_ref, matrix_ref, mixers_ref, out_ref):
    for u in range(per_step):
        mixer = signed_mixer(mixers_ref, index_ref, seed_ref, pl.program_id(0) * per_step + u)
        block = matrix_ref[u * TILE : (u + 1) * TILE, :]
        mixed = jnp.dot(mixer, block, precision=HI, preferred_element_type=F32)
        out_ref[u * TILE : (u + 1) * TILE, :] = mixed.astype(BF16)


def mix_all(matrix, mixers, mixer_index, sign_seed):
    tiles = mixer_index.shape[0]
    rows, cols = matrix.shape
    per_step = 2
    return pl.pallas_call(
        functools.partial(mix_kernel, per_step),
        grid_spec=pltpu.PrefetchScalarGridSpec(
            num_scalar_prefetch=2,
            grid=(tiles // per_step,),
            in_specs=[
                pl.BlockSpec((per_step * TILE, cols), lambda i, *_: (i, 0)),
                pl.BlockSpec(mixers.shape, lambda i, *_: (0, 0, 0)),
            ],
            out_specs=pl.BlockSpec((per_step * TILE, cols), lambda i, *_: (i, 0)),
        ),
        out_shape=jax.ShapeDtypeStruct((rows, cols), BF16),
        compiler_params=params(24),
        cost_estimate=cost(12 * rows * TILE * cols, 6 * rows * cols),
        name="mix_all",
    )(mixer_index, sign_seed, matrix, mixers)


def bucket_kernel(first_ref, second_ref, flip_ref, *refs):
    pieces, out_ref, total = refs[:-2], refs[-2], refs[-1]
    total[...] = jnp.zeros_like(total)
    for j, piece in enumerate(pieces):
        count = piece.shape[0]

        def add(i, carry):
            at = j * count + i
            value = piece[i].astype(F32)
            one, two = first_ref[at], second_ref[at]
            total[one] = total[one] + value
            total[two] = total[two] + flip_ref[at] * value
            return carry

        lax.fori_loop(0, count, add, 0, unroll=8)
    summed = total[...]
    largest = jnp.max(jnp.max(jnp.abs(summed), axis=0), axis=1, keepdims=True)
    scale = jnp.where(largest > 1e-37, 1.0 / largest, 1.0)
    out_ref[...] = summed * scale


def sum_buckets(first, second, flip, pieces):
    width = pieces[0].shape[1]
    return pl.pallas_call(
        bucket_kernel,
        in_specs=[smem()] * 3 + [vmem()] * len(pieces),
        out_specs=vmem(),
        out_shape=jax.ShapeDtypeStruct((NB, width, TILE), F32),
        scratch_shapes=[pltpu.VMEM((NB, width, TILE), F32)],
        compiler_params=params(24),
        cost_estimate=cost(10**6, 4 * 10**6),
        name="sum_buckets",
    )(first, second, flip, *pieces)


def split(value):
    high = value.astype(BF16)
    return high, (value - high.astype(F32)).astype(BF16)


def cross_kernel(parts, groups, first_ref, second_ref, flip_ref, where_ref, mine_ref, other_ref, *refs):
    pieces = refs[: CHUNKS * parts]
    outs = refs[CHUNKS * parts : CHUNKS * parts + groups]
    panel, total = refs[-2:]
    width = pieces[0].shape[1]
    half = P_SIZE // 2
    step, tiles = pl.program_id(0), 2 * pl.num_programs(0)

    @pl.when(step == 0)
    def start():
        total[...] = jnp.zeros_like(total)
        for h in range(CHUNKS):
            for j in range(parts):
                at = h * (half // CHUNKS) + (where_ref[0] ^ j) * width
                panel[:, pl.ds(pl.multiple_of(at, width), width), :] = pieces[h * parts + j][...]

    for side, mixed_ref in enumerate((mine_ref, other_ref)):
        halves = []
        for u in range(2):
            t = side * tiles + 2 * step + u
            weights = panel[first_ref[t]] + flip_ref[t] * panel[second_ref[t]]
            halves.append(split(weights))
        high = jnp.concatenate([halves[0][0], halves[1][0]], axis=1)
        low = jnp.concatenate([halves[0][1], halves[1][1]], axis=1)
        both = jnp.concatenate([high, low], axis=0)
        total[...] += jnp.dot(both, mixed_ref[...], preferred_element_type=F32)

    @pl.when(step == pl.num_programs(0) - 1)
    def finish():
        total[:half, :] = total[:half, :] + total[half:, :]
        size = total.shape[1] // groups
        for j in range(groups):
            if groups == 1:
                outs[j][...] = total[:half, :]
            else:
                group = lax.rem(where_ref[1] + j, groups)
                outs[j][...] = total[:half, pl.ds(pl.multiple_of(group * size, size), size)]


def cross_parts(first, second, flip, where, mine, other, pieces, parts, groups):
    rows, cols = mine.shape
    half = P_SIZE // 2
    block = pl.BlockSpec((2 * TILE, cols), lambda i: (i, 0))
    return pl.pallas_call(
        functools.partial(cross_kernel, parts, groups),
        grid=(rows // (2 * TILE),),
        in_specs=[smem()] * 4 + [block] * 2 + [vmem()] * len(pieces),
        out_specs=[pl.BlockSpec((half, cols // groups), lambda i: (0, 0))] * groups,
        out_shape=[jax.ShapeDtypeStruct((half, cols // groups), F32)] * groups,
        scratch_shapes=[pltpu.VMEM((NB, half, TILE), F32), pltpu.VMEM((2 * half, cols), F32)],
        compiler_params=params(32),
        cost_estimate=cost(8 * rows * half * cols, 4 * rows * cols),
        name="cross_parts",
    )(first, second, flip, where, mine, other, *pieces)


def gram_kernel(parts, where_ref, *refs):
    pieces = refs[: 2 * CHUNKS * parts]
    out_ref, panel = refs[2 * CHUNKS * parts :]
    width = pieces[0].shape[1]
    half = P_SIZE // 2
    for s in range(2):
        core = where_ref[2] if s == 0 else 1 - where_ref[2]
        for h in range(CHUNKS):
            for j in range(parts):
                at = (2 * h + core) * (half // CHUNKS) + (where_ref[0] ^ j) * width
                at = pl.ds(pl.multiple_of(at, width), width)
                panel[:, at, :] = pieces[(s * CHUNKS + h) * parts + j][...]

    def nt(a, b):
        return lax.dot_general(a, b, (((1,), (1,)), ((), ())), preferred_element_type=F32)

    def pair(i, carry):
        square, mixed = carry
        one, two = split(jnp.concatenate([panel[2 * i], panel[2 * i + 1]], axis=1))
        return square + (nt(one, one) + nt(two, two)), mixed + nt(one, two)

    zero = jnp.zeros((P_SIZE, P_SIZE), F32)
    square, mixed = lax.fori_loop(0, NB // 2, pair, (zero, zero), unroll=2)
    out_ref[...] = square + (mixed + mixed.T)


def gram_of(where, pieces, parts):
    return pl.pallas_call(
        functools.partial(gram_kernel, parts),
        in_specs=[smem()] + [vmem()] * len(pieces),
        out_specs=vmem(),
        out_shape=jax.ShapeDtypeStruct((P_SIZE, P_SIZE), F32),
        scratch_shapes=[pltpu.VMEM((NB, P_SIZE, TILE), F32)],
        compiler_params=params(32),
        cost_estimate=cost(6 * NB * TILE * P_SIZE * P_SIZE, 2 * NB * TILE * P_SIZE),
        name="gram_of",
    )(where, *pieces)


def local(matrix, mixers, bucket_pair, mixer_index, sign_seed):
    cols = matrix.shape[1]
    tiles = bucket_pair.shape[0]
    rows_n, parts = lax.axis_size("rows"), lax.axis_size("cols")
    chips = rows_n // 2
    row, part = lax.axis_index("rows"), lax.axis_index("cols")
    core, chip = row % 2, row // 2
    width = P_SIZE // (2 * CHUNKS * parts)
    swap = [(i, i ^ 1) for i in range(rows_n)]

    def shift(value, j):
        return lax.ppermute(value, "rows", [(i, (i + 2 * j) % rows_n) for i in range(rows_n)])

    def across(value, j):
        return lax.ppermute(value, "cols", [(i, i ^ j) for i in range(parts)])

    with jax.named_scope("names"):
        flips = 1 - 2 * (sign_seed >> 29 & 1)
        names = jnp.concatenate([bucket_pair, flips[:, None]], axis=1).T
        names = lax.all_gather(names, "rows")
        order = [(row - 2 * j) % rows_n ^ s for j in range(chips) for s in range(2)]
        named = names[jnp.stack(order)]
        first, second, flip = (named[:, i].reshape(-1) for i in range(3))
        flip = flip.astype(F32)
        where = jnp.stack([part, chip, core]).astype(jnp.int32)

    with jax.named_scope("panel_mix"):
        pieces = mix_panel(matrix, mixers, mixer_index, sign_seed, core[None].astype(jnp.int32), parts, width)
    mine, others = [], []
    for h in range(CHUNKS):
        with jax.named_scope("panel_spread"):
            held = pieces[h * parts]
            for j in range(1, parts):
                got = lax.ppermute(pieces[h * parts + j], "cols", [(0, j)])
                held = jnp.where(part == j, got, held)
            held = jnp.concatenate([held[0], lax.ppermute(held[1], "rows", swap)])
        with jax.named_scope("panel_rows"):
            arrived = [held] + [shift(held, j) for j in range(1, chips)]
        with jax.named_scope("panel_sum"):
            summed = sum_buckets(first, second, flip, arrived).astype(F16)
        with jax.named_scope("panel_cols"):
            all_parts = [summed] + [across(summed, j) for j in range(1, parts)]
            mine += [v.astype(F32) for v in all_parts]
            others += [lax.ppermute(v, "rows", swap).astype(F32) for v in all_parts]

    with jax.named_scope("mix"):
        mixed = mix_all(matrix, mixers, mixer_index, sign_seed)
        mixed_other = lax.ppermute(mixed, "rows", swap)

    fast = cols % (TILE * rows_n) == 0
    with jax.named_scope("cross"):
        crossed = cross_parts(
            first[: 2 * tiles], second[: 2 * tiles], flip[: 2 * tiles], where, mixed, mixed_other, mine, parts, chips if fast else 1
        )
    with jax.named_scope("gram"):
        gram = gram_of(where, mine + others, parts)
    with jax.named_scope("factor"):
        lower = jnp.linalg.cholesky(gram)
        inverse = lax.linalg.triangular_solve(lower, jnp.eye(P_SIZE, dtype=F32), left_side=True, lower=True)

    def both_cores(own, other):
        low, high = jnp.where(core == 0, own, other), jnp.where(core == 0, other, own)
        shape = (CHUNKS, -1, own.shape[1])
        return jnp.concatenate([low.reshape(shape), high.reshape(shape)], axis=1).reshape(P_SIZE, -1)

    share = P_SIZE // rows_n
    if fast:
        with jax.named_scope("cross_sum"):
            total = crossed[0]
            for j in range(1, chips):
                total = total + shift(crossed[j], j)
            size = total.shape[1] // 2
            left, right = total[:, :size], total[:, size:]
            keep = jnp.where(core == 0, left, right)
            give = jnp.where(core == 0, right, left)
            total = both_cores(keep, lax.ppermute(give, "rows", swap))
        with jax.named_scope("solve"):
            solved = jnp.dot(inverse, total, precision=HI, preferred_element_type=F32)
            return lax.all_to_all(solved, "rows", split_axis=0, concat_axis=1, tiled=True)
    zero = jnp.zeros_like(crossed[0])
    total = lax.psum(both_cores(crossed[0], zero), "rows")
    solved = jnp.dot(inverse, total, precision=HI, preferred_element_type=F32)
    return lax.dynamic_slice_in_dim(solved, row * share, share, 0)


def solution(mesh):
    in_specs = (P("rows", "cols"), P(), P("rows", None), P("rows"), P("rows"))
    out_specs = P("rows", "cols")
    return jax.shard_map(local, mesh=mesh, in_specs=in_specs, out_specs=out_specs, check_vma=False)
```

```python
import functools
import jax
import jax.numpy as jnp
from jax import lax
from jax.experimental import pallas as pl
from jax.experimental.pallas import tpu as pltpu
from jax.sharding import PartitionSpec as P

TILE = 128
P_SIZE = 256
NB = 64
CHUNKS = 2
WIDTH = 16
HALF = P_SIZE // CHUNKS
SLICES = HALF // (2 * WIDTH)
BASE = 64
F32, BF16, F16 = jnp.float32, jnp.bfloat16, jnp.float16
HI = lax.Precision.HIGHEST
MIB = 1 << 20


def vmem():
    return pl.BlockSpec(memory_space=pltpu.VMEM)


def smem():
    return pl.BlockSpec(memory_space=pltpu.SMEM)


def anywhere():
    return pl.BlockSpec(memory_space=pl.ANY)


def params(mib):
    return pltpu.CompilerParams(vmem_limit_bytes=mib * MIB)


def cost(flops, bytes_accessed):
    return pl.CostEstimate(flops=flops, bytes_accessed=bytes_accessed, transcendentals=0)


def signed_mixer(mixers_ref, names_ref, tile):
    position = lax.broadcasted_iota(jnp.int32, (1, TILE), 1)
    hashed = (names_ref[4, tile] ^ position * 40503) * 69069
    sign = (1 - 2 * (hashed >> 16 & 1)).astype(F32)
    return mixers_ref[names_ref[3, tile]] * sign


def split(value):
    high = value.astype(BF16)
    return high, (value - high.astype(F32)).astype(BF16)


def product(mixer, block):
    mixer_high, mixer_low = split(mixer)
    block_high, block_low = split(block)
    wide = jnp.dot(jnp.concatenate([mixer_high, mixer_low], axis=0), block_high, preferred_element_type=F32)
    low = jnp.dot(mixer_high, block_low, preferred_element_type=F32)
    return wide[:TILE] + (wide[TILE:] + low)


def panel_kernel(per_step, names_ref, order_ref, matrix_ref, mixers_ref, *refs):
    outs, turned = refs[:-1], refs[-1]
    first = pl.program_id(0) * per_step
    core = order_ref[2 * SLICES + 1]
    for u in range(per_step):
        mixer = signed_mixer(mixers_ref, names_ref, first + u)
        block = matrix_ref[u * TILE : (u + 1) * TILE, :]
        turned[u] = product(mixer, block).T
        for h in range(CHUNKS):
            for c in range(SLICES):
                for s in range(2):
                    who = core if s == 0 else 1 - core
                    start = pl.multiple_of(h * HALF + who * (HALF // 2) + c * WIDTH, WIDTH)
                    outs[h * SLICES + c][s, u] = turned[u, pl.ds(start, WIDTH), :].astype(BF16)


def mix_panel(matrix, mixers, names, order):
    tiles = names.shape[1]
    per_step = 4
    spec = pl.BlockSpec((2, per_step, WIDTH, TILE), lambda i, *_: (0, i, 0, 0))
    return pl.pallas_call(
        functools.partial(panel_kernel, per_step),
        grid_spec=pltpu.PrefetchScalarGridSpec(
            num_scalar_prefetch=2,
            grid=(tiles // per_step,),
            in_specs=[
                pl.BlockSpec((per_step * TILE, P_SIZE), lambda i, *_: (i, 0)),
                pl.BlockSpec(mixers.shape, lambda i, *_: (0, 0, 0)),
            ],
            out_specs=[spec] * (CHUNKS * SLICES),
            scratch_shapes=[pltpu.VMEM((per_step, P_SIZE, TILE), F32)],
        ),
        out_shape=[jax.ShapeDtypeStruct((2, tiles, WIDTH, TILE), BF16)] * (CHUNKS * SLICES),
        compiler_params=params(52),
        cost_estimate=cost(6 * tiles * TILE * TILE * P_SIZE, 6 * tiles * TILE * P_SIZE),
        name="mix_panel",
    )(names, order, matrix, mixers)


def mix_kernel(per_step, start, names_ref, matrix_ref, mixers_ref, after_ref, out_ref):
    first = start + pl.program_id(0) * per_step
    for u in range(per_step):
        mixer = signed_mixer(mixers_ref, names_ref, first + u)
        block = matrix_ref[u * TILE : (u + 1) * TILE, :]
        out_ref[u * TILE : (u + 1) * TILE, :] = product(mixer, block).astype(BF16)


def mix_tiles(matrix, mixers, names, after, start, count):
    cols = matrix.shape[1]
    per_step = 2
    return pl.pallas_call(
        functools.partial(mix_kernel, per_step, start),
        grid_spec=pltpu.PrefetchScalarGridSpec(
            num_scalar_prefetch=1,
            grid=(count // per_step,),
            in_specs=[
                pl.BlockSpec((per_step * TILE, cols), lambda i, *_: (i + start // per_step, 0)),
                pl.BlockSpec(mixers.shape, lambda i, *_: (0, 0, 0)),
                anywhere(),
            ],
            out_specs=pl.BlockSpec((per_step * TILE, cols), lambda i, *_: (i, 0)),
        ),
        out_shape=jax.ShapeDtypeStruct((count * TILE, cols), BF16),
        compiler_params=params(52),
        cost_estimate=cost(12 * count * TILE * TILE * cols, 6 * count * TILE * cols),
        name="mix_tiles",
    )(names, matrix, mixers, after)


def pick_kernel(order_ref, after_ref, *refs):
    sources, (keep_ref, give_ref) = refs[:-2], refs[-2:]
    part = order_ref[2 * SLICES + 2]
    for j, source in enumerate(sources):
        taken = part == j if j else (part == 0) | (part >= len(sources))

        @pl.when(taken)
        def copy():
            keep_ref[...] = source[0]
            give_ref[...] = source[1]


def pick(order, after, sources):
    return pl.pallas_call(
        pick_kernel,
        in_specs=[smem(), anywhere()] + [vmem()] * len(sources),
        out_specs=[vmem()] * 2,
        out_shape=[jax.ShapeDtypeStruct(sources[0].shape[1:], BF16)] * 2,
        compiler_params=params(16),
        cost_estimate=cost(0, 4 * 10**5),
        name="pick",
    )(order, after, *sources)


def tie_kernel(count, *refs):
    del count, refs


def tie(values, after):
    return pl.pallas_call(
        functools.partial(tie_kernel, len(values)),
        in_specs=[anywhere()] * (len(values) + 1),
        out_specs=[anywhere()] * len(values),
        out_shape=[jax.ShapeDtypeStruct(v.shape, v.dtype) for v in values],
        input_output_aliases={i: i for i in range(len(values))},
        cost_estimate=cost(0, 10**4),
        name="tie",
    )(*values, after)


def bucket_kernel(names_ref, after_ref, *refs):
    pieces, out_ref, total = refs[:-2], refs[-2], refs[-1]
    total[...] = jnp.zeros_like(total)
    for j, piece in enumerate(pieces):
        count = piece.shape[0]

        def add(i, carry):
            at = j * count + i
            value = piece[i].astype(F32)
            one, two = names_ref[0, at], names_ref[1, at]
            total[one] = total[one] + value
            total[two] = total[two] + names_ref[2, at].astype(F32) * value
            return carry

        lax.fori_loop(0, count, add, 0, unroll=8)
    summed = total[...]
    largest = jnp.max(jnp.max(jnp.abs(summed), axis=0), axis=1, keepdims=True)
    scale = jnp.where(largest > 1e-37, 1.0 / largest, 1.0)
    out_ref[...] = summed * scale


def sum_buckets(names, after, pieces):
    return pl.pallas_call(
        bucket_kernel,
        in_specs=[smem(), anywhere()] + [vmem()] * len(pieces),
        out_specs=vmem(),
        out_shape=jax.ShapeDtypeStruct((NB, WIDTH, TILE), F32),
        scratch_shapes=[pltpu.VMEM((NB, WIDTH, TILE), F32)],
        compiler_params=params(24),
        cost_estimate=cost(10**6, 4 * 10**6),
        name="sum_buckets",
    )(names, after, *pieces)


def nt(a, b, precision=None):
    return lax.dot_general(a, b, (((1,), (1,)), ((), ())), precision=precision, preferred_element_type=F32)


def nn(a, b):
    return jnp.dot(a, b, precision=HI, preferred_element_type=F32)


def join(order_ref, pieces, panel):
    for q, piece in enumerate(pieces):
        panel[:, pl.ds(pl.multiple_of(order_ref[q] * WIDTH, WIDTH), WIDTH), :] = piece[...]


def cross_kernel(per_step, groups, names_ref, order_ref, after_ref, early_ref, late_ref, *refs):
    pieces, panel, refs = refs[: 2 * SLICES], refs[2 * SLICES], refs[2 * SLICES + 1 :]
    outs, total = refs[:-1], refs[-1]
    step = pl.program_id(0)

    @pl.when(step == 0)
    def start():
        total[...] = jnp.zeros_like(total)
        join(order_ref, pieces, panel)

    for side, mixed_ref in enumerate((early_ref, late_ref)):
        high, low = [], []
        for u in range(per_step):
            t = per_step * (side * pl.num_programs(0) + step) + u
            one, two = split(panel[names_ref[0, t]] + names_ref[2, t].astype(F32) * panel[names_ref[1, t]])
            high.append(one)
            low.append(two)
        weights = jnp.concatenate([jnp.concatenate(high, axis=1), jnp.concatenate(low, axis=1)], axis=0)
        total[...] += jnp.dot(weights, mixed_ref[...], preferred_element_type=F32)

    @pl.when(step == pl.num_programs(0) - 1)
    def finish():
        total[:HALF, :] = total[:HALF, :] + total[HALF:, :]
        if groups == 1:
            outs[0][...] = total[:HALF, :]
        else:
            chip, core = order_ref[2 * SLICES], order_ref[2 * SLICES + 1]
            for s in range(2):
                who = core if s == 0 else 1 - core
                for j in range(groups):
                    at = (2 * lax.rem(chip + j, groups) + who) * TILE
                    outs[s][j] = total[:HALF, pl.ds(pl.multiple_of(at, TILE), TILE)]


def cross_parts(names, order, after, mixed, pieces, groups):
    rows, cols = mixed[0].shape
    per_step = 4
    if groups == 1:
        outs = [jax.ShapeDtypeStruct((HALF, cols), F32)]
    else:
        outs = [jax.ShapeDtypeStruct((groups, HALF, TILE), F32)] * 2
    outs = [jax.ShapeDtypeStruct((NB, HALF, TILE), F32)] + outs
    return pl.pallas_call(
        functools.partial(cross_kernel, per_step, groups),
        grid=(rows // (per_step * TILE),),
        in_specs=[smem(), smem(), anywhere()] + [pl.BlockSpec((per_step * TILE, cols), lambda i: (i, 0))] * 2 + [vmem()] * len(pieces),
        out_specs=[vmem()] * len(outs),
        out_shape=outs,
        scratch_shapes=[pltpu.VMEM((2 * HALF, cols), F32)],
        compiler_params=params(32),
        cost_estimate=cost(8 * rows * HALF * cols, 4 * rows * cols),
        name="cross_parts",
    )(names, order, after, *mixed, *pieces)


def factor_inverse(block):
    row = lax.broadcasted_iota(jnp.int32, (BASE, BASE), 0)
    lane = lax.broadcasted_iota(jnp.int32, (BASE, BASE), 1)
    eye = (row == lane).astype(F32)
    wide = jnp.concatenate([block, eye], axis=1)
    slabs = [wide[8 * g : 8 * g + 8, :] for g in range(BASE // 8)]
    below = lax.broadcasted_iota(jnp.int32, (8, 1), 0)
    for j in range(BASE):
        own, at = j // 8, j % 8
        pivot_row = slabs[own][at : at + 1, :]
        scaled = pivot_row * (1.0 / pivot_row[:, j : j + 1])
        for g in range(own, BASE // 8):
            column = slabs[g][:, j : j + 1]
            if g == own:
                if at == 7:
                    continue
                column = jnp.where(below > at, column, 0.0)
            slabs[g] = slabs[g] - column * scaled
    wide = jnp.concatenate(slabs, axis=0)
    pivots = jnp.sum(wide[:, :BASE] * eye, axis=1, keepdims=True)
    return wide[:, BASE:] * lax.rsqrt(pivots)


def factor_inverse_pair(block):
    first = factor_inverse(block[:BASE, :BASE])
    side = nt(block[BASE:, :BASE], first, HI)
    second = factor_inverse(block[BASE:, BASE:] - nt(side, side, HI))
    corner = -nn(second, nn(side, first))
    top = jnp.concatenate([first, jnp.zeros_like(first)], axis=1)
    return jnp.concatenate([top, jnp.concatenate([corner, second], axis=1)], axis=0)


GROUP = 8


def wide_buckets(panel, i):
    return jnp.concatenate([panel[GROUP * i + u] for u in range(GROUP)], axis=1)


def first_kernel(after_ref, panel, out_ref, acc):
    acc[...] = jnp.zeros_like(acc)

    def step(i, carry):
        one, two = split(wide_buckets(panel, i))
        acc[...] += nt(jnp.concatenate([one, two], axis=0), one)
        return carry

    lax.fori_loop(0, NB // GROUP, step, 0)
    mixed = acc[HALF:, :]
    out_ref[...] = acc[:HALF, :] + (mixed + mixed.T)


def first_gram(after, panel):
    return pl.pallas_call(
        first_kernel,
        in_specs=[anywhere(), vmem()],
        out_specs=vmem(),
        out_shape=jax.ShapeDtypeStruct((HALF, HALF), F32),
        scratch_shapes=[pltpu.VMEM((2 * HALF, HALF), F32)],
        compiler_params=params(32),
        cost_estimate=cost(3 * 10**9, 4 * NB * TILE * HALF),
        name="first_gram",
    )(after, panel)


def factor_kernel(block_ref, out_ref):
    out_ref[...] = factor_inverse_pair(block_ref[...])


def first_factor(block):
    return pl.pallas_call(
        factor_kernel,
        in_specs=[vmem()],
        out_specs=vmem(),
        out_shape=jax.ShapeDtypeStruct((HALF, HALF), F32),
        compiler_params=params(16),
        cost_estimate=cost(10**10, 8 * HALF * HALF),
        name="first_factor",
    )(block)


def second_kernel(after_ref, panel0, panel1, side_ref, block_ref, acc, extra):
    acc[...] = jnp.zeros_like(acc)
    extra[...] = jnp.zeros_like(extra)

    def step(i, carry):
        one0, two0 = split(wide_buckets(panel0, i))
        one1, two1 = split(wide_buckets(panel1, i))
        acc[...] += nt(jnp.concatenate([one1, two1], axis=0), jnp.concatenate([one0, one1], axis=0))
        extra[...] += nt(one1, two0)
        return carry

    lax.fori_loop(0, NB // GROUP, step, 0)
    side_ref[...] = acc[:HALF, :HALF] + (acc[HALF:, :HALF] + extra[...])
    mixed = acc[HALF:, HALF:]
    block_ref[...] = acc[:HALF, HALF:] + (mixed + mixed.T)


def second_gram(after, panel0, panel1):
    return pl.pallas_call(
        second_kernel,
        in_specs=[anywhere()] + [vmem()] * 2,
        out_specs=[vmem()] * 2,
        out_shape=[jax.ShapeDtypeStruct((HALF, HALF), F32)] * 2,
        scratch_shapes=[pltpu.VMEM((2 * HALF, 2 * HALF), F32), pltpu.VMEM((HALF, HALF), F32)],
        compiler_params=params(32),
        cost_estimate=cost(4 * 10**9, 4 * NB * TILE * P_SIZE),
        name="second_gram",
    )(after, panel0, panel1)


def last_kernel(after_ref, side_ref, block_ref, inverse_ref, out_ref):
    first = inverse_ref[...]
    side = nt(side_ref[...], first, HI)
    second = factor_inverse_pair(block_ref[...] - nt(side, side, HI))
    out_ref[:HALF, :HALF] = first
    out_ref[:HALF, HALF:] = jnp.zeros_like(first)
    out_ref[HALF:, :HALF] = -nn(second, nn(side, first))
    out_ref[HALF:, HALF:] = second


def second_factor(after, side, block, inverse):
    return pl.pallas_call(
        last_kernel,
        in_specs=[anywhere()] + [vmem()] * 3,
        out_specs=vmem(),
        out_shape=jax.ShapeDtypeStruct((P_SIZE, P_SIZE), F32),
        compiler_params=params(32),
        cost_estimate=cost(10**10, 4 * P_SIZE * P_SIZE),
        name="second_factor",
    )(after, side, block, inverse)


def local(matrix, mixers, bucket_pair, mixer_index, sign_seed):
    cols = matrix.shape[1]
    rows_n, parts = lax.axis_size("rows"), lax.axis_size("cols")
    chips = rows_n // 2
    row, part = lax.axis_index("rows"), lax.axis_index("cols")
    core, chip = row % 2, row // 2

    def swap(value):
        return lax.ppermute(value, "rows", [(i, i ^ 1) for i in range(rows_n)])

    def shift(value, j):
        return lax.ppermute(value, "rows", [(i, (i + 2 * j) % rows_n) for i in range(rows_n)])

    def across(value, j):
        return lax.ppermute(value, "cols", [(i, i ^ j) for i in range(parts)])

    with jax.named_scope("names"):
        flips = 1 - 2 * (sign_seed >> 29 & 1)
        names = jnp.stack([bucket_pair[:, 0], bucket_pair[:, 1], flips, mixer_index, sign_seed])
        place = [part ^ j if parts == SLICES else j for j in range(SLICES)]
        order = [who * SLICES + c for who in (core, 1 - core) for c in place]
        order = jnp.stack([jnp.asarray(v, jnp.int32) for v in order + [chip, core, part]])
    with jax.named_scope("panel_mix"):
        tiles = mix_panel(matrix, mixers, names, order)
    with jax.named_scope("names"):
        (later,) = tie([names], tiles[0])
        pair = jnp.concatenate([later, swap(later)], axis=1)
        all_names = jnp.concatenate([pair] + [shift(pair, j) for j in range(1, chips)], axis=1)
    groups = chips if cols % (TILE * rows_n) == 0 else 1

    def spread(h, after):
        with jax.named_scope("panel_spread"):
            slices = tiles[h * SLICES : (h + 1) * SLICES]
            got = [slices[0]] + [lax.ppermute(slices[j], "cols", [(0, j)]) for j in range(1, SLICES)]
            keep, give = pick(order, after, got)
            return jnp.concatenate([keep, swap(give)])

    def gather_rows(held):
        with jax.named_scope("panel_rows"):
            return [held] + [shift(held, j) for j in range(1, chips)]

    def gather_cols(summed):
        with jax.named_scope("panel_cols"):
            sent = summed.astype(F16)
            if parts == SLICES:
                mine = [sent] + [across(sent, j) for j in range(1, parts)]
            else:
                mine = list(lax.all_gather(sent, "cols")[:SLICES])
            return [v.astype(F32) for v in mine + [swap(v) for v in mine]]

    half = names.shape[1] // 2
    with jax.named_scope("mix"):
        early = mix_tiles(matrix, mixers, names, tiles[0], 0, half)
    held0 = spread(0, early)
    arrived0 = gather_rows(held0)
    with jax.named_scope("mix"):
        late = mix_tiles(matrix, mixers, names, held0, half, half)
    held1 = spread(1, late)
    arrived1 = gather_rows(held1)
    mixed = (early, late)
    with jax.named_scope("panel_sum"):
        summed0 = sum_buckets(all_names, held1, arrived0)
    pieces0 = gather_cols(summed0)
    with jax.named_scope("panel_sum"):
        summed1 = sum_buckets(all_names, summed0, arrived1)
    pieces1 = gather_cols(summed1)
    with jax.named_scope("cross0"):
        panel0, *crossed0 = cross_parts(names, order, summed1, mixed, pieces0, groups)
    with jax.named_scope("factor0"):
        inverse0 = first_factor(first_gram(summed1, panel0))
    with jax.named_scope("cross1"):
        panel1, *crossed1 = cross_parts(names, order, inverse0, mixed, pieces1, groups)
    with jax.named_scope("gram1"):
        side, block = second_gram(crossed1[0], panel0, panel1)

    if groups == 1:
        inverse = second_factor(side, side, block, inverse0)
        total = lax.psum(jnp.concatenate([crossed0[0], crossed1[0]], axis=0), "rows")
        share = P_SIZE // rows_n
        return lax.dynamic_slice_in_dim(nn(inverse, total), row * share, share, 0)
    with jax.named_scope("cross_sum"):
        on_chip = [keep + swap(give) for keep, give in (crossed0, crossed1)]
    with jax.named_scope("factor1"):
        inverse = second_factor(on_chip[1], side, block, inverse0)
    with jax.named_scope("cross_sum"):
        totals = []
        for v in on_chip:
            total = v[0]
            for j in range(1, chips):
                total = total + shift(v[j], j)
            totals.append(total)
    with jax.named_scope("solve"):
        solved = nn(inverse, jnp.concatenate(totals, axis=0))
        return lax.all_to_all(solved, "rows", split_axis=0, concat_axis=1, tiled=True)


def solution(mesh):
    in_specs = (P("rows", "cols"), P(), P("rows", None), P("rows"), P("rows"))
    out_specs = P("rows", "cols")
    return jax.shard_map(local, mesh=mesh, in_specs=in_specs, out_specs=out_specs, check_vma=False)
```

```python
import functools
import jax
import jax.numpy as jnp
from jax import lax
from jax.experimental import pallas as pl
from jax.experimental.pallas import tpu as pltpu
from jax.sharding import PartitionSpec as P

TILE = 128
P_SIZE = 256
NB = 64
CHUNKS = 2
WIDTH = 16
HALF = P_SIZE // CHUNKS
SLICES = HALF // (2 * WIDTH)
BASE = 64
STEP = 8
F32, BF16, F16 = jnp.float32, jnp.bfloat16, jnp.float16
HI = lax.Precision.HIGHEST
MIB = 1 << 20


def vmem():
    return pl.BlockSpec(memory_space=pltpu.VMEM)


def smem():
    return pl.BlockSpec(memory_space=pltpu.SMEM)


def anywhere():
    return pl.BlockSpec(memory_space=pl.ANY)


def params(mib):
    return pltpu.CompilerParams(vmem_limit_bytes=mib * MIB)


def cost(flops, bytes_accessed):
    return pl.CostEstimate(flops=flops, bytes_accessed=bytes_accessed, transcendentals=0)


LIGHT = cost(10**6, 10**5)


def signed_mixer(mixers_ref, names_ref, tile):
    position = lax.broadcasted_iota(jnp.int32, (1, TILE), 1)
    hashed = (names_ref[4, tile] ^ position * 40503) * 69069
    sign = (1 - 2 * (hashed >> 16 & 1)).astype(F32)
    return mixers_ref[names_ref[3, tile]] * sign


def split(value):
    high = value.astype(BF16)
    return high, (value - high.astype(F32)).astype(BF16)


def product(mixer, block):
    mixer_high, mixer_low = split(mixer)
    block_high, block_low = split(block)
    wide = jnp.dot(jnp.concatenate([mixer_high, mixer_low], axis=0), block_high, preferred_element_type=F32)
    low = jnp.dot(mixer_high, block_low, preferred_element_type=F32)
    return wide[:TILE] + (wide[TILE:] + low)


def panel_kernel(per_step, names_ref, order_ref, matrix_ref, mixers_ref, *refs):
    outs, turned = refs[:-1], refs[-1]
    first = pl.program_id(0) * per_step
    core = order_ref[2 * SLICES + 1]
    for u in range(per_step):
        mixer = signed_mixer(mixers_ref, names_ref, first + u)
        block = matrix_ref[u * TILE : (u + 1) * TILE, :]
        turned[u] = product(mixer, block).T
        for h in range(CHUNKS):
            for c in range(SLICES):
                for s in range(2):
                    who = core if s == 0 else 1 - core
                    start = pl.multiple_of(h * HALF + who * (HALF // 2) + c * WIDTH, WIDTH)
                    outs[h * SLICES + c][s, u] = turned[u, pl.ds(start, WIDTH), :].astype(BF16)


def mix_panel(matrix, mixers, names, order):
    tiles = names.shape[1]
    per_step = 8
    spec = pl.BlockSpec((2, per_step, WIDTH, TILE), lambda i, *_: (0, i, 0, 0))
    return pl.pallas_call(
        functools.partial(panel_kernel, per_step),
        grid_spec=pltpu.PrefetchScalarGridSpec(
            num_scalar_prefetch=2,
            grid=(tiles // per_step,),
            in_specs=[
                pl.BlockSpec((per_step * TILE, P_SIZE), lambda i, *_: (i, 0)),
                pl.BlockSpec(mixers.shape, lambda i, *_: (0, 0, 0)),
            ],
            out_specs=[spec] * (CHUNKS * SLICES),
            scratch_shapes=[pltpu.VMEM((per_step, P_SIZE, TILE), F32)],
        ),
        out_shape=[jax.ShapeDtypeStruct((2, tiles, WIDTH, TILE), BF16)] * (CHUNKS * SLICES),
        compiler_params=params(52),
        cost_estimate=LIGHT,
        name="mix_panel",
    )(names, order, matrix, mixers)


def mix_kernel(per_step, start, names_ref, matrix_ref, mixers_ref, after_ref, out_ref):
    first = start + pl.program_id(0) * per_step
    for u in range(per_step):
        mixer = signed_mixer(mixers_ref, names_ref, first + u)
        block = matrix_ref[u * TILE : (u + 1) * TILE, :]
        out_ref[u * TILE : (u + 1) * TILE, :] = product(mixer, block).astype(BF16)


def mix_tiles(matrix, mixers, names, after, start, count):
    cols = matrix.shape[1]
    per_step = 4
    return pl.pallas_call(
        functools.partial(mix_kernel, per_step, start),
        grid_spec=pltpu.PrefetchScalarGridSpec(
            num_scalar_prefetch=1,
            grid=(count // per_step,),
            in_specs=[
                pl.BlockSpec((per_step * TILE, cols), lambda i, *_: (i + start // per_step, 0)),
                pl.BlockSpec(mixers.shape, lambda i, *_: (0, 0, 0)),
                anywhere(),
            ],
            out_specs=pl.BlockSpec((per_step * TILE, cols), lambda i, *_: (i, 0)),
        ),
        out_shape=jax.ShapeDtypeStruct((count * TILE, cols), BF16),
        compiler_params=params(52),
        cost_estimate=LIGHT,
        name="mix_tiles",
    )(names, matrix, mixers, after)


def pick_kernel(count, order_ref, *refs):
    extra, sources, (keep_ref, give_ref) = refs[:count], refs[count:-2], refs[-2:]
    part = order_ref[2 * SLICES + 2]
    tiles = sources[0].shape[1]
    for j, source in enumerate(sources):
        taken = part == j if j else (part == 0) | (part >= len(sources))

        @pl.when(taken)
        def copy(source=source):
            keep_ref[:tiles] = source[0]
            give_ref[:tiles] = source[1]

    for i, ref in enumerate(extra):
        keep_ref[tiles + i] = ref[...]
        give_ref[tiles + i] = ref[...]


def pick(order, extra, sources):
    tiles = sources[0].shape[1] + len(extra)
    return pl.pallas_call(
        functools.partial(pick_kernel, len(extra)),
        in_specs=[smem()] + [vmem()] * (len(extra) + len(sources)),
        out_specs=[vmem()] * 2,
        out_shape=[jax.ShapeDtypeStruct((tiles, WIDTH, TILE), BF16)] * 2,
        compiler_params=params(16),
        cost_estimate=LIGHT,
        name="pick",
    )(order, *extra, *sources)


def add_tiles(names, stride, tiles, pieces, out_ref, total):
    total[...] = jnp.zeros_like(total)
    for j, piece in enumerate(pieces):
        for s in range(2):

            def add(i, carry, j=j, s=s, piece=piece):
                value = piece[s * stride + i].astype(F32)
                one, two = names[2 * j + s, 0, i], names[2 * j + s, 1, i]
                total[one] = total[one] + value
                total[two] = total[two] + names[2 * j + s, 2, i].astype(F32) * value
                return carry

            lax.fori_loop(0, tiles, add, 0, unroll=8)
    summed = total[...]
    largest = jnp.max(jnp.max(jnp.abs(summed), axis=0), axis=1, keepdims=True)
    out_ref[...] = summed * jnp.where(largest > 1e-37, 1.0 / largest, 1.0)


def first_sum_kernel(after_ref, *refs):
    pieces, (out_ref, names_ref, total, names, sem) = refs[:-5], refs[-5:]
    tiles = pieces[0].shape[0] // 2 - 1
    for j, piece in enumerate(pieces):
        for s in range(2):
            names_ref[2 * j + s] = piece[s * (tiles + 1) + tiles].astype(F32)[:8].astype(jnp.int32)
    copy = pltpu.make_async_copy(names_ref, names, sem)
    copy.start()
    copy.wait()
    add_tiles(names, tiles + 1, tiles, pieces, out_ref, total)


def first_sum(after, pieces):
    names = (2 * len(pieces), 8, TILE)
    return pl.pallas_call(
        first_sum_kernel,
        in_specs=[anywhere()] + [vmem()] * len(pieces),
        out_specs=[vmem()] * 2,
        out_shape=[jax.ShapeDtypeStruct((NB, WIDTH, TILE), F32), jax.ShapeDtypeStruct(names, jnp.int32)],
        scratch_shapes=[pltpu.VMEM((NB, WIDTH, TILE), F32), pltpu.SMEM(names, jnp.int32), pltpu.SemaphoreType.DMA],
        compiler_params=params(24),
        cost_estimate=LIGHT,
        name="first_sum",
    )(after, *pieces)


def next_sum_kernel(names, after_ref, *refs):
    pieces, (out_ref, total) = refs[:-2], refs[-2:]
    tiles = pieces[0].shape[0] // 2
    add_tiles(names, tiles, tiles, pieces, out_ref, total)


def next_sum(names, after, pieces):
    return pl.pallas_call(
        next_sum_kernel,
        in_specs=[smem(), anywhere()] + [vmem()] * len(pieces),
        out_specs=vmem(),
        out_shape=jax.ShapeDtypeStruct((NB, WIDTH, TILE), F32),
        scratch_shapes=[pltpu.VMEM((NB, WIDTH, TILE), F32)],
        compiler_params=params(24),
        cost_estimate=LIGHT,
        name="next_sum",
    )(names, after, *pieces)


def nt(a, b, precision=None):
    return lax.dot_general(a, b, (((1,), (1,)), ((), ())), precision=precision, preferred_element_type=F32)


def nn(a, b):
    return jnp.dot(a, b, precision=HI, preferred_element_type=F32)


def join(order_ref, pieces, panel):
    for q, piece in enumerate(pieces):
        panel[:, pl.ds(pl.multiple_of(order_ref[q] * WIDTH, WIDTH), WIDTH), :] = piece[...]


def cross_kernel(steps, chips, earlier, fast, names_ref, order_ref, after_ref, *refs):
    mixed, refs = refs[: len(steps)], refs[len(steps) :]
    pieces, refs = refs[: 2 * SLICES], refs[2 * SLICES :]
    before, refs = refs[:earlier], refs[earlier:]
    panel, outs, total = refs[0], refs[1:-1], refs[-1]
    step = pl.program_id(0)

    @pl.when(step == 0)
    def start():
        total[...] = jnp.zeros_like(total)
        join(order_ref, pieces, panel)

    high, low = [], []
    for u in range(STEP):
        t = STEP * step + u
        one, two = split(panel[names_ref[0, t]] + names_ref[2, t].astype(F32) * panel[names_ref[1, t]])
        high.append(one)
        low.append(two)
    weights = jnp.concatenate([jnp.concatenate(high, axis=1), jnp.concatenate(low, axis=1)], axis=0)

    begin = 0
    for count, mixed_ref in zip(steps, mixed):

        @pl.when((step >= begin) & (step < begin + count))
        def add(mixed_ref=mixed_ref):
            total[...] += jnp.dot(weights, mixed_ref[...], preferred_element_type=F32)

        begin += count

    @pl.when(step == pl.num_programs(0) - 1)
    def finish():
        total[:HALF, :] = total[:HALF, :] + total[HALF:, :]
        rows = earlier and HALF
        for ref, out in zip(before, outs):
            out[..., :HALF, :] = ref[...]
        if not fast:
            outs[0][rows:, :] = total[:HALF, :]
        else:
            chip, core = order_ref[2 * SLICES], order_ref[2 * SLICES + 1]
            for s in range(2):
                who = core if s == 0 else 1 - core
                for j in range(chips):
                    at = (2 * lax.rem(chip + j, chips) + who) * TILE
                    outs[s][j, rows:, :] = total[:HALF, pl.ds(pl.multiple_of(at, TILE), TILE)]


def cross_parts(names, order, after, mixed, pieces, before, chips, fast):
    cols = mixed[0].shape[1]
    steps = [v.shape[0] // (STEP * TILE) for v in mixed]
    rows = 2 * HALF if before else HALF
    if fast:
        outs = [jax.ShapeDtypeStruct((chips, rows, TILE), F32)] * 2
    else:
        outs = [jax.ShapeDtypeStruct((rows, cols), F32)]
    outs = [jax.ShapeDtypeStruct((NB, HALF, TILE), F32)] + outs
    begins = [sum(steps[:i]) for i in range(len(steps))]
    blocks = [
        pl.BlockSpec((STEP * TILE, cols), lambda i, b=begin, n=count: (jnp.clip(i - b, 0, n - 1), 0))
        for begin, count in zip(begins, steps)
    ]
    return pl.pallas_call(
        functools.partial(cross_kernel, steps, chips, len(before), fast),
        grid=(sum(steps),),
        in_specs=[smem(), smem(), anywhere()] + blocks + [vmem()] * (len(pieces) + len(before)),
        out_specs=[vmem()] * len(outs),
        out_shape=outs,
        scratch_shapes=[pltpu.VMEM((2 * HALF, cols), F32)],
        compiler_params=params(32),
        cost_estimate=LIGHT,
        name="cross_parts",
    )(names, order, after, *mixed, *pieces, *before)


def above(value):
    return jnp.concatenate([value[:1], value[:-1]], axis=0)


def factor_inverse(block):
    row = lax.broadcasted_iota(jnp.int32, (BASE, BASE), 0)
    lane = lax.broadcasted_iota(jnp.int32, (BASE, BASE), 1)
    eye = (row == lane).astype(F32)
    wide = jnp.concatenate([block, eye], axis=1)
    slabs = [wide[8 * g : 8 * g + 8, :] for g in range(BASE // 8)]
    place = lax.broadcasted_iota(jnp.int32, (8, 2 * BASE), 0)

    def full(value):
        return jnp.broadcast_to(value, (8, 2 * BASE))

    for j in range(0, BASE, 2):
        own, at = j // 8, j % 8
        slab = slabs[own]
        col0, col1 = full(slab[:, j : j + 1]), full(slab[:, j + 1 : j + 2])
        row0, row1 = full(slab[at : at + 1, :]), full(slab[at + 1 : at + 2, :])
        first, cross, second = full(col0[at : at + 1, :]), full(col1[at : at + 1, :]), full(col1[at + 1 : at + 2, :])
        scale = 1.0 / (first * second - cross * cross)
        solved0 = (second * row0 - cross * row1) * scale
        solved1 = (first * row1 - cross * row0) * scale
        for g in range(own, BASE // 8):
            if g == own:
                col0, col1 = jnp.where(place > at + 1, col0, 0.0), jnp.where(place > at + 1, col1, 0.0)
            else:
                col0, col1 = slabs[g][:, j : j + 1], slabs[g][:, j + 1 : j + 2]
            slabs[g] = slabs[g] - col0 * solved0 - col1 * solved1
    wide = jnp.concatenate(slabs, axis=0)
    diagonal = jnp.sum(wide[:, :BASE] * eye, axis=1, keepdims=True)
    beside = jnp.sum(jnp.where(lane == row + 1, wide[:, :BASE], 0.0), axis=1, keepdims=True)
    odd = row[:, :1] % 2 == 1
    ratio = jnp.where(odd, above(beside) / above(diagonal), 0.0)
    pivots = jnp.where(odd, diagonal - above(beside) * ratio, diagonal)
    return (wide - ratio * above(wide))[:, BASE:] * lax.rsqrt(pivots)


def factor_inverse_pair(block):
    first = factor_inverse(block[:BASE, :BASE])
    side = nt(block[BASE:, :BASE], first, HI)
    second = factor_inverse(block[BASE:, BASE:] - nt(side, side, HI))
    corner = -nn(second, nn(side, first))
    top = jnp.concatenate([first, jnp.zeros_like(first)], axis=1)
    return jnp.concatenate([top, jnp.concatenate([corner, second], axis=1)], axis=0)


GROUP = 8


def wide_buckets(panel, i):
    return jnp.concatenate([panel[GROUP * i + u] for u in range(GROUP)], axis=1)


def first_kernel(after_ref, panel, out_ref, acc):
    acc[...] = jnp.zeros_like(acc)

    def step(i, carry):
        one, two = split(wide_buckets(panel, i))
        acc[...] += nt(jnp.concatenate([one, two], axis=0), one)
        return carry

    lax.fori_loop(0, NB // GROUP, step, 0)
    mixed = acc[HALF:, :]
    out_ref[...] = acc[:HALF, :] + (mixed + mixed.T)


def first_gram(after, panel):
    return pl.pallas_call(
        first_kernel,
        in_specs=[anywhere(), vmem()],
        out_specs=vmem(),
        out_shape=jax.ShapeDtypeStruct((HALF, HALF), F32),
        scratch_shapes=[pltpu.VMEM((2 * HALF, HALF), F32)],
        compiler_params=params(32),
        cost_estimate=LIGHT,
        name="first_gram",
    )(after, panel)


def factor_kernel(block_ref, out_ref):
    out_ref[...] = factor_inverse_pair(block_ref[...])


def first_factor(block):
    return pl.pallas_call(
        factor_kernel,
        in_specs=[vmem()],
        out_specs=vmem(),
        out_shape=jax.ShapeDtypeStruct((HALF, HALF), F32),
        compiler_params=params(16),
        cost_estimate=LIGHT,
        name="first_factor",
    )(block)


def second_kernel(after_ref, panel0, panel1, side_ref, block_ref, acc, extra):
    acc[...] = jnp.zeros_like(acc)
    extra[...] = jnp.zeros_like(extra)

    def step(i, carry):
        one0, two0 = split(wide_buckets(panel0, i))
        one1, two1 = split(wide_buckets(panel1, i))
        acc[...] += nt(jnp.concatenate([one1, two1], axis=0), jnp.concatenate([one0, one1], axis=0))
        extra[...] += nt(one1, two0)
        return carry

    lax.fori_loop(0, NB // GROUP, step, 0)
    side_ref[...] = acc[:HALF, :HALF] + (acc[HALF:, :HALF] + extra[...])
    mixed = acc[HALF:, HALF:]
    block_ref[...] = acc[:HALF, HALF:] + (mixed + mixed.T)


def second_gram(after, panel0, panel1):
    return pl.pallas_call(
        second_kernel,
        in_specs=[anywhere()] + [vmem()] * 2,
        out_specs=[vmem()] * 2,
        out_shape=[jax.ShapeDtypeStruct((HALF, HALF), F32)] * 2,
        scratch_shapes=[pltpu.VMEM((2 * HALF, 2 * HALF), F32), pltpu.VMEM((HALF, HALF), F32)],
        compiler_params=params(32),
        cost_estimate=LIGHT,
        name="second_gram",
    )(after, panel0, panel1)


def last_kernel(after_ref, side_ref, block_ref, inverse_ref, out_ref):
    first = inverse_ref[...]
    side = nt(side_ref[...], first, HI)
    second = factor_inverse_pair(block_ref[...] - nt(side, side, HI))
    out_ref[:HALF, :HALF] = first
    out_ref[:HALF, HALF:] = jnp.zeros_like(first)
    out_ref[HALF:, :HALF] = -nn(second, nn(side, first))
    out_ref[HALF:, HALF:] = second


def second_factor(after, side, block, inverse):
    return pl.pallas_call(
        last_kernel,
        in_specs=[anywhere()] + [vmem()] * 3,
        out_specs=vmem(),
        out_shape=jax.ShapeDtypeStruct((P_SIZE, P_SIZE), F32),
        compiler_params=params(32),
        cost_estimate=LIGHT,
        name="second_factor",
    )(after, side, block, inverse)


def local(matrix, mixers, bucket_pair, mixer_index, sign_seed):
    cols = matrix.shape[1]
    rows_n, parts = lax.axis_size("rows"), lax.axis_size("cols")
    chips = rows_n // 2
    row, part = lax.axis_index("rows"), lax.axis_index("cols")
    core, chip = row % 2, row // 2

    def swap(value):
        return lax.ppermute(value, "rows", [(i, i ^ 1) for i in range(rows_n)])

    def shift(value, j):
        return lax.ppermute(value, "rows", [(i, (i + 2 * j) % rows_n) for i in range(rows_n)])

    def beside(value, j):
        return lax.ppermute(value, "rows", [(i, i ^ 2 * j) for i in range(rows_n)])

    def across(value, j):
        return lax.ppermute(value, "cols", [(i, i ^ j) for i in range(parts)])

    fast = cols % (TILE * rows_n) == 0
    with jax.named_scope("names"):
        flips = 1 - 2 * (sign_seed >> 29 & 1)
        names = jnp.stack([bucket_pair[:, 0], bucket_pair[:, 1], flips, mixer_index, sign_seed])
        place = [part ^ j if parts == SLICES else j for j in range(SLICES)]
        order = [who * SLICES + c for who in (core, 1 - core) for c in place]
        order = jnp.stack([jnp.asarray(v, jnp.int32) for v in order + [chip, core, part]])
    with jax.named_scope("panel_mix"):
        tiles = mix_panel(matrix, mixers, names, order)
    with jax.named_scope("names"):
        carried = jnp.pad(names[:3].astype(BF16), ((0, WIDTH - 3), (0, TILE - names.shape[1])))

    def spread(h, *extra):
        with jax.named_scope("panel_spread"):
            slices = tiles[h * SLICES : (h + 1) * SLICES]
            got = [slices[0]] + [lax.ppermute(slices[j], "cols", [(0, j)]) for j in range(1, SLICES)]
            keep, give = pick(order, extra, got)
            return jnp.concatenate([keep, swap(give)])

    def gather_rows(held):
        with jax.named_scope("panel_rows"):
            if chips != 4:
                return [held] + [shift(held, j) for j in range(1, chips)]
            far, near = beside(held, 2), beside(held, 1)
            return [held, far, near, beside(far, 1)]

    def gather_cols(summed):
        with jax.named_scope("panel_cols"):
            sent = summed.astype(F16)
            if parts == SLICES:
                return [sent] + [across(sent, j) for j in range(1, parts)]
            return list(lax.all_gather(sent, "cols")[:SLICES])

    def both_cores(mine):
        with jax.named_scope("panel_cores"):
            return [v.astype(F32) for v in mine + [swap(v) for v in mine]]

    def before(values, *others):
        return lax.optimization_barrier((values, others))[0]

    held0 = spread(0, carried)
    arrived0 = gather_rows(held0)
    with jax.named_scope("mix"):
        mixed = [mix_tiles(matrix, mixers, names, held0, 0, names.shape[1])]
    held1 = spread(1)
    arrived1 = gather_rows(held1)
    with jax.named_scope("panel_sum"):
        summed0, all_names = first_sum(mixed[0], arrived0)
    pieces0 = both_cores(gather_cols(summed0))
    with jax.named_scope("panel_sum"):
        summed1 = next_sum(all_names, summed0, arrived1)
    mine1 = gather_cols(summed1)
    with jax.named_scope("cross0"):
        panel0, *crossed0 = cross_parts(names, order, summed1, mixed, pieces0, [], chips, fast)
    with jax.named_scope("factor0"):
        inverse0 = first_factor(first_gram(crossed0[0], panel0))
    pieces1 = both_cores(before(mine1, inverse0, crossed0[0]))
    with jax.named_scope("cross1"):
        panel1, *crossed = cross_parts(names, order, inverse0, mixed, pieces1, crossed0, chips, fast)
    with jax.named_scope("gram1"):
        side, block = second_gram(crossed[0], panel0, panel1)

    if not fast:
        inverse = second_factor(side, side, block, inverse0)
        total = lax.psum(crossed[0], "rows")
        share = P_SIZE // rows_n
        return lax.dynamic_slice_in_dim(nn(inverse, total), row * share, share, 0)
    with jax.named_scope("cross_sum"):
        keep, give = crossed
        on_chip = keep + before(swap(give), side)
    with jax.named_scope("factor1"):
        inverse = second_factor(on_chip, side, block, inverse0)
    with jax.named_scope("cross_sum"):
        total = on_chip[0]
        for j in range(1, chips):
            total = total + shift(on_chip[j], j)
    with jax.named_scope("solve"):
        solved = nn(inverse, total)
        return lax.all_to_all(solved, "rows", split_axis=0, concat_axis=1, tiled=True)


def solution(mesh):
    in_specs = (P("rows", "cols"), P(), P("rows", None), P("rows"), P("rows"))
    out_specs = P("rows", "cols")
    return jax.shard_map(local, mesh=mesh, in_specs=in_specs, out_specs=out_specs, check_vma=False)
```

```python
import functools
import jax
import jax.numpy as jnp
from jax import lax
from jax.experimental import pallas as pl
from jax.experimental.pallas import tpu as pltpu
from jax.sharding import PartitionSpec as P

TILE = 128
P_SIZE = 256
NB = 64
CHUNKS = 2
WIDTH = 16
HALF = P_SIZE // CHUNKS
SLICES = HALF // (2 * WIDTH)
BASE = 64
STEP = 8
F32, BF16, F16 = jnp.float32, jnp.bfloat16, jnp.float16
HI = lax.Precision.HIGHEST
MIB = 1 << 20


def vmem():
    return pl.BlockSpec(memory_space=pltpu.VMEM)


def smem():
    return pl.BlockSpec(memory_space=pltpu.SMEM)


def anywhere():
    return pl.BlockSpec(memory_space=pl.ANY)


def params(mib):
    return pltpu.CompilerParams(vmem_limit_bytes=mib * MIB)


def cost(flops, bytes_accessed):
    return pl.CostEstimate(flops=flops, bytes_accessed=bytes_accessed, transcendentals=0)


LIGHT = cost(10**6, 10**5)


def signed_mixer(mixers_ref, names_ref, tile):
    position = lax.broadcasted_iota(jnp.int32, (1, TILE), 1)
    hashed = (names_ref[4, tile] ^ position * 40503) * 69069
    sign = (1 - 2 * (hashed >> 16 & 1)).astype(F32)
    return mixers_ref[names_ref[3, tile]] * sign


def split(value):
    high = value.astype(BF16)
    return high, (value - high.astype(F32)).astype(BF16)


def product(mixer, block):
    mixer_high, mixer_low = split(mixer)
    block_high, block_low = split(block)
    wide = jnp.dot(jnp.concatenate([mixer_high, mixer_low], axis=0), block_high, preferred_element_type=F32)
    low = jnp.dot(mixer_high, block_low, preferred_element_type=F32)
    return wide[:TILE] + (wide[TILE:] + low)


def panel_kernel(per_step, names_ref, order_ref, matrix_ref, mixers_ref, *refs):
    outs, turned = refs[:-1], refs[-1]
    first = pl.program_id(0) * per_step
    core = order_ref[2 * SLICES + 1]
    for u in range(per_step):
        mixer = signed_mixer(mixers_ref, names_ref, first + u)
        block = matrix_ref[u * TILE : (u + 1) * TILE, :]
        turned[u] = product(mixer, block).T
        for h in range(CHUNKS):
            for c in range(SLICES):
                for s in range(2):
                    who = core if s == 0 else 1 - core
                    start = pl.multiple_of(h * HALF + who * (HALF // 2) + c * WIDTH, WIDTH)
                    outs[h * SLICES + c][s, u] = turned[u, pl.ds(start, WIDTH), :].astype(BF16)


def mix_panel(matrix, mixers, names, order):
    tiles = names.shape[1]
    per_step = 8
    spec = pl.BlockSpec((2, per_step, WIDTH, TILE), lambda i, *_: (0, i, 0, 0))
    return pl.pallas_call(
        functools.partial(panel_kernel, per_step),
        grid_spec=pltpu.PrefetchScalarGridSpec(
            num_scalar_prefetch=2,
            grid=(tiles // per_step,),
            in_specs=[
                pl.BlockSpec((per_step * TILE, P_SIZE), lambda i, *_: (i, 0)),
                pl.BlockSpec(mixers.shape, lambda i, *_: (0, 0, 0)),
            ],
            out_specs=[spec] * (CHUNKS * SLICES),
            scratch_shapes=[pltpu.VMEM((per_step, P_SIZE, TILE), F32)],
        ),
        out_shape=[jax.ShapeDtypeStruct((2, tiles, WIDTH, TILE), BF16)] * (CHUNKS * SLICES),
        compiler_params=params(49),
        cost_estimate=LIGHT,
        name="mix_panel",
    )(names, order, matrix, mixers)


def mix_kernel(per_step, start, names_ref, matrix_ref, mixers_ref, after_ref, out_ref, token_ref):
    first = start + pl.program_id(0) * per_step
    for u in range(per_step):
        mixer = signed_mixer(mixers_ref, names_ref, first + u)
        block = matrix_ref[u * TILE : (u + 1) * TILE, :]
        out_ref[u * TILE : (u + 1) * TILE, :] = product(mixer, block).astype(BF16)
    token_ref[...] = jnp.zeros_like(token_ref)


def mix_tiles(matrix, mixers, names, after, start, count):
    cols = matrix.shape[1]
    per_step = 4
    return pl.pallas_call(
        functools.partial(mix_kernel, per_step, start),
        grid_spec=pltpu.PrefetchScalarGridSpec(
            num_scalar_prefetch=1,
            grid=(count // per_step,),
            in_specs=[
                pl.BlockSpec((per_step * TILE, cols), lambda i, *_: (i + start // per_step, 0)),
                pl.BlockSpec(mixers.shape, lambda i, *_: (0, 0, 0)),
                anywhere(),
            ],
            out_specs=[
                pl.BlockSpec((per_step * TILE, cols), lambda i, *_: (i, 0)),
                pl.BlockSpec((8, TILE), lambda i, *_: (0, 0)),
            ],
        ),
        out_shape=[jax.ShapeDtypeStruct((count * TILE, cols), BF16), jax.ShapeDtypeStruct((8, TILE), F32)],
        compiler_params=params(49),
        cost_estimate=LIGHT,
        name="mix_tiles",
    )(names, matrix, mixers, after)


def pick_kernel(count, order_ref, after_ref, *refs):
    extra, sources, (keep_ref, give_ref) = refs[:count], refs[count:-2], refs[-2:]
    part = order_ref[2 * SLICES + 2]
    tiles = sources[0].shape[1]
    for j, source in enumerate(sources):
        taken = part == j if j else (part == 0) | (part >= len(sources))

        @pl.when(taken)
        def copy(source=source):
            keep_ref[:tiles] = source[0]
            give_ref[:tiles] = source[1]

    for i, ref in enumerate(extra):
        keep_ref[tiles + i] = ref[...]
        give_ref[tiles + i] = ref[...]


def pick(order, after, extra, sources):
    tiles = sources[0].shape[1] + len(extra)
    return pl.pallas_call(
        functools.partial(pick_kernel, len(extra)),
        in_specs=[smem(), anywhere()] + [vmem()] * (len(extra) + len(sources)),
        out_specs=[vmem()] * 2,
        out_shape=[jax.ShapeDtypeStruct((tiles, WIDTH, TILE), BF16)] * 2,
        compiler_params=params(16),
        cost_estimate=LIGHT,
        name="pick",
    )(order, after, *extra, *sources)


def add_tiles(names, stride, tiles, pieces, out_ref, total):
    total[...] = jnp.zeros_like(total)
    for j, piece in enumerate(pieces):
        for s in range(2):

            def add(i, carry, j=j, s=s, piece=piece):
                value = piece[s * stride + i].astype(F32)
                one, two = names[2 * j + s, 0, i], names[2 * j + s, 1, i]
                total[one] = total[one] + value
                total[two] = total[two] + names[2 * j + s, 2, i].astype(F32) * value
                return carry

            lax.fori_loop(0, tiles, add, 0, unroll=8)
    summed = total[...]
    largest = jnp.max(jnp.max(jnp.abs(summed), axis=0), axis=1, keepdims=True)
    out_ref[...] = summed * jnp.where(largest > 1e-37, 1.0 / largest, 1.0)


def first_sum_kernel(after_ref, *refs):
    pieces, (out_ref, names_ref, total, names, sem) = refs[:-5], refs[-5:]
    tiles = pieces[0].shape[0] // 2 - 1
    for j, piece in enumerate(pieces):
        for s in range(2):
            names_ref[2 * j + s] = piece[s * (tiles + 1) + tiles].astype(F32)[:8].astype(jnp.int32)
    copy = pltpu.make_async_copy(names_ref, names, sem)
    copy.start()
    copy.wait()
    add_tiles(names, tiles + 1, tiles, pieces, out_ref, total)


def first_sum(after, pieces):
    names = (2 * len(pieces), 8, TILE)
    return pl.pallas_call(
        first_sum_kernel,
        in_specs=[anywhere()] + [vmem()] * len(pieces),
        out_specs=[vmem()] * 2,
        out_shape=[jax.ShapeDtypeStruct((NB, WIDTH, TILE), F32), jax.ShapeDtypeStruct(names, jnp.int32)],
        scratch_shapes=[pltpu.VMEM((NB, WIDTH, TILE), F32), pltpu.SMEM(names, jnp.int32), pltpu.SemaphoreType.DMA],
        compiler_params=params(24),
        cost_estimate=LIGHT,
        name="first_sum",
    )(after, *pieces)


def next_sum_kernel(names, after_ref, *refs):
    pieces, (out_ref, total) = refs[:-2], refs[-2:]
    tiles = pieces[0].shape[0] // 2
    add_tiles(names, tiles, tiles, pieces, out_ref, total)


def next_sum(names, after, pieces):
    return pl.pallas_call(
        next_sum_kernel,
        in_specs=[smem(), anywhere()] + [vmem()] * len(pieces),
        out_specs=vmem(),
        out_shape=jax.ShapeDtypeStruct((NB, WIDTH, TILE), F32),
        scratch_shapes=[pltpu.VMEM((NB, WIDTH, TILE), F32)],
        compiler_params=params(24),
        cost_estimate=LIGHT,
        name="next_sum",
    )(names, after, *pieces)


def nt(a, b, precision=None):
    return lax.dot_general(a, b, (((1,), (1,)), ((), ())), precision=precision, preferred_element_type=F32)


def nn(a, b):
    return jnp.dot(a, b, precision=HI, preferred_element_type=F32)


def join(order_ref, pieces, panel):
    for q, piece in enumerate(pieces):
        panel[:, pl.ds(pl.multiple_of(order_ref[q] * WIDTH, WIDTH), WIDTH), :] = piece[...]


def cross_kernel(steps, chips, earlier, fast, names_ref, order_ref, after_ref, *refs):
    mixed, refs = refs[: len(steps)], refs[len(steps) :]
    pieces, refs = refs[: 2 * SLICES], refs[2 * SLICES :]
    before, refs = refs[:earlier], refs[earlier:]
    panel, outs, total = refs[0], refs[1:-1], refs[-1]
    step = pl.program_id(0)

    @pl.when(step == 0)
    def start():
        total[...] = jnp.zeros_like(total)
        join(order_ref, pieces, panel)

    high, low = [], []
    for u in range(STEP):
        t = STEP * step + u
        one, two = split(panel[names_ref[0, t]] + names_ref[2, t].astype(F32) * panel[names_ref[1, t]])
        high.append(one)
        low.append(two)
    weights = jnp.concatenate([jnp.concatenate(high, axis=1), jnp.concatenate(low, axis=1)], axis=0)

    begin = 0
    for count, mixed_ref in zip(steps, mixed):

        @pl.when((step >= begin) & (step < begin + count))
        def add(mixed_ref=mixed_ref):
            total[...] += jnp.dot(weights, mixed_ref[...], preferred_element_type=F32)

        begin += count

    @pl.when(step == pl.num_programs(0) - 1)
    def finish():
        total[:HALF, :] = total[:HALF, :] + total[HALF:, :]
        rows = earlier and HALF
        for ref, out in zip(before, outs):
            out[..., :HALF, :] = ref[...]
        if not fast:
            outs[0][rows:, :] = total[:HALF, :]
        else:
            chip, core = order_ref[2 * SLICES], order_ref[2 * SLICES + 1]
            for s in range(2):
                who = core if s == 0 else 1 - core
                for j in range(chips):
                    at = (2 * lax.rem(chip + j, chips) + who) * TILE
                    outs[s][j, rows:, :] = total[:HALF, pl.ds(pl.multiple_of(at, TILE), TILE)]


def cross_parts(names, order, after, mixed, pieces, before, chips, fast):
    cols = mixed[0].shape[1]
    steps = [v.shape[0] // (STEP * TILE) for v in mixed]
    rows = 2 * HALF if before else HALF
    if fast:
        outs = [jax.ShapeDtypeStruct((chips, rows, TILE), F32)] * 2
    else:
        outs = [jax.ShapeDtypeStruct((rows, cols), F32)]
    outs = [jax.ShapeDtypeStruct((NB, HALF, TILE), F32)] + outs
    begins = [sum(steps[:i]) for i in range(len(steps))]
    blocks = [
        pl.BlockSpec((STEP * TILE, cols), lambda i, b=begin, n=count: (jnp.clip(i - b, 0, n - 1), 0))
        for begin, count in zip(begins, steps)
    ]
    return pl.pallas_call(
        functools.partial(cross_kernel, steps, chips, len(before), fast),
        grid=(sum(steps),),
        in_specs=[smem(), smem(), anywhere()] + blocks + [vmem()] * (len(pieces) + len(before)),
        out_specs=[vmem()] * len(outs),
        out_shape=outs,
        scratch_shapes=[pltpu.VMEM((2 * HALF, cols), F32)],
        compiler_params=params(32),
        cost_estimate=LIGHT,
        name="cross_parts",
    )(names, order, after, *mixed, *pieces, *before)


def above(value):
    return jnp.concatenate([value[:1], value[:-1]], axis=0)


def factor_inverse(block):
    row = lax.broadcasted_iota(jnp.int32, (BASE, BASE), 0)
    lane = lax.broadcasted_iota(jnp.int32, (BASE, BASE), 1)
    eye = (row == lane).astype(F32)
    wide = jnp.concatenate([block, eye], axis=1)
    slabs = [wide[8 * g : 8 * g + 8, :] for g in range(BASE // 8)]
    place = lax.broadcasted_iota(jnp.int32, (8, 2 * BASE), 0)

    def full(value):
        return jnp.broadcast_to(value, (8, 2 * BASE))

    for j in range(0, BASE, 2):
        own, at = j // 8, j % 8
        slab = slabs[own]
        col0, col1 = full(slab[:, j : j + 1]), full(slab[:, j + 1 : j + 2])
        row0, row1 = full(slab[at : at + 1, :]), full(slab[at + 1 : at + 2, :])
        first, cross, second = full(col0[at : at + 1, :]), full(col1[at : at + 1, :]), full(col1[at + 1 : at + 2, :])
        scale = 1.0 / (first * second - cross * cross)
        solved0 = (second * row0 - cross * row1) * scale
        solved1 = (first * row1 - cross * row0) * scale
        for g in range(own, BASE // 8):
            if g == own:
                col0, col1 = jnp.where(place > at + 1, col0, 0.0), jnp.where(place > at + 1, col1, 0.0)
            else:
                col0, col1 = slabs[g][:, j : j + 1], slabs[g][:, j + 1 : j + 2]
            slabs[g] = slabs[g] - col0 * solved0 - col1 * solved1
    wide = jnp.concatenate(slabs, axis=0)
    diagonal = jnp.sum(wide[:, :BASE] * eye, axis=1, keepdims=True)
    beside = jnp.sum(jnp.where(lane == row + 1, wide[:, :BASE], 0.0), axis=1, keepdims=True)
    odd = row[:, :1] % 2 == 1
    ratio = jnp.where(odd, above(beside) / above(diagonal), 0.0)
    pivots = jnp.where(odd, diagonal - above(beside) * ratio, diagonal)
    return (wide - ratio * above(wide))[:, BASE:] * lax.rsqrt(pivots)


def factor_inverse_pair(block):
    first = factor_inverse(block[:BASE, :BASE])
    side = nt(block[BASE:, :BASE], first, HI)
    second = factor_inverse(block[BASE:, BASE:] - nt(side, side, HI))
    corner = -nn(second, nn(side, first))
    top = jnp.concatenate([first, jnp.zeros_like(first)], axis=1)
    return jnp.concatenate([top, jnp.concatenate([corner, second], axis=1)], axis=0)


GROUP = 8


def wide_buckets(panel, i):
    return jnp.concatenate([panel[GROUP * i + u] for u in range(GROUP)], axis=1)


def first_kernel(after_ref, panel, out_ref, acc):
    acc[...] = jnp.zeros_like(acc)

    def step(i, carry):
        one, two = split(wide_buckets(panel, i))
        acc[...] += nt(jnp.concatenate([one, two], axis=0), one)
        return carry

    lax.fori_loop(0, NB // GROUP, step, 0)
    mixed = acc[HALF:, :]
    out_ref[...] = acc[:HALF, :] + (mixed + mixed.T)


def first_gram(after, panel):
    return pl.pallas_call(
        first_kernel,
        in_specs=[anywhere(), vmem()],
        out_specs=vmem(),
        out_shape=jax.ShapeDtypeStruct((HALF, HALF), F32),
        scratch_shapes=[pltpu.VMEM((2 * HALF, HALF), F32)],
        compiler_params=params(32),
        cost_estimate=LIGHT,
        name="first_gram",
    )(after, panel)


def factor_kernel(block_ref, out_ref):
    out_ref[...] = factor_inverse_pair(block_ref[...])


def first_factor(block):
    return pl.pallas_call(
        factor_kernel,
        in_specs=[vmem()],
        out_specs=vmem(),
        out_shape=jax.ShapeDtypeStruct((HALF, HALF), F32),
        compiler_params=params(16),
        cost_estimate=LIGHT,
        name="first_factor",
    )(block)


def second_kernel(after_ref, panel0, panel1, side_ref, block_ref, acc, extra):
    acc[...] = jnp.zeros_like(acc)
    extra[...] = jnp.zeros_like(extra)

    def step(i, carry):
        one0, two0 = split(wide_buckets(panel0, i))
        one1, two1 = split(wide_buckets(panel1, i))
        acc[...] += nt(jnp.concatenate([one1, two1], axis=0), jnp.concatenate([one0, one1], axis=0))
        extra[...] += nt(one1, two0)
        return carry

    lax.fori_loop(0, NB // GROUP, step, 0)
    side_ref[...] = acc[:HALF, :HALF] + (acc[HALF:, :HALF] + extra[...])
    mixed = acc[HALF:, HALF:]
    block_ref[...] = acc[:HALF, HALF:] + (mixed + mixed.T)


def second_gram(after, panel0, panel1):
    return pl.pallas_call(
        second_kernel,
        in_specs=[anywhere()] + [vmem()] * 2,
        out_specs=[vmem()] * 2,
        out_shape=[jax.ShapeDtypeStruct((HALF, HALF), F32)] * 2,
        scratch_shapes=[pltpu.VMEM((2 * HALF, 2 * HALF), F32), pltpu.VMEM((HALF, HALF), F32)],
        compiler_params=params(32),
        cost_estimate=LIGHT,
        name="second_gram",
    )(after, panel0, panel1)


def last_kernel(after_ref, side_ref, block_ref, inverse_ref, out_ref):
    first = inverse_ref[...]
    side = nt(side_ref[...], first, HI)
    second = factor_inverse_pair(block_ref[...] - nt(side, side, HI))
    out_ref[:HALF, :HALF] = first
    out_ref[:HALF, HALF:] = jnp.zeros_like(first)
    out_ref[HALF:, :HALF] = -nn(second, nn(side, first))
    out_ref[HALF:, HALF:] = second


def second_factor(after, side, block, inverse):
    return pl.pallas_call(
        last_kernel,
        in_specs=[anywhere()] + [vmem()] * 3,
        out_specs=vmem(),
        out_shape=jax.ShapeDtypeStruct((P_SIZE, P_SIZE), F32),
        compiler_params=params(32),
        cost_estimate=LIGHT,
        name="second_factor",
    )(after, side, block, inverse)


def local(matrix, mixers, bucket_pair, mixer_index, sign_seed):
    cols = matrix.shape[1]
    rows_n, parts = lax.axis_size("rows"), lax.axis_size("cols")
    chips = rows_n // 2
    row, part = lax.axis_index("rows"), lax.axis_index("cols")
    core, chip = row % 2, row // 2

    def swap(value):
        return lax.ppermute(value, "rows", [(i, i ^ 1) for i in range(rows_n)])

    def shift(value, j):
        return lax.ppermute(value, "rows", [(i, (i + 2 * j) % rows_n) for i in range(rows_n)])

    def beside(value, j):
        return lax.ppermute(value, "rows", [(i, i ^ 2 * j) for i in range(rows_n)])

    def across(value, j):
        return lax.ppermute(value, "cols", [(i, i ^ j) for i in range(parts)])

    fast = cols % (TILE * rows_n) == 0
    with jax.named_scope("names"):
        flips = 1 - 2 * (sign_seed >> 29 & 1)
        names = jnp.stack([bucket_pair[:, 0], bucket_pair[:, 1], flips, mixer_index, sign_seed])
        place = [part ^ j if parts == SLICES else j for j in range(SLICES)]
        order = [who * SLICES + c for who in (core, 1 - core) for c in place]
        order = jnp.stack([jnp.asarray(v, jnp.int32) for v in order + [chip, core, part]])
    with jax.named_scope("panel_mix"):
        tiles = mix_panel(matrix, mixers, names, order)
    with jax.named_scope("names"):
        carried = jnp.pad(names[:3].astype(BF16), ((0, WIDTH - 3), (0, TILE - names.shape[1])))

    def before(values, *others):
        return lax.optimization_barrier((values, others))[0]

    def scatter(h):
        with jax.named_scope("panel_spread"):
            slices = tiles[h * SLICES : (h + 1) * SLICES]
            return [slices[0]] + [lax.ppermute(slices[j], "cols", [(0, j)]) for j in range(1, SLICES)]

    def spread(got, after, *extra):
        with jax.named_scope("panel_spread"):
            keep, give = pick(order, after, extra, got)
            return jnp.concatenate([keep, swap(give)])

    def gather_rows(held):
        with jax.named_scope("panel_rows"):
            if chips != 4:
                return [held] + [shift(held, j) for j in range(1, chips)]
            far, near = beside(held, 2), beside(held, 1)
            return [held, far, near, beside(far, 1)]

    def gather_cols(summed):
        with jax.named_scope("panel_cols"):
            sent = summed.astype(F16)
            if parts == SLICES:
                return [sent] + [across(sent, j) for j in range(1, parts)]
            return list(lax.all_gather(sent, "cols")[:SLICES])

    def both_cores(mine):
        with jax.named_scope("panel_cores"):
            return [v.astype(F32) for v in mine + [swap(v) for v in mine]]

    mixed = []

    def mix_next(after, count):
        for _ in range(count):
            with jax.named_scope("mix"):
                more, after = mix_tiles(matrix, mixers, names, after, len(mixed) * STEP, STEP)
            mixed.append(more)
        return after

    early = names.shape[1] // STEP // 2
    token = mix_next(tiles[0], early)
    held0 = spread(scatter(0), token, carried)
    held1 = spread(scatter(1), token)
    arrived0, arrived1 = gather_rows(held0), gather_rows(held1)
    token = mix_next(held1, names.shape[1] // STEP - early)
    with jax.named_scope("panel_sum"):
        summed0, all_names = first_sum(token, arrived0)
    mine0 = gather_cols(summed0)
    with jax.named_scope("panel_sum"):
        summed1 = next_sum(all_names, summed0, arrived1)
    mine1 = gather_cols(summed1)
    pieces0 = both_cores(before(mine0, summed1))
    with jax.named_scope("cross0"):
        panel0, *crossed0 = cross_parts(names, order, summed1, mixed, pieces0, [], chips, fast)
    with jax.named_scope("factor0"):
        inverse0 = first_factor(first_gram(crossed0[0], panel0))
    pieces1 = both_cores(before(mine1, inverse0, crossed0[0]))
    with jax.named_scope("cross1"):
        panel1, *crossed = cross_parts(names, order, inverse0, mixed, pieces1, crossed0, chips, fast)
    with jax.named_scope("gram1"):
        side, block = second_gram(crossed[0], panel0, panel1)

    if not fast:
        inverse = second_factor(side, side, block, inverse0)
        total = lax.psum(crossed[0], "rows")
        share = P_SIZE // rows_n
        return lax.dynamic_slice_in_dim(nn(inverse, total), row * share, share, 0)
    with jax.named_scope("cross_sum"):
        keep, give = crossed
        on_chip = keep + before(swap(give), side)
    with jax.named_scope("factor1"):
        inverse = second_factor(on_chip, side, block, inverse0)
    with jax.named_scope("cross_sum"):
        total = on_chip[0]
        for j in range(1, chips):
            total = total + shift(on_chip[j], j)
    with jax.named_scope("solve"):
        solved = nn(inverse, total)
        return lax.all_to_all(solved, "rows", split_axis=0, concat_axis=1, tiled=True)


def solution(mesh):
    in_specs = (P("rows", "cols"), P(), P("rows", None), P("rows"), P("rows"))
    out_specs = P("rows", "cols")
    return jax.shard_map(local, mesh=mesh, in_specs=in_specs, out_specs=out_specs, check_vma=False)
```

```python
import functools
import jax
import jax.numpy as jnp
from jax import lax
from jax.experimental import pallas as pl
from jax.experimental.pallas import tpu as pltpu
from jax.sharding import PartitionSpec as P

TILE = 128
P_SIZE = 256
NB = 64
CHUNKS = 2
WIDTH = 16
HALF = P_SIZE // CHUNKS
SLICES = HALF // (2 * WIDTH)
BASE = 64
STEP = 8
F32, BF16, F16 = jnp.float32, jnp.bfloat16, jnp.float16
HI = lax.Precision.HIGHEST
MIB = 1 << 20


def vmem():
    return pl.BlockSpec(memory_space=pltpu.VMEM)


def smem():
    return pl.BlockSpec(memory_space=pltpu.SMEM)


def anywhere():
    return pl.BlockSpec(memory_space=pl.ANY)


def params(mib):
    return pltpu.CompilerParams(vmem_limit_bytes=mib * MIB)


def cost(flops, bytes_accessed):
    return pl.CostEstimate(flops=flops, bytes_accessed=bytes_accessed, transcendentals=0)


LIGHT = cost(10**6, 10**5)


def signed_mixer(mixers_ref, names_ref, tile):
    position = lax.broadcasted_iota(jnp.int32, (1, TILE), 1)
    hashed = (names_ref[1, tile] ^ position * 40503) * 69069
    sign = (1 - 2 * (hashed >> 16 & 1)).astype(F32)
    return mixers_ref[names_ref[0, tile]] * sign


def split(value):
    high = value.astype(BF16)
    return high, (value - high.astype(F32)).astype(BF16)


def product(mixer, block):
    mixer_high, mixer_low = split(mixer)
    block_high, block_low = split(block)
    wide = jnp.dot(jnp.concatenate([mixer_high, mixer_low], axis=0), block_high, preferred_element_type=F32)
    low = jnp.dot(mixer_high, block_low, preferred_element_type=F32)
    return wide[:TILE] + (wide[TILE:] + low)


def panel_kernel(per_step, names_ref, order_ref, matrix_ref, mixers_ref, *refs):
    outs, turned = refs[:-1], refs[-1]
    first = pl.program_id(0) * per_step
    core = order_ref[2 * SLICES + 1]
    for u in range(per_step):
        mixer = signed_mixer(mixers_ref, names_ref, first + u)
        block = matrix_ref[u * TILE : (u + 1) * TILE, :]
        turned[u] = product(mixer, block).T
        for h in range(CHUNKS):
            for c in range(SLICES):
                for s in range(2):
                    who = core if s == 0 else 1 - core
                    start = pl.multiple_of(h * HALF + who * (HALF // 2) + c * WIDTH, WIDTH)
                    outs[h * SLICES + c][s, u] = turned[u, pl.ds(start, WIDTH), :].astype(BF16)


def mix_panel(matrix, mixers, names, order):
    tiles = names.shape[1]
    per_step = 8
    spec = pl.BlockSpec((2, per_step, WIDTH, TILE), lambda i, *_: (0, i, 0, 0))
    return pl.pallas_call(
        functools.partial(panel_kernel, per_step),
        grid_spec=pltpu.PrefetchScalarGridSpec(
            num_scalar_prefetch=2,
            grid=(tiles // per_step,),
            in_specs=[
                pl.BlockSpec((per_step * TILE, P_SIZE), lambda i, *_: (i, 0)),
                pl.BlockSpec(mixers.shape, lambda i, *_: (0, 0, 0)),
            ],
            out_specs=[spec] * (CHUNKS * SLICES),
            scratch_shapes=[pltpu.VMEM((per_step, P_SIZE, TILE), F32)],
        ),
        out_shape=[jax.ShapeDtypeStruct((2, tiles, WIDTH, TILE), BF16)] * (CHUNKS * SLICES),
        compiler_params=params(49),
        cost_estimate=LIGHT,
        name="mix_panel",
    )(names, order, matrix, mixers)


def mix_kernel(per_step, start, names_ref, matrix_ref, mixers_ref, after_ref, out_ref, token_ref):
    first = start + pl.program_id(0) * per_step
    for u in range(per_step):
        mixer = signed_mixer(mixers_ref, names_ref, first + u)
        block = matrix_ref[u * TILE : (u + 1) * TILE, :]
        out_ref[u * TILE : (u + 1) * TILE, :] = product(mixer, block).astype(BF16)
    token_ref[...] = jnp.zeros_like(token_ref)


def mix_tiles(matrix, mixers, names, after, start, count):
    cols = matrix.shape[1]
    per_step = 4
    return pl.pallas_call(
        functools.partial(mix_kernel, per_step, start),
        grid_spec=pltpu.PrefetchScalarGridSpec(
            num_scalar_prefetch=1,
            grid=(count // per_step,),
            in_specs=[
                pl.BlockSpec((per_step * TILE, cols), lambda i, *_: (i + start // per_step, 0)),
                pl.BlockSpec(mixers.shape, lambda i, *_: (0, 0, 0)),
                anywhere(),
            ],
            out_specs=[
                pl.BlockSpec((per_step * TILE, cols), lambda i, *_: (i, 0)),
                pl.BlockSpec((8, TILE), lambda i, *_: (0, 0)),
            ],
        ),
        out_shape=[jax.ShapeDtypeStruct((count * TILE, cols), BF16), jax.ShapeDtypeStruct((8, TILE), F32)],
        compiler_params=params(49),
        cost_estimate=LIGHT,
        name="mix_tiles",
    )(names, matrix, mixers, after)


def pick_kernel(count, order_ref, after_ref, *refs):
    extra, sources, (keep_ref, give_ref) = refs[:count], refs[count:-2], refs[-2:]
    part = order_ref[2 * SLICES + 2]
    tiles = sources[0].shape[1]
    for j, source in enumerate(sources):
        taken = part == j if j else (part == 0) | (part >= len(sources))

        @pl.when(taken)
        def copy(source=source):
            keep_ref[:tiles] = source[0]
            give_ref[:tiles] = source[1]

    for i, ref in enumerate(extra):
        keep_ref[tiles + i] = ref[...]
        give_ref[tiles + i] = ref[...]


def pick(order, after, extra, sources):
    tiles = sources[0].shape[1] + len(extra)
    return pl.pallas_call(
        functools.partial(pick_kernel, len(extra)),
        in_specs=[smem(), anywhere()] + [vmem()] * (len(extra) + len(sources)),
        out_specs=[vmem()] * 2,
        out_shape=[jax.ShapeDtypeStruct((tiles, WIDTH, TILE), BF16)] * 2,
        compiler_params=params(16),
        cost_estimate=LIGHT,
        name="pick",
    )(order, after, *extra, *sources)


def add_tiles(names, stride, tiles, pieces, out_ref, total):
    total[...] = jnp.zeros_like(total)
    for j, piece in enumerate(pieces):
        for s in range(2):

            def add(i, carry, j=j, s=s, piece=piece):
                value = piece[s * stride + i].astype(F32)
                one, two = names[2 * j + s, 0, i], names[2 * j + s, 1, i]
                total[one] = total[one] + value
                total[two] = total[two] + names[2 * j + s, 2, i].astype(F32) * value
                return carry

            lax.fori_loop(0, tiles, add, 0, unroll=8)
    summed = total[...]
    largest = jnp.max(jnp.max(jnp.abs(summed), axis=0), axis=1, keepdims=True)
    out_ref[...] = summed * jnp.where(largest > 1e-37, 1.0 / largest, 1.0)


def first_sum_kernel(after_ref, *refs):
    pieces, (out_ref, names_ref, total, names, sem) = refs[:-5], refs[-5:]
    tiles = pieces[0].shape[0] // 2 - 1
    for j, piece in enumerate(pieces):
        for s in range(2):
            names_ref[2 * j + s] = piece[s * (tiles + 1) + tiles].astype(F32)[:8].astype(jnp.int32)
    copy = pltpu.make_async_copy(names_ref, names, sem)
    copy.start()
    copy.wait()
    add_tiles(names, tiles + 1, tiles, pieces, out_ref, total)


def first_sum(after, pieces):
    names = (2 * len(pieces), 8, TILE)
    return pl.pallas_call(
        first_sum_kernel,
        in_specs=[anywhere()] + [vmem()] * len(pieces),
        out_specs=[vmem()] * 2,
        out_shape=[jax.ShapeDtypeStruct((NB, WIDTH, TILE), F32), jax.ShapeDtypeStruct(names, jnp.int32)],
        scratch_shapes=[pltpu.VMEM((NB, WIDTH, TILE), F32), pltpu.SMEM(names, jnp.int32), pltpu.SemaphoreType.DMA],
        compiler_params=params(24),
        cost_estimate=LIGHT,
        name="first_sum",
    )(after, *pieces)


def next_sum_kernel(names, after_ref, *refs):
    pieces, (out_ref, total) = refs[:-2], refs[-2:]
    tiles = pieces[0].shape[0] // 2
    add_tiles(names, tiles, tiles, pieces, out_ref, total)


def next_sum(names, after, pieces):
    return pl.pallas_call(
        next_sum_kernel,
        in_specs=[smem(), anywhere()] + [vmem()] * len(pieces),
        out_specs=vmem(),
        out_shape=jax.ShapeDtypeStruct((NB, WIDTH, TILE), F32),
        scratch_shapes=[pltpu.VMEM((NB, WIDTH, TILE), F32)],
        compiler_params=params(24),
        cost_estimate=LIGHT,
        name="next_sum",
    )(names, after, *pieces)


def nt(a, b, precision=None):
    return lax.dot_general(a, b, (((1,), (1,)), ((), ())), precision=precision, preferred_element_type=F32)


def nn(a, b):
    return jnp.dot(a, b, precision=HI, preferred_element_type=F32)


def join(order_ref, pieces, panel):
    for q, piece in enumerate(pieces):
        panel[:, pl.ds(pl.multiple_of(order_ref[q] * WIDTH, WIDTH), WIDTH), :] = piece[...]


def cross_kernel(steps, chips, earlier, fast, names_ref, order_ref, after_ref, *refs):
    mixed, refs = refs[: len(steps)], refs[len(steps) :]
    pieces, refs = refs[: 2 * SLICES], refs[2 * SLICES :]
    before, refs = refs[:earlier], refs[earlier:]
    panel, outs, total = refs[0], refs[1:-1], refs[-1]
    step = pl.program_id(0)

    @pl.when(step == 0)
    def start():
        total[...] = jnp.zeros_like(total)
        join(order_ref, pieces, panel)

    high, low = [], []
    for u in range(STEP):
        t = STEP * step + u
        one, two = split(panel[names_ref[0, t]] + names_ref[2, t].astype(F32) * panel[names_ref[1, t]])
        high.append(one)
        low.append(two)
    weights = jnp.concatenate([jnp.concatenate(high, axis=1), jnp.concatenate(low, axis=1)], axis=0)

    begin = 0
    for count, mixed_ref in zip(steps, mixed):

        @pl.when((step >= begin) & (step < begin + count))
        def add(mixed_ref=mixed_ref):
            total[...] += jnp.dot(weights, mixed_ref[...], preferred_element_type=F32)

        begin += count

    @pl.when(step == pl.num_programs(0) - 1)
    def finish():
        total[:HALF, :] = total[:HALF, :] + total[HALF:, :]
        rows = earlier and HALF
        for ref, out in zip(before, outs):
            out[..., :HALF, :] = ref[...]
        if not fast:
            outs[0][rows:, :] = total[:HALF, :]
        else:
            chip, core = order_ref[2 * SLICES], order_ref[2 * SLICES + 1]
            for s in range(2):
                who = core if s == 0 else 1 - core
                for j in range(chips):
                    at = (2 * lax.rem(chip + j, chips) + who) * TILE
                    outs[s][j, rows:, :] = total[:HALF, pl.ds(pl.multiple_of(at, TILE), TILE)]


def cross_parts(names, order, after, mixed, pieces, before, chips, fast):
    cols = mixed[0].shape[1]
    steps = [v.shape[0] // (STEP * TILE) for v in mixed]
    rows = 2 * HALF if before else HALF
    if fast:
        outs = [jax.ShapeDtypeStruct((chips, rows, TILE), F32)] * 2
    else:
        outs = [jax.ShapeDtypeStruct((rows, cols), F32)]
    outs = [jax.ShapeDtypeStruct((NB, HALF, TILE), F32)] + outs
    begins = [sum(steps[:i]) for i in range(len(steps))]
    blocks = [
        pl.BlockSpec((STEP * TILE, cols), lambda i, b=begin, n=count: (jnp.clip(i - b, 0, n - 1), 0))
        for begin, count in zip(begins, steps)
    ]
    return pl.pallas_call(
        functools.partial(cross_kernel, steps, chips, len(before), fast),
        grid=(sum(steps),),
        in_specs=[smem(), smem(), anywhere()] + blocks + [vmem()] * (len(pieces) + len(before)),
        out_specs=[vmem()] * len(outs),
        out_shape=outs,
        scratch_shapes=[pltpu.VMEM((2 * HALF, cols), F32)],
        compiler_params=params(32),
        cost_estimate=LIGHT,
        name="cross_parts",
    )(names, order, after, *mixed, *pieces, *before)


def factor_inverse(block):
    row = lax.broadcasted_iota(jnp.int32, (BASE, BASE), 0)
    lane = lax.broadcasted_iota(jnp.int32, (BASE, BASE), 1)
    wide = jnp.concatenate([block, (row == lane).astype(F32)], axis=1)
    slabs = [wide[8 * g : 8 * g + 8, :] for g in range(BASE // 8)]
    place = lax.broadcasted_iota(jnp.int32, (8, 2 * BASE), 0)

    def full(value):
        return jnp.broadcast_to(value, (8, 2 * BASE))

    done = []
    for own in range(BASE // 8):
        slab, first = slabs[own], 8 * own
        cols = [full(slab[:, first + k : first + k + 1]) for k in range(8)]
        rows = [full(slab[k : k + 1, :]) for k in range(8)]
        entry = {(a, b): full(cols[b][a : a + 1, :]) for a in range(8) for b in range(a, 8)}
        factor, scale = {}, []
        for k in range(8):
            scale.append(1.0 / entry[k, k])
            for a in range(k + 1, 8):
                factor[a, k] = entry[k, a] * scale[k]
            for a in range(k + 1, 8):
                for b in range(a, 8):
                    entry[a, b] = entry[a, b] - factor[a, k] * entry[k, b]
                rows[a] = rows[a] - factor[a, k] * rows[k]
        solved = [None] * 8
        for k in reversed(range(8)):
            value = rows[k] * scale[k]
            for m in range(k + 1, 8):
                value = value - factor[m, k] * solved[m]
            solved[k] = value
        for g in range(own + 1, BASE // 8):
            before = slabs[g]
            for k in range(8):
                slabs[g] = slabs[g] - before[:, first + k : first + k + 1] * solved[k]
        out = jnp.zeros((8, 2 * BASE), F32)
        for k in range(8):
            out = jnp.where(place == k, rows[k] * lax.rsqrt(entry[k, k]), out)
        done.append(out)
    return jnp.concatenate(done, axis=0)[:, BASE:]


def factor_inverse_pair(block):
    first = factor_inverse(block[:BASE, :BASE])
    side = nt(block[BASE:, :BASE], first, HI)
    second = factor_inverse(block[BASE:, BASE:] - nt(side, side, HI))
    corner = -nn(second, nn(side, first))
    top = jnp.concatenate([first, jnp.zeros_like(first)], axis=1)
    return jnp.concatenate([top, jnp.concatenate([corner, second], axis=1)], axis=0)


GROUP = 8


def wide_buckets(panel, i):
    return jnp.concatenate([panel[GROUP * i + u] for u in range(GROUP)], axis=1)


def first_kernel(after_ref, panel, out_ref, acc):
    acc[...] = jnp.zeros_like(acc)

    def step(i, carry):
        one, two = split(wide_buckets(panel, i))
        acc[...] += nt(jnp.concatenate([one, two], axis=0), one)
        return carry

    lax.fori_loop(0, NB // GROUP, step, 0)
    mixed = acc[HALF:, :]
    out_ref[...] = acc[:HALF, :] + (mixed + mixed.T)


def first_gram(after, panel):
    return pl.pallas_call(
        first_kernel,
        in_specs=[anywhere(), vmem()],
        out_specs=vmem(),
        out_shape=jax.ShapeDtypeStruct((HALF, HALF), F32),
        scratch_shapes=[pltpu.VMEM((2 * HALF, HALF), F32)],
        compiler_params=params(32),
        cost_estimate=LIGHT,
        name="first_gram",
    )(after, panel)


def factor_kernel(block_ref, out_ref):
    out_ref[...] = factor_inverse_pair(block_ref[...])


def first_factor(block):
    return pl.pallas_call(
        factor_kernel,
        in_specs=[vmem()],
        out_specs=vmem(),
        out_shape=jax.ShapeDtypeStruct((HALF, HALF), F32),
        compiler_params=params(16),
        cost_estimate=LIGHT,
        name="first_factor",
    )(block)


def second_kernel(after_ref, panel0, panel1, side_ref, block_ref, acc, extra):
    acc[...] = jnp.zeros_like(acc)
    extra[...] = jnp.zeros_like(extra)

    def step(i, carry):
        one0, two0 = split(wide_buckets(panel0, i))
        one1, two1 = split(wide_buckets(panel1, i))
        acc[...] += nt(jnp.concatenate([one1, two1], axis=0), jnp.concatenate([one0, one1], axis=0))
        extra[...] += nt(one1, two0)
        return carry

    lax.fori_loop(0, NB // GROUP, step, 0)
    side_ref[...] = acc[:HALF, :HALF] + (acc[HALF:, :HALF] + extra[...])
    mixed = acc[HALF:, HALF:]
    block_ref[...] = acc[:HALF, HALF:] + (mixed + mixed.T)


def second_gram(after, panel0, panel1):
    return pl.pallas_call(
        second_kernel,
        in_specs=[anywhere()] + [vmem()] * 2,
        out_specs=[vmem()] * 2,
        out_shape=[jax.ShapeDtypeStruct((HALF, HALF), F32)] * 2,
        scratch_shapes=[pltpu.VMEM((2 * HALF, 2 * HALF), F32), pltpu.VMEM((HALF, HALF), F32)],
        compiler_params=params(32),
        cost_estimate=LIGHT,
        name="second_gram",
    )(after, panel0, panel1)


def last_kernel(after_ref, side_ref, block_ref, inverse_ref, out_ref):
    first = inverse_ref[...]
    side = nt(side_ref[...], first, HI)
    second = factor_inverse_pair(block_ref[...] - nt(side, side, HI))
    out_ref[:HALF, :HALF] = first
    out_ref[:HALF, HALF:] = jnp.zeros_like(first)
    out_ref[HALF:, :HALF] = -nn(second, nn(side, first))
    out_ref[HALF:, HALF:] = second


def second_factor(after, side, block, inverse):
    return pl.pallas_call(
        last_kernel,
        in_specs=[anywhere()] + [vmem()] * 3,
        out_specs=vmem(),
        out_shape=jax.ShapeDtypeStruct((P_SIZE, P_SIZE), F32),
        compiler_params=params(32),
        cost_estimate=LIGHT,
        name="second_factor",
    )(after, side, block, inverse)


def local(matrix, mixers, bucket_pair, mixer_index, sign_seed):
    cols = matrix.shape[1]
    rows_n, parts = lax.axis_size("rows"), lax.axis_size("cols")
    chips = rows_n // 2
    row, part = lax.axis_index("rows"), lax.axis_index("cols")
    core, chip = row % 2, row // 2

    def swap(value):
        return lax.ppermute(value, "rows", [(i, i ^ 1) for i in range(rows_n)])

    def shift(value, j):
        return lax.ppermute(value, "rows", [(i, (i + 2 * j) % rows_n) for i in range(rows_n)])

    def beside(value, j):
        return lax.ppermute(value, "rows", [(i, i ^ 2 * j) for i in range(rows_n)])

    def across(value, j):
        return lax.ppermute(value, "cols", [(i, i ^ j) for i in range(parts)])

    fast = cols % (TILE * rows_n) == 0
    with jax.named_scope("names"):
        flips = 1 - 2 * (sign_seed >> 29 & 1)
        names = jnp.concatenate([bucket_pair.T, flips[None]])
        kinds = jnp.stack([mixer_index, sign_seed])
        place = [part ^ j if parts == SLICES else j for j in range(SLICES)]
        order = [who * SLICES + c for who in (core, 1 - core) for c in place]
        order = jnp.stack([jnp.asarray(v, jnp.int32) for v in order + [chip, core, part]])
    with jax.named_scope("panel_mix"):
        tiles = mix_panel(matrix, mixers, kinds, order)
    with jax.named_scope("names"):
        carried = jnp.pad(names.astype(BF16), ((0, WIDTH - 3), (0, TILE - names.shape[1])))

    def before(values, *others):
        return lax.optimization_barrier((values, others))[0]

    def scatter(h):
        with jax.named_scope("panel_spread"):
            slices = tiles[h * SLICES : (h + 1) * SLICES]
            return [slices[0]] + [lax.ppermute(slices[j], "cols", [(0, j)]) for j in range(1, SLICES)]

    def spread(got, after, *extra):
        with jax.named_scope("panel_spread"):
            keep, give = pick(order, after, extra, got)
            return jnp.concatenate([keep, swap(give)])

    def gather_rows(held):
        with jax.named_scope("panel_rows"):
            if chips != 4:
                return [held] + [shift(held, j) for j in range(1, chips)]
            far, near = beside(held, 2), beside(held, 1)
            return [held, far, near, beside(far, 1)]

    def gather_cols(summed):
        with jax.named_scope("panel_cols"):
            sent = summed.astype(F16)
            if parts == SLICES:
                return [sent] + [across(sent, j) for j in range(1, parts)]
            return list(lax.all_gather(sent, "cols")[:SLICES])

    def both_cores(mine):
        with jax.named_scope("panel_cores"):
            return [v.astype(F32) for v in mine + [swap(v) for v in mine]]

    mixed = []

    def mix_next(after, count):
        for _ in range(count):
            with jax.named_scope("mix"):
                more, after = mix_tiles(matrix, mixers, kinds, after, len(mixed) * STEP, STEP)
            mixed.append(more)
        return after

    early = names.shape[1] // STEP // 2
    token = mix_next(tiles[0], early)
    held0 = spread(scatter(0), token, carried)
    arrived0 = gather_rows(held0)
    held1 = spread(scatter(1), arrived0[1])
    arrived1 = gather_rows(held1)
    token = mix_next(held1, names.shape[1] // STEP - early)
    with jax.named_scope("panel_sum"):
        summed0, all_names = first_sum(token, arrived0)
    mine0 = gather_cols(summed0)
    with jax.named_scope("panel_sum"):
        summed1 = next_sum(all_names, summed0, arrived1)
    mine1 = gather_cols(summed1)
    pieces0 = both_cores(mine0[:2] + list(before(mine0[2:], summed1)))
    with jax.named_scope("cross0"):
        panel0, *crossed0 = cross_parts(names, order, summed1, mixed, pieces0, [], chips, fast)
    with jax.named_scope("factor0"):
        inverse0 = first_factor(first_gram(crossed0[0], panel0))
    pieces1 = both_cores(before(mine1, inverse0, crossed0[0]))
    with jax.named_scope("cross1"):
        panel1, *crossed = cross_parts(names, order, inverse0, mixed, pieces1, crossed0, chips, fast)
    with jax.named_scope("gram1"):
        side, block = second_gram(crossed[0], panel0, panel1)

    if not fast:
        inverse = second_factor(side, side, block, inverse0)
        total = lax.psum(crossed[0], "rows")
        share = P_SIZE // rows_n
        return lax.dynamic_slice_in_dim(nn(inverse, total), row * share, share, 0)
    with jax.named_scope("cross_sum"):
        keep, give = crossed
        on_chip = keep + swap(give)
    with jax.named_scope("factor1"):
        inverse = second_factor(on_chip, side, block, inverse0)
    with jax.named_scope("cross_sum"):
        total = on_chip[0]
        for j in range(1, chips):
            total = total + shift(on_chip[j], j)
    with jax.named_scope("solve"):
        solved = nn(inverse, total)
        return lax.all_to_all(solved, "rows", split_axis=0, concat_axis=1, tiled=True)


def solution(mesh):
    in_specs = (P("rows", "cols"), P(), P("rows", None), P("rows"), P("rows"))
    out_specs = P("rows", "cols")
    return jax.shard_map(local, mesh=mesh, in_specs=in_specs, out_specs=out_specs, check_vma=False)
```

```python
import functools
import jax
import jax.numpy as jnp
from jax import lax
from jax.experimental import pallas as pl
from jax.experimental.pallas import tpu as pltpu
from jax.sharding import PartitionSpec as P

TILE = 128
P_SIZE = 256
NB = 64
CHUNKS = 2
WIDTH = 16
HALF = P_SIZE // CHUNKS
SLICES = HALF // (2 * WIDTH)
BASE = 64
STEP = 8
F32, BF16, F16 = jnp.float32, jnp.bfloat16, jnp.float16
HI = lax.Precision.HIGHEST
MIB = 1 << 20


def vmem():
    return pl.BlockSpec(memory_space=pltpu.VMEM)


def smem():
    return pl.BlockSpec(memory_space=pltpu.SMEM)


def anywhere():
    return pl.BlockSpec(memory_space=pl.ANY)


def params(mib):
    return pltpu.CompilerParams(vmem_limit_bytes=mib * MIB)


def cost(flops, bytes_accessed):
    return pl.CostEstimate(flops=flops, bytes_accessed=bytes_accessed, transcendentals=0)


LIGHT = cost(10**6, 10**5)


def signed_mixer(mixers_ref, names_ref, tile):
    position = lax.broadcasted_iota(jnp.int32, (1, TILE), 1)
    hashed = (names_ref[1, tile] ^ position * 40503) * 69069
    sign = (1 - 2 * (hashed >> 16 & 1)).astype(F32)
    return mixers_ref[names_ref[0, tile]] * sign


def split(value):
    high = value.astype(BF16)
    return high, (value - high.astype(F32)).astype(BF16)


def product(mixer, block):
    mixer_high, mixer_low = split(mixer)
    block_high, block_low = split(block)
    wide = jnp.dot(jnp.concatenate([mixer_high, mixer_low], axis=0), block_high, preferred_element_type=F32)
    low = jnp.dot(mixer_high, block_low, preferred_element_type=F32)
    return wide[:TILE] + (wide[TILE:] + low)


def panel_kernel(per_step, names_ref, order_ref, matrix_ref, mixers_ref, *refs):
    outs, turned = refs[:-1], refs[-1]
    first = pl.program_id(0) * per_step
    core = order_ref[2 * SLICES + 1]
    for u in range(per_step):
        mixer = signed_mixer(mixers_ref, names_ref, first + u)
        block = matrix_ref[u * TILE : (u + 1) * TILE, :]
        turned[u] = product(mixer, block).T
        for h in range(CHUNKS):
            for c in range(SLICES):
                for s in range(2):
                    who = core if s == 0 else 1 - core
                    start = pl.multiple_of(h * HALF + who * (HALF // 2) + c * WIDTH, WIDTH)
                    outs[h * SLICES + c][s, u] = turned[u, pl.ds(start, WIDTH), :].astype(BF16)


def mix_panel(matrix, mixers, names, order):
    tiles = names.shape[1]
    per_step = 16
    spec = pl.BlockSpec((2, per_step, WIDTH, TILE), lambda i, *_: (0, i, 0, 0))
    return pl.pallas_call(
        functools.partial(panel_kernel, per_step),
        grid_spec=pltpu.PrefetchScalarGridSpec(
            num_scalar_prefetch=2,
            grid=(tiles // per_step,),
            in_specs=[
                pl.BlockSpec((per_step * TILE, P_SIZE), lambda i, *_: (i, 0)),
                pl.BlockSpec(mixers.shape, lambda i, *_: (0, 0, 0)),
            ],
            out_specs=[spec] * (CHUNKS * SLICES),
            scratch_shapes=[pltpu.VMEM((per_step, P_SIZE, TILE), F32)],
        ),
        out_shape=[jax.ShapeDtypeStruct((2, tiles, WIDTH, TILE), BF16)] * (CHUNKS * SLICES),
        compiler_params=params(49),
        cost_estimate=LIGHT,
        name="mix_panel",
    )(names, order, matrix, mixers)


def mix_kernel(per_step, start, names_ref, matrix_ref, mixers_ref, after_ref, out_ref, token_ref):
    first = start + pl.program_id(0) * per_step
    for u in range(per_step):
        mixer = signed_mixer(mixers_ref, names_ref, first + u)
        block = matrix_ref[u * TILE : (u + 1) * TILE, :]
        out_ref[u * TILE : (u + 1) * TILE, :] = product(mixer, block).astype(BF16)
    token_ref[...] = jnp.zeros_like(token_ref)


def mix_tiles(matrix, mixers, names, after, start, count):
    cols = matrix.shape[1]
    per_step = 4
    return pl.pallas_call(
        functools.partial(mix_kernel, per_step, start),
        grid_spec=pltpu.PrefetchScalarGridSpec(
            num_scalar_prefetch=1,
            grid=(count // per_step,),
            in_specs=[
                pl.BlockSpec((per_step * TILE, cols), lambda i, *_: (i + start // per_step, 0)),
                pl.BlockSpec(mixers.shape, lambda i, *_: (0, 0, 0)),
                anywhere(),
            ],
            out_specs=[
                pl.BlockSpec((per_step * TILE, cols), lambda i, *_: (i, 0)),
                pl.BlockSpec((8, TILE), lambda i, *_: (0, 0)),
            ],
        ),
        out_shape=[jax.ShapeDtypeStruct((count * TILE, cols), BF16), jax.ShapeDtypeStruct((8, TILE), F32)],
        compiler_params=params(49),
        cost_estimate=LIGHT,
        name="mix_tiles",
    )(names, matrix, mixers, after)


def pick_kernel(count, order_ref, after_ref, *refs):
    extra, sources, (keep_ref, give_ref) = refs[:count], refs[count:-2], refs[-2:]
    part = order_ref[2 * SLICES + 2]
    tiles = sources[0].shape[1]
    for j, source in enumerate(sources):
        taken = part == j if j else (part == 0) | (part >= len(sources))

        @pl.when(taken)
        def copy(source=source):
            keep_ref[:tiles] = source[0]
            give_ref[:tiles] = source[1]

    for i, ref in enumerate(extra):
        keep_ref[tiles + i] = ref[...]
        give_ref[tiles + i] = ref[...]


def pick(order, after, extra, sources):
    tiles = sources[0].shape[1] + len(extra)
    return pl.pallas_call(
        functools.partial(pick_kernel, len(extra)),
        in_specs=[smem(), anywhere()] + [vmem()] * (len(extra) + len(sources)),
        out_specs=[vmem()] * 2,
        out_shape=[jax.ShapeDtypeStruct((tiles, WIDTH, TILE), BF16)] * 2,
        compiler_params=params(16),
        cost_estimate=LIGHT,
        name="pick",
    )(order, after, *extra, *sources)


def add_tiles(names, stride, tiles, pieces, out_ref, total):
    total[...] = jnp.zeros_like(total)
    for j, piece in enumerate(pieces):
        for s in range(2):

            def add(i, carry, j=j, s=s, piece=piece):
                value = piece[s * stride + i].astype(F32)
                one, two = names[2 * j + s, 0, i], names[2 * j + s, 1, i]
                total[one] = total[one] + value
                total[two] = total[two] + names[2 * j + s, 2, i].astype(F32) * value
                return carry

            lax.fori_loop(0, tiles, add, 0, unroll=8)
    summed = total[...]
    largest = jnp.max(jnp.max(jnp.abs(summed), axis=0), axis=1, keepdims=True)
    out_ref[...] = summed * jnp.where(largest > 1e-37, 1.0 / largest, 1.0)


def first_sum_kernel(after_ref, *refs):
    pieces, (out_ref, names_ref, total, names, sem) = refs[:-5], refs[-5:]
    tiles = pieces[0].shape[0] // 2 - 1
    for j, piece in enumerate(pieces):
        for s in range(2):
            names_ref[2 * j + s] = piece[s * (tiles + 1) + tiles].astype(F32)[:8].astype(jnp.int32)
    copy = pltpu.make_async_copy(names_ref, names, sem)
    copy.start()
    copy.wait()
    add_tiles(names, tiles + 1, tiles, pieces, out_ref, total)


def first_sum(after, pieces):
    names = (2 * len(pieces), 8, TILE)
    return pl.pallas_call(
        first_sum_kernel,
        in_specs=[anywhere()] + [vmem()] * len(pieces),
        out_specs=[vmem()] * 2,
        out_shape=[jax.ShapeDtypeStruct((NB, WIDTH, TILE), F32), jax.ShapeDtypeStruct(names, jnp.int32)],
        scratch_shapes=[pltpu.VMEM((NB, WIDTH, TILE), F32), pltpu.SMEM(names, jnp.int32), pltpu.SemaphoreType.DMA],
        compiler_params=params(24),
        cost_estimate=LIGHT,
        name="first_sum",
    )(after, *pieces)


def next_sum_kernel(names, after_ref, *refs):
    pieces, (out_ref, total) = refs[:-2], refs[-2:]
    tiles = pieces[0].shape[0] // 2
    add_tiles(names, tiles, tiles, pieces, out_ref, total)


def next_sum(names, after, pieces):
    return pl.pallas_call(
        next_sum_kernel,
        in_specs=[smem(), anywhere()] + [vmem()] * len(pieces),
        out_specs=vmem(),
        out_shape=jax.ShapeDtypeStruct((NB, WIDTH, TILE), F32),
        scratch_shapes=[pltpu.VMEM((NB, WIDTH, TILE), F32)],
        compiler_params=params(24),
        cost_estimate=LIGHT,
        name="next_sum",
    )(names, after, *pieces)


def nt(a, b, precision=None):
    return lax.dot_general(a, b, (((1,), (1,)), ((), ())), precision=precision, preferred_element_type=F32)


def nn(a, b):
    return jnp.dot(a, b, precision=HI, preferred_element_type=F32)


def join(order_ref, pieces, panel):
    for q, piece in enumerate(pieces):
        panel[:, pl.ds(pl.multiple_of(order_ref[q] * WIDTH, WIDTH), WIDTH), :] = piece[...]


def cross_kernel(steps, chips, earlier, fast, names_ref, order_ref, after_ref, *refs):
    mixed, refs = refs[: len(steps)], refs[len(steps) :]
    pieces, refs = refs[: 2 * SLICES], refs[2 * SLICES :]
    before, refs = refs[:earlier], refs[earlier:]
    panel, outs, total = refs[0], refs[1:-1], refs[-1]
    step = pl.program_id(0)

    @pl.when(step == 0)
    def start():
        total[...] = jnp.zeros_like(total)
        join(order_ref, pieces, panel)

    high, low = [], []
    for u in range(STEP):
        t = STEP * step + u
        one, two = split(panel[names_ref[0, t]] + names_ref[2, t].astype(F32) * panel[names_ref[1, t]])
        high.append(one)
        low.append(two)
    weights = jnp.concatenate([jnp.concatenate(high, axis=1), jnp.concatenate(low, axis=1)], axis=0)

    begin = 0
    for count, mixed_ref in zip(steps, mixed):

        @pl.when((step >= begin) & (step < begin + count))
        def add(mixed_ref=mixed_ref):
            total[...] += jnp.dot(weights, mixed_ref[...], preferred_element_type=F32)

        begin += count

    @pl.when(step == pl.num_programs(0) - 1)
    def finish():
        total[:HALF, :] = total[:HALF, :] + total[HALF:, :]
        rows = earlier and HALF
        for ref, out in zip(before, outs):
            out[..., :HALF, :] = ref[...]
        if not fast:
            outs[0][rows:, :] = total[:HALF, :]
        else:
            chip, core = order_ref[2 * SLICES], order_ref[2 * SLICES + 1]
            for s in range(2):
                who = core if s == 0 else 1 - core
                for j in range(chips):
                    at = (2 * lax.rem(chip + j, chips) + who) * TILE
                    outs[s][j, rows:, :] = total[:HALF, pl.ds(pl.multiple_of(at, TILE), TILE)]


def cross_parts(names, order, after, mixed, pieces, before, chips, fast):
    cols = mixed[0].shape[1]
    steps = [v.shape[0] // (STEP * TILE) for v in mixed]
    rows = 2 * HALF if before else HALF
    if fast:
        outs = [jax.ShapeDtypeStruct((chips, rows, TILE), F32)] * 2
    else:
        outs = [jax.ShapeDtypeStruct((rows, cols), F32)]
    outs = [jax.ShapeDtypeStruct((NB, HALF, TILE), F32)] + outs
    begins = [sum(steps[:i]) for i in range(len(steps))]
    blocks = [
        pl.BlockSpec((STEP * TILE, cols), lambda i, b=begin, n=count: (jnp.clip(i - b, 0, n - 1), 0))
        for begin, count in zip(begins, steps)
    ]
    return pl.pallas_call(
        functools.partial(cross_kernel, steps, chips, len(before), fast),
        grid=(sum(steps),),
        in_specs=[smem(), smem(), anywhere()] + blocks + [vmem()] * (len(pieces) + len(before)),
        out_specs=[vmem()] * len(outs),
        out_shape=outs,
        scratch_shapes=[pltpu.VMEM((2 * HALF, cols), F32)],
        compiler_params=params(32),
        cost_estimate=LIGHT,
        name="cross_parts",
    )(names, order, after, *mixed, *pieces, *before)


def factor_inverse(block):
    row = lax.broadcasted_iota(jnp.int32, (BASE, BASE), 0)
    lane = lax.broadcasted_iota(jnp.int32, (BASE, BASE), 1)
    wide = jnp.concatenate([block, (row == lane).astype(F32)], axis=1)
    slabs = [wide[8 * g : 8 * g + 8, :] for g in range(BASE // 8)]
    place = lax.broadcasted_iota(jnp.int32, (8, 2 * BASE), 0)

    def full(value):
        return jnp.broadcast_to(value, (8, 2 * BASE))

    done = []
    for own in range(BASE // 8):
        slab, first = slabs[own], 8 * own
        cols = [full(slab[:, first + k : first + k + 1]) for k in range(8)]
        rows = [full(slab[k : k + 1, :]) for k in range(8)]
        entry = {(a, b): full(cols[b][a : a + 1, :]) for a in range(8) for b in range(a, 8)}
        factor, scale = {}, []
        for k in range(8):
            scale.append(1.0 / entry[k, k])
            for a in range(k + 1, 8):
                factor[a, k] = entry[k, a] * scale[k]
            for a in range(k + 1, 8):
                for b in range(a, 8):
                    entry[a, b] = entry[a, b] - factor[a, k] * entry[k, b]
                rows[a] = rows[a] - factor[a, k] * rows[k]
        solved = [None] * 8
        for k in reversed(range(8)):
            value = rows[k] * scale[k]
            for m in range(k + 1, 8):
                value = value - factor[m, k] * solved[m]
            solved[k] = value
        for g in range(own + 1, BASE // 8):
            before = slabs[g]
            for k in range(8):
                slabs[g] = slabs[g] - before[:, first + k : first + k + 1] * solved[k]
        out = jnp.zeros((8, 2 * BASE), F32)
        for k in range(8):
            out = jnp.where(place == k, rows[k] * lax.rsqrt(entry[k, k]), out)
        done.append(out)
    return jnp.concatenate(done, axis=0)[:, BASE:]


def factor_inverse_pair(block):
    first = factor_inverse(block[:BASE, :BASE])
    side = nt(block[BASE:, :BASE], first, HI)
    second = factor_inverse(block[BASE:, BASE:] - nt(side, side, HI))
    corner = -nn(second, nn(side, first))
    top = jnp.concatenate([first, jnp.zeros_like(first)], axis=1)
    return jnp.concatenate([top, jnp.concatenate([corner, second], axis=1)], axis=0)


GROUP = 8


def wide_buckets(panel, i):
    return jnp.concatenate([panel[GROUP * i + u] for u in range(GROUP)], axis=1)


def first_kernel(after_ref, panel, out_ref, acc):
    acc[...] = jnp.zeros_like(acc)

    def step(i, carry):
        one, two = split(wide_buckets(panel, i))
        acc[...] += nt(jnp.concatenate([one, two], axis=0), one)
        return carry

    lax.fori_loop(0, NB // GROUP, step, 0)
    mixed = acc[HALF:, :]
    out_ref[...] = acc[:HALF, :] + (mixed + mixed.T)


def first_gram(after, panel):
    return pl.pallas_call(
        first_kernel,
        in_specs=[anywhere(), vmem()],
        out_specs=vmem(),
        out_shape=jax.ShapeDtypeStruct((HALF, HALF), F32),
        scratch_shapes=[pltpu.VMEM((2 * HALF, HALF), F32)],
        compiler_params=params(32),
        cost_estimate=LIGHT,
        name="first_gram",
    )(after, panel)


def factor_kernel(block_ref, out_ref):
    out_ref[...] = factor_inverse_pair(block_ref[...])


def first_factor(block):
    return pl.pallas_call(
        factor_kernel,
        in_specs=[vmem()],
        out_specs=vmem(),
        out_shape=jax.ShapeDtypeStruct((HALF, HALF), F32),
        compiler_params=params(16),
        cost_estimate=LIGHT,
        name="first_factor",
    )(block)


def second_kernel(after_ref, panel0, panel1, side_ref, block_ref, acc, extra):
    acc[...] = jnp.zeros_like(acc)
    extra[...] = jnp.zeros_like(extra)

    def step(i, carry):
        one0, two0 = split(wide_buckets(panel0, i))
        one1, two1 = split(wide_buckets(panel1, i))
        acc[...] += nt(jnp.concatenate([one1, two1], axis=0), jnp.concatenate([one0, one1], axis=0))
        extra[...] += nt(one1, two0)
        return carry

    lax.fori_loop(0, NB // GROUP, step, 0)
    side_ref[...] = acc[:HALF, :HALF] + (acc[HALF:, :HALF] + extra[...])
    mixed = acc[HALF:, HALF:]
    block_ref[...] = acc[:HALF, HALF:] + (mixed + mixed.T)


def second_gram(after, panel0, panel1):
    return pl.pallas_call(
        second_kernel,
        in_specs=[anywhere()] + [vmem()] * 2,
        out_specs=[vmem()] * 2,
        out_shape=[jax.ShapeDtypeStruct((HALF, HALF), F32)] * 2,
        scratch_shapes=[pltpu.VMEM((2 * HALF, 2 * HALF), F32), pltpu.VMEM((HALF, HALF), F32)],
        compiler_params=params(32),
        cost_estimate=LIGHT,
        name="second_gram",
    )(after, panel0, panel1)


def last_kernel(after_ref, side_ref, block_ref, inverse_ref, out_ref):
    first = inverse_ref[...]
    side = nt(side_ref[...], first, HI)
    second = factor_inverse_pair(block_ref[...] - nt(side, side, HI))
    out_ref[:HALF, :HALF] = first
    out_ref[:HALF, HALF:] = jnp.zeros_like(first)
    out_ref[HALF:, :HALF] = -nn(second, nn(side, first))
    out_ref[HALF:, HALF:] = second


def second_factor(after, side, block, inverse):
    return pl.pallas_call(
        last_kernel,
        in_specs=[anywhere()] + [vmem()] * 3,
        out_specs=vmem(),
        out_shape=jax.ShapeDtypeStruct((P_SIZE, P_SIZE), F32),
        compiler_params=params(32),
        cost_estimate=LIGHT,
        name="second_factor",
    )(after, side, block, inverse)


def local(matrix, mixers, bucket_pair, mixer_index, sign_seed):
    cols = matrix.shape[1]
    rows_n, parts = lax.axis_size("rows"), lax.axis_size("cols")
    chips = rows_n // 2
    row, part = lax.axis_index("rows"), lax.axis_index("cols")
    core, chip = row % 2, row // 2

    def swap(value):
        return lax.ppermute(value, "rows", [(i, i ^ 1) for i in range(rows_n)])

    def shift(value, j):
        return lax.ppermute(value, "rows", [(i, (i + 2 * j) % rows_n) for i in range(rows_n)])

    def beside(value, j):
        return lax.ppermute(value, "rows", [(i, i ^ 2 * j) for i in range(rows_n)])

    def across(value, j):
        return lax.ppermute(value, "cols", [(i, i ^ j) for i in range(parts)])

    fast = cols % (TILE * rows_n) == 0
    with jax.named_scope("names"):
        flips = 1 - 2 * (sign_seed >> 29 & 1)
        names = jnp.concatenate([bucket_pair.T, flips[None]])
        kinds = jnp.stack([mixer_index, sign_seed])
        place = [part ^ j if parts == SLICES else j for j in range(SLICES)]
        order = [who * SLICES + c for who in (core, 1 - core) for c in place]
        order = jnp.stack([jnp.asarray(v, jnp.int32) for v in order + [chip, core, part]])
    with jax.named_scope("panel_mix"):
        tiles = mix_panel(matrix, mixers, kinds, order)
    with jax.named_scope("names"):
        carried = jnp.pad(names.astype(BF16), ((0, WIDTH - 3), (0, TILE - names.shape[1])))

    def before(values, *others):
        return lax.optimization_barrier((values, others))[0]

    def scatter(h):
        with jax.named_scope("panel_spread"):
            slices = tiles[h * SLICES : (h + 1) * SLICES]
            return [slices[0]] + [lax.ppermute(slices[j], "cols", [(0, j)]) for j in range(1, SLICES)]

    def spread(got, after, *extra):
        with jax.named_scope("panel_spread"):
            keep, give = pick(order, after, extra, got)
            return jnp.concatenate([keep, swap(give)])

    def gather_rows(held):
        with jax.named_scope("panel_rows"):
            if chips != 4:
                return [held] + [shift(held, j) for j in range(1, chips)]
            far, near = beside(held, 2), beside(held, 1)
            return [held, far, near, beside(far, 1)]

    def gather_cols(summed):
        with jax.named_scope("panel_cols"):
            sent = summed.astype(F16)
            if parts == SLICES:
                return [sent] + [across(sent, j) for j in range(1, parts)]
            return list(lax.all_gather(sent, "cols")[:SLICES])

    def both_cores(mine):
        with jax.named_scope("panel_cores"):
            return [v.astype(F32) for v in mine + [swap(v) for v in mine]]

    mixed = []

    def mix_next(after, count):
        for _ in range(count):
            with jax.named_scope("mix"):
                more, after = mix_tiles(matrix, mixers, kinds, after, len(mixed) * STEP, STEP)
            mixed.append(more)
        return after

    early = names.shape[1] // STEP // 2
    token = mix_next(tiles[0], early)
    held0 = spread(scatter(0), token, carried)
    arrived0 = gather_rows(held0)
    held1 = spread(scatter(1), arrived0[1])
    arrived1 = gather_rows(held1)
    token = mix_next(held1, names.shape[1] // STEP - early)
    with jax.named_scope("panel_sum"):
        summed0, all_names = first_sum(token, arrived0)
    mine0 = gather_cols(summed0)
    with jax.named_scope("panel_sum"):
        summed1 = next_sum(all_names, summed0, arrived1)
    mine1 = gather_cols(summed1)
    pieces0 = both_cores(mine0[:-1] + list(before(mine0[-1:], summed1)))
    with jax.named_scope("cross0"):
        panel0, *crossed0 = cross_parts(names, order, summed1, mixed, pieces0, [], chips, fast)
    with jax.named_scope("factor0"):
        inverse0 = first_factor(first_gram(crossed0[0], panel0))
    pieces1 = both_cores(before(mine1, inverse0, crossed0[0]))
    with jax.named_scope("cross1"):
        panel1, *crossed = cross_parts(names, order, inverse0, mixed, pieces1, crossed0, chips, fast)
    with jax.named_scope("gram1"):
        side, block = second_gram(crossed[0], panel0, panel1)

    if not fast:
        inverse = second_factor(side, side, block, inverse0)
        total = lax.psum(crossed[0], "rows")
        share = P_SIZE // rows_n
        return lax.dynamic_slice_in_dim(nn(inverse, total), row * share, share, 0)
    with jax.named_scope("cross_sum"):
        keep, give = crossed
        on_chip = keep + swap(give)
    with jax.named_scope("factor1"):
        inverse = second_factor(on_chip, side, block, inverse0)
    with jax.named_scope("cross_sum"):
        total = on_chip[0]
        for j in range(1, chips):
            total = total + shift(on_chip[j], j)
    with jax.named_scope("solve"):
        solved = nn(inverse, total)
        return lax.all_to_all(solved, "rows", split_axis=0, concat_axis=1, tiled=True)


def solution(mesh):
    in_specs = (P("rows", "cols"), P(), P("rows", None), P("rows"), P("rows"))
    out_specs = P("rows", "cols")
    return jax.shard_map(local, mesh=mesh, in_specs=in_specs, out_specs=out_specs, check_vma=False)
```

```python
import functools
import jax
import jax.numpy as jnp
from jax import lax
from jax.experimental import pallas as pl
from jax.experimental.pallas import tpu as pltpu
from jax.sharding import PartitionSpec as P

TILE = 128
P_SIZE = 256
NB = 64
CHUNKS = 2
WIDTH = 16
HALF = P_SIZE // CHUNKS
SLICES = HALF // (2 * WIDTH)
BASE = 64
STEP = 8
F32, BF16, F16 = jnp.float32, jnp.bfloat16, jnp.float16
HI = lax.Precision.HIGHEST
MIB = 1 << 20


def vmem():
    return pl.BlockSpec(memory_space=pltpu.VMEM)


def smem():
    return pl.BlockSpec(memory_space=pltpu.SMEM)


def anywhere():
    return pl.BlockSpec(memory_space=pl.ANY)


def params(mib):
    return pltpu.CompilerParams(vmem_limit_bytes=mib * MIB)


def cost(flops, bytes_accessed):
    return pl.CostEstimate(flops=flops, bytes_accessed=bytes_accessed, transcendentals=0)


LIGHT = cost(10**6, 10**5)


def signed_mixer(mixers_ref, names_ref, tile):
    position = lax.broadcasted_iota(jnp.int32, (1, TILE), 1)
    hashed = (names_ref[1, tile] ^ position * 40503) * 69069
    sign = (1 - 2 * (hashed >> 16 & 1)).astype(F32)
    return mixers_ref[names_ref[0, tile]] * sign


def split(value):
    high = value.astype(BF16)
    return high, (value - high.astype(F32)).astype(BF16)


def product(mixer, block):
    mixer_high, mixer_low = split(mixer)
    block_high, block_low = split(block)
    wide = jnp.dot(jnp.concatenate([mixer_high, mixer_low], axis=0), block_high, preferred_element_type=F32)
    low = jnp.dot(mixer_high, block_low, preferred_element_type=F32)
    return wide[:TILE] + (wide[TILE:] + low)


def panel_kernel(per_step, names_ref, order_ref, matrix_ref, mixers_ref, after_ref, *refs):
    outs, turned = refs[:-1], refs[-1]
    first = pl.program_id(0) * per_step
    core = order_ref[2 * SLICES + 1]
    for u in range(per_step):
        mixer = signed_mixer(mixers_ref, names_ref, first + u)
        block = matrix_ref[u * TILE : (u + 1) * TILE, :]
        turned[u] = product(mixer, block).T
        for c in range(SLICES):
            for s in range(2):
                who = core if s == 0 else 1 - core
                start = pl.multiple_of(who * (HALF // 2) + c * WIDTH, WIDTH)
                outs[c][s, u] = turned[u, pl.ds(start, WIDTH), :].astype(BF16)


def mix_panel(matrix, mixers, names, order, after, chunk):
    tiles = names.shape[1]
    per_step = 16
    spec = pl.BlockSpec((2, per_step, WIDTH, TILE), lambda i, *_: (0, i, 0, 0))
    return pl.pallas_call(
        functools.partial(panel_kernel, per_step),
        grid_spec=pltpu.PrefetchScalarGridSpec(
            num_scalar_prefetch=2,
            grid=(tiles // per_step,),
            in_specs=[
                pl.BlockSpec((per_step * TILE, HALF), lambda i, *_: (i, chunk)),
                pl.BlockSpec(mixers.shape, lambda i, *_: (0, 0, 0)),
                anywhere(),
            ],
            out_specs=[spec] * SLICES,
            scratch_shapes=[pltpu.VMEM((per_step, HALF, TILE), F32)],
        ),
        out_shape=[jax.ShapeDtypeStruct((2, tiles, WIDTH, TILE), BF16)] * SLICES,
        compiler_params=params(49),
        cost_estimate=LIGHT,
        name="mix_panel",
    )(names, order, matrix, mixers, after)


def mix_kernel(per_step, start, names_ref, matrix_ref, mixers_ref, after_ref, out_ref, token_ref):
    first = start + pl.program_id(0) * per_step
    for u in range(per_step):
        mixer = signed_mixer(mixers_ref, names_ref, first + u)
        block = matrix_ref[u * TILE : (u + 1) * TILE, :]
        out_ref[u * TILE : (u + 1) * TILE, :] = product(mixer, block).astype(BF16)
    token_ref[...] = jnp.zeros_like(token_ref)


def mix_tiles(matrix, mixers, names, after, start, count):
    cols = matrix.shape[1]
    per_step = 4
    return pl.pallas_call(
        functools.partial(mix_kernel, per_step, start),
        grid_spec=pltpu.PrefetchScalarGridSpec(
            num_scalar_prefetch=1,
            grid=(count // per_step,),
            in_specs=[
                pl.BlockSpec((per_step * TILE, cols), lambda i, *_: (i + start // per_step, 0)),
                pl.BlockSpec(mixers.shape, lambda i, *_: (0, 0, 0)),
                anywhere(),
            ],
            out_specs=[
                pl.BlockSpec((per_step * TILE, cols), lambda i, *_: (i, 0)),
                pl.BlockSpec((8, TILE), lambda i, *_: (0, 0)),
            ],
        ),
        out_shape=[jax.ShapeDtypeStruct((count * TILE, cols), BF16), jax.ShapeDtypeStruct((8, TILE), F32)],
        compiler_params=params(49),
        cost_estimate=LIGHT,
        name="mix_tiles",
    )(names, matrix, mixers, after)


def pick_kernel(count, order_ref, after_ref, *refs):
    extra, sources, (keep_ref, give_ref) = refs[:count], refs[count:-2], refs[-2:]
    part = order_ref[2 * SLICES + 2]
    tiles = sources[0].shape[1]
    for j, source in enumerate(sources):
        taken = part == j if j else (part == 0) | (part >= len(sources))

        @pl.when(taken)
        def copy(source=source):
            keep_ref[:tiles] = source[0]
            give_ref[:tiles] = source[1]

    for i, ref in enumerate(extra):
        keep_ref[tiles + i] = ref[...]
        give_ref[tiles + i] = ref[...]


def pick(order, after, extra, sources):
    tiles = sources[0].shape[1] + len(extra)
    return pl.pallas_call(
        functools.partial(pick_kernel, len(extra)),
        in_specs=[smem(), anywhere()] + [vmem()] * (len(extra) + len(sources)),
        out_specs=[vmem()] * 2,
        out_shape=[jax.ShapeDtypeStruct((tiles, WIDTH, TILE), BF16)] * 2,
        compiler_params=params(16),
        cost_estimate=LIGHT,
        name="pick",
    )(order, after, *extra, *sources)


def add_tiles(names, stride, tiles, pieces, out_ref, total):
    total[...] = jnp.zeros_like(total)
    for j, piece in enumerate(pieces):
        for s in range(2):

            def add(i, carry, j=j, s=s, piece=piece):
                value = piece[s * stride + i].astype(F32)
                one, two = names[2 * j + s, 0, i], names[2 * j + s, 1, i]
                total[one] = total[one] + value
                total[two] = total[two] + names[2 * j + s, 2, i].astype(F32) * value
                return carry

            lax.fori_loop(0, tiles, add, 0, unroll=8)
    summed = total[...]
    largest = jnp.max(jnp.max(jnp.abs(summed), axis=0), axis=1, keepdims=True)
    out_ref[...] = summed * jnp.where(largest > 1e-37, 1.0 / largest, 1.0)


def first_sum_kernel(after_ref, *refs):
    pieces, (out_ref, names_ref, total, names, sem) = refs[:-5], refs[-5:]
    tiles = pieces[0].shape[0] // 2 - 1
    for j, piece in enumerate(pieces):
        for s in range(2):
            names_ref[2 * j + s] = piece[s * (tiles + 1) + tiles].astype(F32)[:8].astype(jnp.int32)
    copy = pltpu.make_async_copy(names_ref, names, sem)
    copy.start()
    copy.wait()
    add_tiles(names, tiles + 1, tiles, pieces, out_ref, total)


def first_sum(after, pieces):
    names = (2 * len(pieces), 8, TILE)
    return pl.pallas_call(
        first_sum_kernel,
        in_specs=[anywhere()] + [vmem()] * len(pieces),
        out_specs=[vmem()] * 2,
        out_shape=[jax.ShapeDtypeStruct((NB, WIDTH, TILE), F32), jax.ShapeDtypeStruct(names, jnp.int32)],
        scratch_shapes=[pltpu.VMEM((NB, WIDTH, TILE), F32), pltpu.SMEM(names, jnp.int32), pltpu.SemaphoreType.DMA],
        compiler_params=params(24),
        cost_estimate=LIGHT,
        name="first_sum",
    )(after, *pieces)


def next_sum_kernel(names, after_ref, *refs):
    pieces, (out_ref, total) = refs[:-2], refs[-2:]
    tiles = pieces[0].shape[0] // 2
    add_tiles(names, tiles, tiles, pieces, out_ref, total)


def next_sum(names, after, pieces):
    return pl.pallas_call(
        next_sum_kernel,
        in_specs=[smem(), anywhere()] + [vmem()] * len(pieces),
        out_specs=vmem(),
        out_shape=jax.ShapeDtypeStruct((NB, WIDTH, TILE), F32),
        scratch_shapes=[pltpu.VMEM((NB, WIDTH, TILE), F32)],
        compiler_params=params(24),
        cost_estimate=LIGHT,
        name="next_sum",
    )(names, after, *pieces)


def nt(a, b, precision=None):
    return lax.dot_general(a, b, (((1,), (1,)), ((), ())), precision=precision, preferred_element_type=F32)


def nn(a, b):
    return jnp.dot(a, b, precision=HI, preferred_element_type=F32)


def join(order_ref, pieces, panel):
    for q, piece in enumerate(pieces):
        panel[:, pl.ds(pl.multiple_of(order_ref[q] * WIDTH, WIDTH), WIDTH), :] = piece[...]


def cross_kernel(steps, chips, earlier, fast, names_ref, order_ref, after_ref, *refs):
    mixed, refs = refs[: len(steps)], refs[len(steps) :]
    pieces, refs = refs[: 2 * SLICES], refs[2 * SLICES :]
    before, refs = refs[:earlier], refs[earlier:]
    panel, outs, total = refs[0], refs[1:-1], refs[-1]
    step = pl.program_id(0)

    @pl.when(step == 0)
    def start():
        total[...] = jnp.zeros_like(total)
        join(order_ref, pieces, panel)

    high, low = [], []
    for u in range(STEP):
        t = STEP * step + u
        one, two = split(panel[names_ref[0, t]] + names_ref[2, t].astype(F32) * panel[names_ref[1, t]])
        high.append(one)
        low.append(two)
    weights = jnp.concatenate([jnp.concatenate(high, axis=1), jnp.concatenate(low, axis=1)], axis=0)

    begin = 0
    for count, mixed_ref in zip(steps, mixed):

        @pl.when((step >= begin) & (step < begin + count))
        def add(mixed_ref=mixed_ref):
            total[...] += jnp.dot(weights, mixed_ref[...], preferred_element_type=F32)

        begin += count

    @pl.when(step == pl.num_programs(0) - 1)
    def finish():
        total[:HALF, :] = total[:HALF, :] + total[HALF:, :]
        rows = earlier and HALF
        for ref, out in zip(before, outs):
            out[..., :HALF, :] = ref[...]
        if not fast:
            outs[0][rows:, :] = total[:HALF, :]
        else:
            chip, core = order_ref[2 * SLICES], order_ref[2 * SLICES + 1]
            for s in range(2):
                who = core if s == 0 else 1 - core
                for j in range(chips):
                    at = (2 * lax.rem(chip + j, chips) + who) * TILE
                    outs[s][j, rows:, :] = total[:HALF, pl.ds(pl.multiple_of(at, TILE), TILE)]


def cross_parts(names, order, after, mixed, pieces, before, chips, fast):
    cols = mixed[0].shape[1]
    steps = [v.shape[0] // (STEP * TILE) for v in mixed]
    rows = 2 * HALF if before else HALF
    if fast:
        outs = [jax.ShapeDtypeStruct((chips, rows, TILE), F32)] * 2
    else:
        outs = [jax.ShapeDtypeStruct((rows, cols), F32)]
    outs = [jax.ShapeDtypeStruct((NB, HALF, TILE), F32)] + outs
    begins = [sum(steps[:i]) for i in range(len(steps))]
    blocks = [
        pl.BlockSpec((STEP * TILE, cols), lambda i, b=begin, n=count: (jnp.clip(i - b, 0, n - 1), 0))
        for begin, count in zip(begins, steps)
    ]
    return pl.pallas_call(
        functools.partial(cross_kernel, steps, chips, len(before), fast),
        grid=(sum(steps),),
        in_specs=[smem(), smem(), anywhere()] + blocks + [vmem()] * (len(pieces) + len(before)),
        out_specs=[vmem()] * len(outs),
        out_shape=outs,
        scratch_shapes=[pltpu.VMEM((2 * HALF, cols), F32)],
        compiler_params=params(32),
        cost_estimate=LIGHT,
        name="cross_parts",
    )(names, order, after, *mixed, *pieces, *before)


def factor_inverse(block):
    row = lax.broadcasted_iota(jnp.int32, (BASE, BASE), 0)
    lane = lax.broadcasted_iota(jnp.int32, (BASE, BASE), 1)
    wide = jnp.concatenate([block, (row == lane).astype(F32)], axis=1)
    slabs = [wide[8 * g : 8 * g + 8, :] for g in range(BASE // 8)]
    place = lax.broadcasted_iota(jnp.int32, (8, 2 * BASE), 0)

    def full(value):
        return jnp.broadcast_to(value, (8, 2 * BASE))

    done = []
    for own in range(BASE // 8):
        slab, first = slabs[own], 8 * own
        cols = [full(slab[:, first + k : first + k + 1]) for k in range(8)]
        rows = [full(slab[k : k + 1, :]) for k in range(8)]
        entry = {(a, b): full(cols[b][a : a + 1, :]) for a in range(8) for b in range(a, 8)}
        factor, scale = {}, []
        for k in range(8):
            scale.append(1.0 / entry[k, k])
            for a in range(k + 1, 8):
                factor[a, k] = entry[k, a] * scale[k]
            for a in range(k + 1, 8):
                for b in range(a, 8):
                    entry[a, b] = entry[a, b] - factor[a, k] * entry[k, b]
                rows[a] = rows[a] - factor[a, k] * rows[k]
        solved = [None] * 8
        for k in reversed(range(8)):
            value = rows[k] * scale[k]
            for m in range(k + 1, 8):
                value = value - factor[m, k] * solved[m]
            solved[k] = value
        for g in range(own + 1, BASE // 8):
            before = slabs[g]
            for k in range(8):
                slabs[g] = slabs[g] - before[:, first + k : first + k + 1] * solved[k]
        out = jnp.zeros((8, 2 * BASE), F32)
        for k in range(8):
            out = jnp.where(place == k, rows[k] * lax.rsqrt(entry[k, k]), out)
        done.append(out)
    return jnp.concatenate(done, axis=0)[:, BASE:]


def factor_inverse_pair(block):
    first = factor_inverse(block[:BASE, :BASE])
    side = nt(block[BASE:, :BASE], first, HI)
    second = factor_inverse(block[BASE:, BASE:] - nt(side, side, HI))
    corner = -nn(second, nn(side, first))
    top = jnp.concatenate([first, jnp.zeros_like(first)], axis=1)
    return jnp.concatenate([top, jnp.concatenate([corner, second], axis=1)], axis=0)


GROUP = 8


def wide_buckets(panel, i):
    return jnp.concatenate([panel[GROUP * i + u] for u in range(GROUP)], axis=1)


def first_kernel(after_ref, panel, out_ref, acc):
    acc[...] = jnp.zeros_like(acc)

    def step(i, carry):
        one, two = split(wide_buckets(panel, i))
        acc[...] += nt(jnp.concatenate([one, two], axis=0), one)
        return carry

    lax.fori_loop(0, NB // GROUP, step, 0)
    mixed = acc[HALF:, :]
    out_ref[...] = acc[:HALF, :] + (mixed + mixed.T)


def first_gram(after, panel):
    return pl.pallas_call(
        first_kernel,
        in_specs=[anywhere(), vmem()],
        out_specs=vmem(),
        out_shape=jax.ShapeDtypeStruct((HALF, HALF), F32),
        scratch_shapes=[pltpu.VMEM((2 * HALF, HALF), F32)],
        compiler_params=params(32),
        cost_estimate=LIGHT,
        name="first_gram",
    )(after, panel)


def factor_kernel(block_ref, out_ref):
    out_ref[...] = factor_inverse_pair(block_ref[...])


def first_factor(block):
    return pl.pallas_call(
        factor_kernel,
        in_specs=[vmem()],
        out_specs=vmem(),
        out_shape=jax.ShapeDtypeStruct((HALF, HALF), F32),
        compiler_params=params(16),
        cost_estimate=LIGHT,
        name="first_factor",
    )(block)


def second_kernel(after_ref, panel0, panel1, side_ref, block_ref, acc, extra):
    acc[...] = jnp.zeros_like(acc)
    extra[...] = jnp.zeros_like(extra)

    def step(i, carry):
        one0, two0 = split(wide_buckets(panel0, i))
        one1, two1 = split(wide_buckets(panel1, i))
        acc[...] += nt(jnp.concatenate([one1, two1], axis=0), jnp.concatenate([one0, one1], axis=0))
        extra[...] += nt(one1, two0)
        return carry

    lax.fori_loop(0, NB // GROUP, step, 0)
    side_ref[...] = acc[:HALF, :HALF] + (acc[HALF:, :HALF] + extra[...])
    mixed = acc[HALF:, HALF:]
    block_ref[...] = acc[:HALF, HALF:] + (mixed + mixed.T)


def second_gram(after, panel0, panel1):
    return pl.pallas_call(
        second_kernel,
        in_specs=[anywhere()] + [vmem()] * 2,
        out_specs=[vmem()] * 2,
        out_shape=[jax.ShapeDtypeStruct((HALF, HALF), F32)] * 2,
        scratch_shapes=[pltpu.VMEM((2 * HALF, 2 * HALF), F32), pltpu.VMEM((HALF, HALF), F32)],
        compiler_params=params(32),
        cost_estimate=LIGHT,
        name="second_gram",
    )(after, panel0, panel1)


def last_kernel(after_ref, side_ref, block_ref, inverse_ref, out_ref):
    first = inverse_ref[...]
    side = nt(side_ref[...], first, HI)
    second = factor_inverse_pair(block_ref[...] - nt(side, side, HI))
    out_ref[:HALF, :HALF] = first
    out_ref[:HALF, HALF:] = jnp.zeros_like(first)
    out_ref[HALF:, :HALF] = -nn(second, nn(side, first))
    out_ref[HALF:, HALF:] = second


def second_factor(after, side, block, inverse):
    return pl.pallas_call(
        last_kernel,
        in_specs=[anywhere()] + [vmem()] * 3,
        out_specs=vmem(),
        out_shape=jax.ShapeDtypeStruct((P_SIZE, P_SIZE), F32),
        compiler_params=params(32),
        cost_estimate=LIGHT,
        name="second_factor",
    )(after, side, block, inverse)


def local(matrix, mixers, bucket_pair, mixer_index, sign_seed):
    cols = matrix.shape[1]
    rows_n, parts = lax.axis_size("rows"), lax.axis_size("cols")
    chips = rows_n // 2
    row, part = lax.axis_index("rows"), lax.axis_index("cols")
    core, chip = row % 2, row // 2

    def swap(value):
        return lax.ppermute(value, "rows", [(i, i ^ 1) for i in range(rows_n)])

    def shift(value, j):
        return lax.ppermute(value, "rows", [(i, (i + 2 * j) % rows_n) for i in range(rows_n)])

    def beside(value, j):
        return lax.ppermute(value, "rows", [(i, i ^ 2 * j) for i in range(rows_n)])

    def across(value, j):
        return lax.ppermute(value, "cols", [(i, i ^ j) for i in range(parts)])

    fast = cols % (TILE * rows_n) == 0
    with jax.named_scope("names"):
        flips = 1 - 2 * (sign_seed >> 29 & 1)
        names = jnp.concatenate([bucket_pair.T, flips[None]])
        kinds = jnp.stack([mixer_index, sign_seed])
        place = [part ^ j if parts == SLICES else j for j in range(SLICES)]
        order = [who * SLICES + c for who in (core, 1 - core) for c in place]
        order = jnp.stack([jnp.asarray(v, jnp.int32) for v in order + [chip, core, part]])
    with jax.named_scope("panel_mix"):
        tiles = mix_panel(matrix, mixers, kinds, order, order, 0)
        tiles = tiles + mix_panel(matrix, mixers, kinds, order, tiles[0], 1)
    with jax.named_scope("names"):
        carried = jnp.pad(names.astype(BF16), ((0, WIDTH - 3), (0, TILE - names.shape[1])))

    def before(values, *others):
        return lax.optimization_barrier((values, others))[0]

    def scatter(h):
        with jax.named_scope("panel_spread"):
            slices = tiles[h * SLICES : (h + 1) * SLICES]
            return [slices[0]] + [lax.ppermute(slices[j], "cols", [(0, j)]) for j in range(1, SLICES)]

    def spread(got, after, *extra):
        with jax.named_scope("panel_spread"):
            keep, give = pick(order, after, extra, got)
            return jnp.concatenate([keep, swap(give)])

    def gather_rows(held):
        with jax.named_scope("panel_rows"):
            if chips != 4:
                return [held] + [shift(held, j) for j in range(1, chips)]
            far, near = beside(held, 2), beside(held, 1)
            return [held, far, near, beside(far, 1)]

    def gather_cols(summed):
        with jax.named_scope("panel_cols"):
            sent = summed.astype(F16)
            if parts == SLICES:
                return [sent] + [across(sent, j) for j in range(1, parts)]
            return list(lax.all_gather(sent, "cols")[:SLICES])

    def both_cores(mine):
        with jax.named_scope("panel_cores"):
            return [v.astype(F32) for v in mine + [swap(v) for v in mine]]

    mixed = []

    def mix_next(after, count):
        for _ in range(count):
            with jax.named_scope("mix"):
                more, after = mix_tiles(matrix, mixers, kinds, after, len(mixed) * STEP, STEP)
            mixed.append(more)
        return after

    early = names.shape[1] // STEP // 2
    token = mix_next(tiles[0], early)
    held0 = spread(scatter(0), token, carried)
    arrived0 = gather_rows(held0)
    held1 = spread(scatter(1), arrived0[1])
    arrived1 = gather_rows(held1)
    token = mix_next(held1, names.shape[1] // STEP - early)
    with jax.named_scope("panel_sum"):
        summed0, all_names = first_sum(token, arrived0)
    mine0 = gather_cols(summed0)
    with jax.named_scope("panel_sum"):
        summed1 = next_sum(all_names, summed0, arrived1)
    mine1 = gather_cols(summed1)
    pieces0 = both_cores(mine0[:-1] + list(before(mine0[-1:], summed1)))
    with jax.named_scope("cross0"):
        panel0, *crossed0 = cross_parts(names, order, summed1, mixed, pieces0, [], chips, fast)
    with jax.named_scope("factor0"):
        inverse0 = first_factor(first_gram(crossed0[0], panel0))
    pieces1 = both_cores(before(mine1, inverse0, crossed0[0]))
    with jax.named_scope("cross1"):
        panel1, *crossed = cross_parts(names, order, inverse0, mixed, pieces1, crossed0, chips, fast)
    with jax.named_scope("gram1"):
        side, block = second_gram(crossed[0], panel0, panel1)

    if not fast:
        inverse = second_factor(side, side, block, inverse0)
        total = lax.psum(crossed[0], "rows")
        share = P_SIZE // rows_n
        return lax.dynamic_slice_in_dim(nn(inverse, total), row * share, share, 0)
    with jax.named_scope("cross_sum"):
        keep, give = crossed
        on_chip = keep + swap(give)
    with jax.named_scope("factor1"):
        inverse = second_factor(on_chip, side, block, inverse0)
    with jax.named_scope("cross_sum"):
        total = on_chip[0]
        for j in range(1, chips):
            total = total + shift(on_chip[j], j)
    with jax.named_scope("solve"):
        solved = nn(inverse, total)
        return lax.all_to_all(solved, "rows", split_axis=0, concat_axis=1, tiled=True)


def solution(mesh):
    in_specs = (P("rows", "cols"), P(), P("rows", None), P("rows"), P("rows"))
    out_specs = P("rows", "cols")
    return jax.shard_map(local, mesh=mesh, in_specs=in_specs, out_specs=out_specs, check_vma=False)
```

```python
import functools
import jax
import jax.numpy as jnp
from jax import lax
from jax.experimental import pallas as pl
from jax.experimental.pallas import tpu as pltpu
from jax.sharding import PartitionSpec as P

TILE = 128
P_SIZE = 256
NB = 64
CHUNKS = 2
WIDTH = 16
HALF = P_SIZE // CHUNKS
SLICES = HALF // (2 * WIDTH)
BASE = 64
STEP = 8
F32, BF16, F16 = jnp.float32, jnp.bfloat16, jnp.float16
HI = lax.Precision.HIGHEST
MIB = 1 << 20


def vmem():
    return pl.BlockSpec(memory_space=pltpu.VMEM)


def smem():
    return pl.BlockSpec(memory_space=pltpu.SMEM)


def anywhere():
    return pl.BlockSpec(memory_space=pl.ANY)


def params(mib):
    return pltpu.CompilerParams(vmem_limit_bytes=mib * MIB)


def cost(flops, bytes_accessed):
    return pl.CostEstimate(flops=flops, bytes_accessed=bytes_accessed, transcendentals=0)


LIGHT = cost(10**6, 10**5)


def signed_mixer(mixers_ref, names_ref, tile):
    position = lax.broadcasted_iota(jnp.int32, (1, TILE), 1)
    hashed = (names_ref[1, tile] ^ position * 40503) * 69069
    sign = (1 - 2 * (hashed >> 16 & 1)).astype(F32)
    return mixers_ref[names_ref[0, tile]] * sign


def split(value):
    high = value.astype(BF16)
    return high, (value - high.astype(F32)).astype(BF16)


def product(mixer, block):
    mixer_high, mixer_low = split(mixer)
    block_high, block_low = split(block)
    wide = jnp.dot(jnp.concatenate([mixer_high, mixer_low], axis=0), block_high, preferred_element_type=F32)
    low = jnp.dot(mixer_high, block_low, preferred_element_type=F32)
    return wide[:TILE] + (wide[TILE:] + low)


def panel_kernel(per_step, names_ref, order_ref, matrix_ref, mixers_ref, after_ref, *refs):
    outs, turned = refs[:-1], refs[-1]
    first = pl.program_id(0) * per_step
    core = order_ref[2 * SLICES + 1]
    for u in range(per_step):
        mixer = signed_mixer(mixers_ref, names_ref, first + u)
        block = matrix_ref[u * TILE : (u + 1) * TILE, :]
        turned[u] = product(mixer, block).T
        for c in range(SLICES):
            for s in range(2):
                who = core if s == 0 else 1 - core
                start = pl.multiple_of(who * (HALF // 2) + c * WIDTH, WIDTH)
                outs[c][s, u] = turned[u, pl.ds(start, WIDTH), :].astype(BF16)


def mix_panel(matrix, mixers, names, order, after, chunk):
    tiles = names.shape[1]
    per_step = 16
    spec = pl.BlockSpec((2, per_step, WIDTH, TILE), lambda i, *_: (0, i, 0, 0))
    return pl.pallas_call(
        functools.partial(panel_kernel, per_step),
        grid_spec=pltpu.PrefetchScalarGridSpec(
            num_scalar_prefetch=2,
            grid=(tiles // per_step,),
            in_specs=[
                pl.BlockSpec((per_step * TILE, HALF), lambda i, *_: (i, chunk)),
                pl.BlockSpec(mixers.shape, lambda i, *_: (0, 0, 0)),
                anywhere(),
            ],
            out_specs=[spec] * SLICES,
            scratch_shapes=[pltpu.VMEM((per_step, HALF, TILE), F32)],
        ),
        out_shape=[jax.ShapeDtypeStruct((2, tiles, WIDTH, TILE), BF16)] * SLICES,
        compiler_params=params(49),
        cost_estimate=LIGHT,
        name="mix_panel",
    )(names, order, matrix, mixers, after)


def mix_kernel(per_step, start, names_ref, matrix_ref, mixers_ref, after_ref, out_ref, token_ref):
    first = start + pl.program_id(0) * per_step
    for u in range(per_step):
        mixer = signed_mixer(mixers_ref, names_ref, first + u)
        block = matrix_ref[u * TILE : (u + 1) * TILE, :]
        out_ref[u * TILE : (u + 1) * TILE, :] = product(mixer, block).astype(BF16)
    token_ref[...] = jnp.zeros_like(token_ref)


def mix_tiles(matrix, mixers, names, after, start, count):
    cols = matrix.shape[1]
    per_step = 4
    return pl.pallas_call(
        functools.partial(mix_kernel, per_step, start),
        grid_spec=pltpu.PrefetchScalarGridSpec(
            num_scalar_prefetch=1,
            grid=(count // per_step,),
            in_specs=[
                pl.BlockSpec((per_step * TILE, cols), lambda i, *_: (i + start // per_step, 0)),
                pl.BlockSpec(mixers.shape, lambda i, *_: (0, 0, 0)),
                anywhere(),
            ],
            out_specs=[
                pl.BlockSpec((per_step * TILE, cols), lambda i, *_: (i, 0)),
                pl.BlockSpec((8, TILE), lambda i, *_: (0, 0)),
            ],
        ),
        out_shape=[jax.ShapeDtypeStruct((count * TILE, cols), BF16), jax.ShapeDtypeStruct((8, TILE), F32)],
        compiler_params=params(49),
        cost_estimate=LIGHT,
        name="mix_tiles",
    )(names, matrix, mixers, after)


def pick_kernel(count, order_ref, after_ref, *refs):
    extra, sources, (keep_ref, give_ref) = refs[:count], refs[count:-2], refs[-2:]
    part = order_ref[2 * SLICES + 2]
    tiles = sources[0].shape[1]
    for j, source in enumerate(sources):
        taken = part == j if j else (part == 0) | (part >= len(sources))

        @pl.when(taken)
        def copy(source=source):
            keep_ref[:tiles] = source[0]
            give_ref[:tiles] = source[1]

    for i, ref in enumerate(extra):
        keep_ref[tiles + i] = ref[...]
        give_ref[tiles + i] = ref[...]


def pick(order, after, extra, sources):
    tiles = sources[0].shape[1] + len(extra)
    return pl.pallas_call(
        functools.partial(pick_kernel, len(extra)),
        in_specs=[smem(), anywhere()] + [vmem()] * (len(extra) + len(sources)),
        out_specs=[vmem()] * 2,
        out_shape=[jax.ShapeDtypeStruct((tiles, WIDTH, TILE), BF16)] * 2,
        compiler_params=params(16),
        cost_estimate=LIGHT,
        name="pick",
    )(order, after, *extra, *sources)


def add_tiles(names, stride, tiles, pieces, out_ref, total):
    total[...] = jnp.zeros_like(total)
    for j, piece in enumerate(pieces):
        for s in range(2):

            def add(i, carry, j=j, s=s, piece=piece):
                value = piece[s * stride + i].astype(F32)
                one, two = names[2 * j + s, 0, i], names[2 * j + s, 1, i]
                total[one] = total[one] + value
                total[two] = total[two] + names[2 * j + s, 2, i].astype(F32) * value
                return carry

            lax.fori_loop(0, tiles, add, 0, unroll=8)
    summed = total[...]
    largest = jnp.max(jnp.max(jnp.abs(summed), axis=0), axis=1, keepdims=True)
    out_ref[...] = summed * jnp.where(largest > 1e-37, 1.0 / largest, 1.0)


def first_sum_kernel(after_ref, *refs):
    pieces, (out_ref, names_ref, total, names, sem) = refs[:-5], refs[-5:]
    tiles = pieces[0].shape[0] // 2 - 1
    for j, piece in enumerate(pieces):
        for s in range(2):
            names_ref[2 * j + s] = piece[s * (tiles + 1) + tiles].astype(F32)[:8].astype(jnp.int32)
    copy = pltpu.make_async_copy(names_ref, names, sem)
    copy.start()
    copy.wait()
    add_tiles(names, tiles + 1, tiles, pieces, out_ref, total)


def first_sum(after, pieces):
    names = (2 * len(pieces), 8, TILE)
    return pl.pallas_call(
        first_sum_kernel,
        in_specs=[anywhere()] + [vmem()] * len(pieces),
        out_specs=[vmem()] * 2,
        out_shape=[jax.ShapeDtypeStruct((NB, WIDTH, TILE), F32), jax.ShapeDtypeStruct(names, jnp.int32)],
        scratch_shapes=[pltpu.VMEM((NB, WIDTH, TILE), F32), pltpu.SMEM(names, jnp.int32), pltpu.SemaphoreType.DMA],
        compiler_params=params(24),
        cost_estimate=LIGHT,
        name="first_sum",
    )(after, *pieces)


def next_sum_kernel(names, after_ref, *refs):
    pieces, (out_ref, total) = refs[:-2], refs[-2:]
    tiles = pieces[0].shape[0] // 2
    add_tiles(names, tiles, tiles, pieces, out_ref, total)


def next_sum(names, after, pieces):
    return pl.pallas_call(
        next_sum_kernel,
        in_specs=[smem(), anywhere()] + [vmem()] * len(pieces),
        out_specs=vmem(),
        out_shape=jax.ShapeDtypeStruct((NB, WIDTH, TILE), F32),
        scratch_shapes=[pltpu.VMEM((NB, WIDTH, TILE), F32)],
        compiler_params=params(24),
        cost_estimate=LIGHT,
        name="next_sum",
    )(names, after, *pieces)


def nt(a, b, precision=None):
    return lax.dot_general(a, b, (((1,), (1,)), ((), ())), precision=precision, preferred_element_type=F32)


def nn(a, b):
    return jnp.dot(a, b, precision=HI, preferred_element_type=F32)


def join(order_ref, pieces, panel):
    for q, piece in enumerate(pieces):
        panel[:, pl.ds(pl.multiple_of(order_ref[q] * WIDTH, WIDTH), WIDTH), :] = piece[...]


def cross_kernel(steps, chips, earlier, fast, names_ref, order_ref, after_ref, *refs):
    mixed, refs = refs[: len(steps)], refs[len(steps) :]
    pieces, refs = refs[: 2 * SLICES], refs[2 * SLICES :]
    before, refs = refs[:earlier], refs[earlier:]
    panel, outs, total = refs[0], refs[1:-1], refs[-1]
    step = pl.program_id(0)

    @pl.when(step == 0)
    def start():
        total[...] = jnp.zeros_like(total)
        join(order_ref, pieces, panel)

    high, low = [], []
    for u in range(STEP):
        t = STEP * step + u
        one, two = split(panel[names_ref[0, t]] + names_ref[2, t].astype(F32) * panel[names_ref[1, t]])
        high.append(one)
        low.append(two)
    weights = jnp.concatenate([jnp.concatenate(high, axis=1), jnp.concatenate(low, axis=1)], axis=0)

    begin = 0
    for count, mixed_ref in zip(steps, mixed):

        @pl.when((step >= begin) & (step < begin + count))
        def add(mixed_ref=mixed_ref):
            total[...] += jnp.dot(weights, mixed_ref[...], preferred_element_type=F32)

        begin += count

    @pl.when(step == pl.num_programs(0) - 1)
    def finish():
        total[:HALF, :] = total[:HALF, :] + total[HALF:, :]
        rows = earlier and HALF
        for ref, out in zip(before, outs):
            out[..., :HALF, :] = ref[...]
        if not fast:
            outs[0][rows:, :] = total[:HALF, :]
        else:
            chip, core = order_ref[2 * SLICES], order_ref[2 * SLICES + 1]
            for s in range(2):
                who = core if s == 0 else 1 - core
                for j in range(chips):
                    at = (2 * lax.rem(chip + j, chips) + who) * TILE
                    outs[s][j, rows:, :] = total[:HALF, pl.ds(pl.multiple_of(at, TILE), TILE)]


def cross_parts(names, order, after, mixed, pieces, before, chips, fast):
    cols = mixed[0].shape[1]
    steps = [v.shape[0] // (STEP * TILE) for v in mixed]
    rows = 2 * HALF if before else HALF
    if fast:
        outs = [jax.ShapeDtypeStruct((chips, rows, TILE), F32)] * 2
    else:
        outs = [jax.ShapeDtypeStruct((rows, cols), F32)]
    outs = [jax.ShapeDtypeStruct((NB, HALF, TILE), F32)] + outs
    begins = [sum(steps[:i]) for i in range(len(steps))]
    blocks = [
        pl.BlockSpec((STEP * TILE, cols), lambda i, b=begin, n=count: (jnp.clip(i - b, 0, n - 1), 0))
        for begin, count in zip(begins, steps)
    ]
    return pl.pallas_call(
        functools.partial(cross_kernel, steps, chips, len(before), fast),
        grid=(sum(steps),),
        in_specs=[smem(), smem(), anywhere()] + blocks + [vmem()] * (len(pieces) + len(before)),
        out_specs=[vmem()] * len(outs),
        out_shape=outs,
        scratch_shapes=[pltpu.VMEM((2 * HALF, cols), F32)],
        compiler_params=params(32),
        cost_estimate=LIGHT,
        name="cross_parts",
    )(names, order, after, *mixed, *pieces, *before)


def factor_inverse(block):
    row = lax.broadcasted_iota(jnp.int32, (BASE, BASE), 0)
    lane = lax.broadcasted_iota(jnp.int32, (BASE, BASE), 1)
    wide = jnp.concatenate([block, (row == lane).astype(F32)], axis=1)
    slabs = [wide[8 * g : 8 * g + 8, :] for g in range(BASE // 8)]
    place = lax.broadcasted_iota(jnp.int32, (8, 2 * BASE), 0)

    def full(value):
        return jnp.broadcast_to(value, (8, 2 * BASE))

    done = []
    for own in range(BASE // 8):
        slab, first = slabs[own], 8 * own
        cols = [full(slab[:, first + k : first + k + 1]) for k in range(8)]
        rows = [full(slab[k : k + 1, :]) for k in range(8)]
        entry = {(a, b): full(cols[b][a : a + 1, :]) for a in range(8) for b in range(a, 8)}
        factor, scale = {}, []
        for k in range(8):
            scale.append(1.0 / entry[k, k])
            for a in range(k + 1, 8):
                factor[a, k] = entry[k, a] * scale[k]
            for a in range(k + 1, 8):
                for b in range(a, 8):
                    entry[a, b] = entry[a, b] - factor[a, k] * entry[k, b]
                rows[a] = rows[a] - factor[a, k] * rows[k]
        solved = [None] * 8
        for k in reversed(range(8)):
            value = rows[k] * scale[k]
            for m in range(k + 1, 8):
                value = value - factor[m, k] * solved[m]
            solved[k] = value
        for g in range(own + 1, BASE // 8):
            before = slabs[g]
            for k in range(8):
                slabs[g] = slabs[g] - before[:, first + k : first + k + 1] * solved[k]
        out = jnp.zeros((8, 2 * BASE), F32)
        for k in range(8):
            out = jnp.where(place == k, rows[k] * lax.rsqrt(entry[k, k]), out)
        done.append(out)
    return jnp.concatenate(done, axis=0)[:, BASE:]


def factor_inverse_pair(block):
    first = factor_inverse(block[:BASE, :BASE])
    side = nt(block[BASE:, :BASE], first, HI)
    second = factor_inverse(block[BASE:, BASE:] - nt(side, side, HI))
    corner = -nn(second, nn(side, first))
    top = jnp.concatenate([first, jnp.zeros_like(first)], axis=1)
    return jnp.concatenate([top, jnp.concatenate([corner, second], axis=1)], axis=0)


GROUP = 8


def wide_buckets(panel, i):
    return jnp.concatenate([panel[GROUP * i + u] for u in range(GROUP)], axis=1)


def first_kernel(after_ref, panel, out_ref, acc):
    acc[...] = jnp.zeros_like(acc)

    def step(i, carry):
        one, two = split(wide_buckets(panel, i))
        acc[...] += nt(jnp.concatenate([one, two], axis=0), one)
        return carry

    lax.fori_loop(0, NB // GROUP, step, 0)
    mixed = acc[HALF:, :]
    out_ref[...] = acc[:HALF, :] + (mixed + mixed.T)


def first_gram(after, panel):
    return pl.pallas_call(
        first_kernel,
        in_specs=[anywhere(), vmem()],
        out_specs=vmem(),
        out_shape=jax.ShapeDtypeStruct((HALF, HALF), F32),
        scratch_shapes=[pltpu.VMEM((2 * HALF, HALF), F32)],
        compiler_params=params(32),
        cost_estimate=LIGHT,
        name="first_gram",
    )(after, panel)


def factor_kernel(block_ref, out_ref):
    out_ref[...] = factor_inverse_pair(block_ref[...])


def first_factor(block):
    return pl.pallas_call(
        factor_kernel,
        in_specs=[vmem()],
        out_specs=vmem(),
        out_shape=jax.ShapeDtypeStruct((HALF, HALF), F32),
        compiler_params=params(16),
        cost_estimate=LIGHT,
        name="first_factor",
    )(block)


def second_kernel(after_ref, panel0, panel1, side_ref, block_ref, acc, extra):
    acc[...] = jnp.zeros_like(acc)
    extra[...] = jnp.zeros_like(extra)

    def step(i, carry):
        one0, two0 = split(wide_buckets(panel0, i))
        one1, two1 = split(wide_buckets(panel1, i))
        acc[...] += nt(jnp.concatenate([one1, two1], axis=0), jnp.concatenate([one0, one1], axis=0))
        extra[...] += nt(one1, two0)
        return carry

    lax.fori_loop(0, NB // GROUP, step, 0)
    side_ref[...] = acc[:HALF, :HALF] + (acc[HALF:, :HALF] + extra[...])
    mixed = acc[HALF:, HALF:]
    block_ref[...] = acc[:HALF, HALF:] + (mixed + mixed.T)


def second_gram(after, panel0, panel1):
    return pl.pallas_call(
        second_kernel,
        in_specs=[anywhere()] + [vmem()] * 2,
        out_specs=[vmem()] * 2,
        out_shape=[jax.ShapeDtypeStruct((HALF, HALF), F32)] * 2,
        scratch_shapes=[pltpu.VMEM((2 * HALF, 2 * HALF), F32), pltpu.VMEM((HALF, HALF), F32)],
        compiler_params=params(32),
        cost_estimate=LIGHT,
        name="second_gram",
    )(after, panel0, panel1)


def last_kernel(after_ref, side_ref, block_ref, inverse_ref, out_ref):
    first = inverse_ref[...]
    side = nt(side_ref[...], first, HI)
    second = factor_inverse_pair(block_ref[...] - nt(side, side, HI))
    out_ref[:HALF, :HALF] = first
    out_ref[:HALF, HALF:] = jnp.zeros_like(first)
    out_ref[HALF:, :HALF] = -nn(second, nn(side, first))
    out_ref[HALF:, HALF:] = second


def second_factor(after, side, block, inverse):
    return pl.pallas_call(
        last_kernel,
        in_specs=[anywhere()] + [vmem()] * 3,
        out_specs=vmem(),
        out_shape=jax.ShapeDtypeStruct((P_SIZE, P_SIZE), F32),
        compiler_params=params(32),
        cost_estimate=LIGHT,
        name="second_factor",
    )(after, side, block, inverse)


def local(matrix, mixers, bucket_pair, mixer_index, sign_seed):
    cols = matrix.shape[1]
    rows_n, parts = lax.axis_size("rows"), lax.axis_size("cols")
    chips = rows_n // 2
    row, part = lax.axis_index("rows"), lax.axis_index("cols")
    core, chip = row % 2, row // 2

    def swap(value):
        return lax.ppermute(value, "rows", [(i, i ^ 1) for i in range(rows_n)])

    def shift(value, j):
        return lax.ppermute(value, "rows", [(i, (i + 2 * j) % rows_n) for i in range(rows_n)])

    def beside(value, j):
        return lax.ppermute(value, "rows", [(i, i ^ 2 * j) for i in range(rows_n)])

    def across(value, j):
        return lax.ppermute(value, "cols", [(i, i ^ j) for i in range(parts)])

    fast = cols % (TILE * rows_n) == 0
    with jax.named_scope("names"):
        flips = 1 - 2 * (sign_seed >> 29 & 1)
        names = jnp.concatenate([bucket_pair.T, flips[None]])
        kinds = jnp.stack([mixer_index, sign_seed])
        place = [part ^ j if parts == SLICES else j for j in range(SLICES)]
        order = [who * SLICES + c for who in (core, 1 - core) for c in place]
        order = jnp.stack([jnp.asarray(v, jnp.int32) for v in order + [chip, core, part]])
    with jax.named_scope("panel_mix"):
        tiles = mix_panel(matrix, mixers, kinds, order, order, 0)
        tiles = tiles + mix_panel(matrix, mixers, kinds, order, tiles[0], 1)
    with jax.named_scope("names"):
        carried = jnp.pad(names.astype(BF16), ((0, WIDTH - 3), (0, TILE - names.shape[1])))

    def before(values, *others):
        return lax.optimization_barrier((values, others))[0]

    def scatter(h):
        with jax.named_scope("panel_spread"):
            slices = tiles[h * SLICES : (h + 1) * SLICES]
            return [slices[0]] + [lax.ppermute(slices[j], "cols", [(0, j)]) for j in range(1, SLICES)]

    def spread(got, after, *extra):
        with jax.named_scope("panel_spread"):
            keep, give = pick(order, after, extra, got)
            return jnp.concatenate([keep, swap(give)])

    def gather_rows(held, forward):
        with jax.named_scope("panel_rows"):
            if chips != 4:
                return [held] + [shift(held, j) for j in range(1, chips)]
            far, near = beside(held, 2), beside(held, 1)
            return [held, far, near, beside(far, 1) if forward else beside(held, 3)]

    def gather_cols(summed):
        with jax.named_scope("panel_cols"):
            sent = summed.astype(F16)
            if parts == SLICES:
                return [sent] + [across(sent, j) for j in range(1, parts)]
            return list(lax.all_gather(sent, "cols")[:SLICES])

    def both_cores(mine):
        with jax.named_scope("panel_cores"):
            return [v.astype(F32) for v in mine + [swap(v) for v in mine]]

    mixed = []

    def mix_next(after, count):
        for _ in range(count):
            with jax.named_scope("mix"):
                more, after = mix_tiles(matrix, mixers, kinds, after, len(mixed) * STEP, STEP)
            mixed.append(more)
        return after

    early = names.shape[1] // STEP // 2
    token = mix_next(tiles[0], early)
    held0 = spread(scatter(0), token, carried)
    arrived0 = gather_rows(held0, True)
    held1 = spread(scatter(1), arrived0[1])
    arrived1 = gather_rows(held1, False)
    token = mix_next(held1, names.shape[1] // STEP - early)
    with jax.named_scope("panel_sum"):
        summed0, all_names = first_sum(token, arrived0)
    mine0 = gather_cols(summed0)
    with jax.named_scope("panel_sum"):
        summed1 = next_sum(all_names, summed0, arrived1)
    mine1 = gather_cols(summed1)
    pieces0 = both_cores(mine0[:-1] + list(before(mine0[-1:], summed1)))
    with jax.named_scope("cross0"):
        panel0, *crossed0 = cross_parts(names, order, summed1, mixed, pieces0, [], chips, fast)
    with jax.named_scope("factor0"):
        inverse0 = first_factor(first_gram(crossed0[0], panel0))
    pieces1 = both_cores(before(mine1, inverse0, crossed0[0]))
    with jax.named_scope("cross1"):
        panel1, *crossed = cross_parts(names, order, inverse0, mixed, pieces1, crossed0, chips, fast)
    with jax.named_scope("gram1"):
        side, block = second_gram(crossed[0], panel0, panel1)

    if not fast:
        inverse = second_factor(side, side, block, inverse0)
        total = lax.psum(crossed[0], "rows")
        share = P_SIZE // rows_n
        return lax.dynamic_slice_in_dim(nn(inverse, total), row * share, share, 0)
    with jax.named_scope("cross_sum"):
        keep, give = crossed
        on_chip = keep + swap(give)
    with jax.named_scope("factor1"):
        inverse = second_factor(on_chip, side, block, inverse0)
    with jax.named_scope("cross_sum"):
        total = on_chip[0]
        for j in range(1, chips):
            total = total + shift(on_chip[j], j)
    with jax.named_scope("solve"):
        solved = nn(inverse, total)
        return lax.all_to_all(solved, "rows", split_axis=0, concat_axis=1, tiled=True)


def solution(mesh):
    in_specs = (P("rows", "cols"), P(), P("rows", None), P("rows"), P("rows"))
    out_specs = P("rows", "cols")
    return jax.shard_map(local, mesh=mesh, in_specs=in_specs, out_specs=out_specs, check_vma=False)
```

```python
import functools
import jax
import jax.numpy as jnp
from jax import lax
from jax.experimental import pallas as pl
from jax.experimental.pallas import tpu as pltpu
from jax.sharding import PartitionSpec as P

TILE = 128
P_SIZE = 256
NB = 64
CHUNKS = 2
WIDTH = 16
HALF = P_SIZE // CHUNKS
SLICES = HALF // (2 * WIDTH)
BASE = 64
STEP = 8
F32, BF16, F16 = jnp.float32, jnp.bfloat16, jnp.float16
HI = lax.Precision.HIGHEST
MIB = 1 << 20


def vmem():
    return pl.BlockSpec(memory_space=pltpu.VMEM)


def smem():
    return pl.BlockSpec(memory_space=pltpu.SMEM)


def anywhere():
    return pl.BlockSpec(memory_space=pl.ANY)


def params(mib):
    return pltpu.CompilerParams(vmem_limit_bytes=mib * MIB)


def cost(flops, bytes_accessed):
    return pl.CostEstimate(flops=flops, bytes_accessed=bytes_accessed, transcendentals=0)


LIGHT = cost(10**6, 10**5)


def signed_mixer(mixers_ref, names_ref, tile):
    position = lax.broadcasted_iota(jnp.int32, (1, TILE), 1)
    hashed = (names_ref[1, tile] ^ position * 40503) * 69069
    sign = (1 - 2 * (hashed >> 16 & 1)).astype(F32)
    return mixers_ref[names_ref[0, tile]] * sign


def split(value):
    high = value.astype(BF16)
    return high, (value - high.astype(F32)).astype(BF16)


def product(mixer, block):
    mixer_high, mixer_low = split(mixer)
    block_high, block_low = split(block)
    wide = jnp.dot(jnp.concatenate([mixer_high, mixer_low], axis=0), block_high, preferred_element_type=F32)
    low = jnp.dot(mixer_high, block_low, preferred_element_type=F32)
    return wide[:TILE] + (wide[TILE:] + low)


def panel_kernel(per_step, names_ref, order_ref, matrix_ref, mixers_ref, after_ref, *refs):
    outs, turned = refs[:-1], refs[-1]
    first = pl.program_id(0) * per_step
    core = order_ref[2 * SLICES + 1]
    for u in range(per_step):
        mixer = signed_mixer(mixers_ref, names_ref, first + u)
        block = matrix_ref[u * TILE : (u + 1) * TILE, :]
        turned[u] = product(mixer, block).T
        for c in range(SLICES):
            for s in range(2):
                who = core if s == 0 else 1 - core
                start = pl.multiple_of(who * (HALF // 2) + c * WIDTH, WIDTH)
                outs[c][s, u] = turned[u, pl.ds(start, WIDTH), :].astype(BF16)


def mix_panel(matrix, mixers, names, order, after, chunk):
    tiles = names.shape[1]
    per_step = 16
    spec = pl.BlockSpec((2, per_step, WIDTH, TILE), lambda i, *_: (0, i, 0, 0))
    return pl.pallas_call(
        functools.partial(panel_kernel, per_step),
        grid_spec=pltpu.PrefetchScalarGridSpec(
            num_scalar_prefetch=2,
            grid=(tiles // per_step,),
            in_specs=[
                pl.BlockSpec((per_step * TILE, HALF), lambda i, *_: (i, chunk)),
                pl.BlockSpec(mixers.shape, lambda i, *_: (0, 0, 0)),
                anywhere(),
            ],
            out_specs=[spec] * SLICES,
            scratch_shapes=[pltpu.VMEM((per_step, HALF, TILE), F32)],
        ),
        out_shape=[jax.ShapeDtypeStruct((2, tiles, WIDTH, TILE), BF16)] * SLICES,
        compiler_params=params(49),
        cost_estimate=LIGHT,
        name="mix_panel",
    )(names, order, matrix, mixers, after)


def mix_kernel(per_step, start, names_ref, matrix_ref, mixers_ref, after_ref, out_ref, token_ref):
    first = start + pl.program_id(0) * per_step
    for u in range(per_step):
        mixer = signed_mixer(mixers_ref, names_ref, first + u)
        block = matrix_ref[u * TILE : (u + 1) * TILE, :]
        out_ref[u * TILE : (u + 1) * TILE, :] = product(mixer, block).astype(BF16)
    token_ref[...] = jnp.zeros_like(token_ref)


def mix_tiles(matrix, mixers, names, after, start, count):
    cols = matrix.shape[1]
    per_step = 4
    return pl.pallas_call(
        functools.partial(mix_kernel, per_step, start),
        grid_spec=pltpu.PrefetchScalarGridSpec(
            num_scalar_prefetch=1,
            grid=(count // per_step,),
            in_specs=[
                pl.BlockSpec((per_step * TILE, cols), lambda i, *_: (i + start // per_step, 0)),
                pl.BlockSpec(mixers.shape, lambda i, *_: (0, 0, 0)),
                anywhere(),
            ],
            out_specs=[
                pl.BlockSpec((per_step * TILE, cols), lambda i, *_: (i, 0)),
                pl.BlockSpec((8, TILE), lambda i, *_: (0, 0)),
            ],
        ),
        out_shape=[jax.ShapeDtypeStruct((count * TILE, cols), BF16), jax.ShapeDtypeStruct((8, TILE), F32)],
        compiler_params=params(49),
        cost_estimate=LIGHT,
        name="mix_tiles",
    )(names, matrix, mixers, after)


def pick_kernel(count, order_ref, after_ref, *refs):
    extra, sources, (keep_ref, give_ref) = refs[:count], refs[count:-2], refs[-2:]
    part = order_ref[2 * SLICES + 2]
    tiles = sources[0].shape[1]
    for j, source in enumerate(sources):
        taken = part == j if j else (part == 0) | (part >= len(sources))

        @pl.when(taken)
        def copy(source=source):
            keep_ref[:tiles] = source[0]
            give_ref[:tiles] = source[1]

    for i, ref in enumerate(extra):
        keep_ref[tiles + i] = ref[...]
        give_ref[tiles + i] = ref[...]


def pick(order, after, extra, sources):
    tiles = sources[0].shape[1] + len(extra)
    return pl.pallas_call(
        functools.partial(pick_kernel, len(extra)),
        in_specs=[smem(), anywhere()] + [vmem()] * (len(extra) + len(sources)),
        out_specs=[vmem()] * 2,
        out_shape=[jax.ShapeDtypeStruct((tiles, WIDTH, TILE), BF16)] * 2,
        compiler_params=params(16),
        cost_estimate=LIGHT,
        name="pick",
    )(order, after, *extra, *sources)


def add_tiles(names, stride, tiles, pieces, out_ref, total):
    total[...] = jnp.zeros_like(total)
    for j, piece in enumerate(pieces):
        for s in range(2):

            def add(i, carry, j=j, s=s, piece=piece):
                value = piece[s * stride + i].astype(F32)
                one, two = names[2 * j + s, 0, i], names[2 * j + s, 1, i]
                total[one] = total[one] + value
                total[two] = total[two] + names[2 * j + s, 2, i].astype(F32) * value
                return carry

            lax.fori_loop(0, tiles, add, 0, unroll=8)
    summed = total[...]
    largest = jnp.max(jnp.max(jnp.abs(summed), axis=0), axis=1, keepdims=True)
    out_ref[...] = summed * jnp.where(largest > 1e-37, 1.0 / largest, 1.0)


def first_sum_kernel(after_ref, *refs):
    pieces, (out_ref, names_ref, total, names, sem) = refs[:-5], refs[-5:]
    tiles = pieces[0].shape[0] // 2 - 1
    for j, piece in enumerate(pieces):
        for s in range(2):
            names_ref[2 * j + s] = piece[s * (tiles + 1) + tiles].astype(F32)[:8].astype(jnp.int32)
    copy = pltpu.make_async_copy(names_ref, names, sem)
    copy.start()
    copy.wait()
    add_tiles(names, tiles + 1, tiles, pieces, out_ref, total)


def first_sum(after, pieces):
    names = (2 * len(pieces), 8, TILE)
    return pl.pallas_call(
        first_sum_kernel,
        in_specs=[anywhere()] + [vmem()] * len(pieces),
        out_specs=[vmem()] * 2,
        out_shape=[jax.ShapeDtypeStruct((NB, WIDTH, TILE), F32), jax.ShapeDtypeStruct(names, jnp.int32)],
        scratch_shapes=[pltpu.VMEM((NB, WIDTH, TILE), F32), pltpu.SMEM(names, jnp.int32), pltpu.SemaphoreType.DMA],
        compiler_params=params(24),
        cost_estimate=LIGHT,
        name="first_sum",
    )(after, *pieces)


def next_sum_kernel(names, after_ref, *refs):
    pieces, (out_ref, total) = refs[:-2], refs[-2:]
    tiles = pieces[0].shape[0] // 2
    add_tiles(names, tiles, tiles, pieces, out_ref, total)


def next_sum(names, after, pieces):
    return pl.pallas_call(
        next_sum_kernel,
        in_specs=[smem(), anywhere()] + [vmem()] * len(pieces),
        out_specs=vmem(),
        out_shape=jax.ShapeDtypeStruct((NB, WIDTH, TILE), F32),
        scratch_shapes=[pltpu.VMEM((NB, WIDTH, TILE), F32)],
        compiler_params=params(24),
        cost_estimate=LIGHT,
        name="next_sum",
    )(names, after, *pieces)


def nt(a, b, precision=None):
    return lax.dot_general(a, b, (((1,), (1,)), ((), ())), precision=precision, preferred_element_type=F32)


def nn(a, b):
    return jnp.dot(a, b, precision=HI, preferred_element_type=F32)


def join(order_ref, pieces, panel):
    for q, piece in enumerate(pieces):
        panel[:, pl.ds(pl.multiple_of(order_ref[q] * WIDTH, WIDTH), WIDTH), :] = piece[...]


def cross_kernel(steps, chips, earlier, fast, names_ref, order_ref, after_ref, *refs):
    mixed, refs = refs[: len(steps)], refs[len(steps) :]
    pieces, refs = refs[: 2 * SLICES], refs[2 * SLICES :]
    before, refs = refs[:earlier], refs[earlier:]
    panel, outs, total = refs[0], refs[1:-1], refs[-1]
    step = pl.program_id(0)

    @pl.when(step == 0)
    def start():
        total[...] = jnp.zeros_like(total)
        join(order_ref, pieces, panel)

    high, low = [], []
    for u in range(STEP):
        t = STEP * step + u
        one, two = split(panel[names_ref[0, t]] + names_ref[2, t].astype(F32) * panel[names_ref[1, t]])
        high.append(one)
        low.append(two)
    weights = jnp.concatenate([jnp.concatenate(high, axis=1), jnp.concatenate(low, axis=1)], axis=0)

    begin = 0
    for count, mixed_ref in zip(steps, mixed):

        @pl.when((step >= begin) & (step < begin + count))
        def add(mixed_ref=mixed_ref):
            total[...] += jnp.dot(weights, mixed_ref[...], preferred_element_type=F32)

        begin += count

    @pl.when(step == pl.num_programs(0) - 1)
    def finish():
        total[:HALF, :] = total[:HALF, :] + total[HALF:, :]
        rows = earlier and HALF
        for ref, out in zip(before, outs):
            out[..., :HALF, :] = ref[...]
        if not fast:
            outs[0][rows:, :] = total[:HALF, :]
        else:
            chip, core = order_ref[2 * SLICES], order_ref[2 * SLICES + 1]
            for s in range(2):
                who = core if s == 0 else 1 - core
                for j in range(chips):
                    at = (2 * lax.rem(chip + j, chips) + who) * TILE
                    outs[s][j, rows:, :] = total[:HALF, pl.ds(pl.multiple_of(at, TILE), TILE)]


def cross_parts(names, order, after, mixed, pieces, before, chips, fast):
    cols = mixed[0].shape[1]
    steps = [v.shape[0] // (STEP * TILE) for v in mixed]
    rows = 2 * HALF if before else HALF
    if fast:
        outs = [jax.ShapeDtypeStruct((chips, rows, TILE), F32)] * 2
    else:
        outs = [jax.ShapeDtypeStruct((rows, cols), F32)]
    outs = [jax.ShapeDtypeStruct((NB, HALF, TILE), F32)] + outs
    begins = [sum(steps[:i]) for i in range(len(steps))]
    blocks = [
        pl.BlockSpec((STEP * TILE, cols), lambda i, b=begin, n=count: (jnp.clip(i - b, 0, n - 1), 0))
        for begin, count in zip(begins, steps)
    ]
    return pl.pallas_call(
        functools.partial(cross_kernel, steps, chips, len(before), fast),
        grid=(sum(steps),),
        in_specs=[smem(), smem(), anywhere()] + blocks + [vmem()] * (len(pieces) + len(before)),
        out_specs=[vmem()] * len(outs),
        out_shape=outs,
        scratch_shapes=[pltpu.VMEM((2 * HALF, cols), F32)],
        compiler_params=params(32),
        cost_estimate=LIGHT,
        name="cross_parts",
    )(names, order, after, *mixed, *pieces, *before)


def factor_inverse(block):
    row = lax.broadcasted_iota(jnp.int32, (BASE, BASE), 0)
    lane = lax.broadcasted_iota(jnp.int32, (BASE, BASE), 1)
    wide = jnp.concatenate([block, (row == lane).astype(F32)], axis=1)
    slabs = [wide[8 * g : 8 * g + 8, :] for g in range(BASE // 8)]
    place = lax.broadcasted_iota(jnp.int32, (8, 2 * BASE), 0)

    def full(value):
        return jnp.broadcast_to(value, (8, 2 * BASE))

    done = []
    for own in range(BASE // 8):
        slab, first = slabs[own], 8 * own
        cols = [full(slab[:, first + k : first + k + 1]) for k in range(8)]
        rows = [full(slab[k : k + 1, :]) for k in range(8)]
        entry = {(a, b): full(cols[b][a : a + 1, :]) for a in range(8) for b in range(a, 8)}
        factor, scale = {}, []
        for k in range(8):
            scale.append(1.0 / entry[k, k])
            for a in range(k + 1, 8):
                factor[a, k] = entry[k, a] * scale[k]
            for a in range(k + 1, 8):
                for b in range(a, 8):
                    entry[a, b] = entry[a, b] - factor[a, k] * entry[k, b]
                rows[a] = rows[a] - factor[a, k] * rows[k]
        solved = [None] * 8
        for k in reversed(range(8)):
            value = rows[k] * scale[k]
            for m in range(k + 1, 8):
                value = value - factor[m, k] * solved[m]
            solved[k] = value
        for g in range(own + 1, BASE // 8):
            before = slabs[g]
            for k in range(8):
                slabs[g] = slabs[g] - before[:, first + k : first + k + 1] * solved[k]
        out = jnp.zeros((8, 2 * BASE), F32)
        for k in range(8):
            out = jnp.where(place == k, rows[k] * lax.rsqrt(entry[k, k]), out)
        done.append(out)
    return jnp.concatenate(done, axis=0)[:, BASE:]


def factor_inverse_pair(block):
    first = factor_inverse(block[:BASE, :BASE])
    side = nt(block[BASE:, :BASE], first, HI)
    second = factor_inverse(block[BASE:, BASE:] - nt(side, side, HI))
    corner = -nn(second, nn(side, first))
    top = jnp.concatenate([first, jnp.zeros_like(first)], axis=1)
    return jnp.concatenate([top, jnp.concatenate([corner, second], axis=1)], axis=0)


GROUP = 8


def wide_buckets(panel, i):
    return jnp.concatenate([panel[GROUP * i + u] for u in range(GROUP)], axis=1)


def first_kernel(after_ref, panel, out_ref, acc):
    acc[...] = jnp.zeros_like(acc)

    def step(i, carry):
        one, two = split(wide_buckets(panel, i))
        acc[...] += nt(jnp.concatenate([one, two], axis=0), one)
        return carry

    lax.fori_loop(0, NB // GROUP, step, 0)
    mixed = acc[HALF:, :]
    out_ref[...] = acc[:HALF, :] + (mixed + mixed.T)


def first_gram(after, panel):
    return pl.pallas_call(
        first_kernel,
        in_specs=[anywhere(), vmem()],
        out_specs=vmem(),
        out_shape=jax.ShapeDtypeStruct((HALF, HALF), F32),
        scratch_shapes=[pltpu.VMEM((2 * HALF, HALF), F32)],
        compiler_params=params(32),
        cost_estimate=LIGHT,
        name="first_gram",
    )(after, panel)


def factor_kernel(block_ref, out_ref):
    out_ref[...] = factor_inverse_pair(block_ref[...])


def first_factor(block):
    return pl.pallas_call(
        factor_kernel,
        in_specs=[vmem()],
        out_specs=vmem(),
        out_shape=jax.ShapeDtypeStruct((HALF, HALF), F32),
        compiler_params=params(16),
        cost_estimate=LIGHT,
        name="first_factor",
    )(block)


def second_kernel(after_ref, panel0, panel1, side_ref, block_ref, acc, extra):
    acc[...] = jnp.zeros_like(acc)
    extra[...] = jnp.zeros_like(extra)

    def step(i, carry):
        one0, two0 = split(wide_buckets(panel0, i))
        one1, two1 = split(wide_buckets(panel1, i))
        acc[...] += nt(jnp.concatenate([one1, two1], axis=0), jnp.concatenate([one0, one1], axis=0))
        extra[...] += nt(one1, two0)
        return carry

    lax.fori_loop(0, NB // GROUP, step, 0)
    side_ref[...] = acc[:HALF, :HALF] + (acc[HALF:, :HALF] + extra[...])
    mixed = acc[HALF:, HALF:]
    block_ref[...] = acc[:HALF, HALF:] + (mixed + mixed.T)


def second_gram(after, panel0, panel1):
    return pl.pallas_call(
        second_kernel,
        in_specs=[anywhere()] + [vmem()] * 2,
        out_specs=[vmem()] * 2,
        out_shape=[jax.ShapeDtypeStruct((HALF, HALF), F32)] * 2,
        scratch_shapes=[pltpu.VMEM((2 * HALF, 2 * HALF), F32), pltpu.VMEM((HALF, HALF), F32)],
        compiler_params=params(32),
        cost_estimate=LIGHT,
        name="second_gram",
    )(after, panel0, panel1)


def last_kernel(after_ref, side_ref, block_ref, inverse_ref, out_ref):
    first = inverse_ref[...]
    side = nt(side_ref[...], first, HI)
    second = factor_inverse_pair(block_ref[...] - nt(side, side, HI))
    out_ref[:HALF, :HALF] = first
    out_ref[:HALF, HALF:] = jnp.zeros_like(first)
    out_ref[HALF:, :HALF] = -nn(second, nn(side, first))
    out_ref[HALF:, HALF:] = second


def second_factor(after, side, block, inverse):
    return pl.pallas_call(
        last_kernel,
        in_specs=[anywhere()] + [vmem()] * 3,
        out_specs=vmem(),
        out_shape=jax.ShapeDtypeStruct((P_SIZE, P_SIZE), F32),
        compiler_params=params(32),
        cost_estimate=LIGHT,
        name="second_factor",
    )(after, side, block, inverse)


def local(matrix, mixers, bucket_pair, mixer_index, sign_seed):
    cols = matrix.shape[1]
    rows_n, parts = lax.axis_size("rows"), lax.axis_size("cols")
    chips = rows_n // 2
    row, part = lax.axis_index("rows"), lax.axis_index("cols")
    core, chip = row % 2, row // 2

    def swap(value):
        return lax.ppermute(value, "rows", [(i, i ^ 1) for i in range(rows_n)])

    def shift(value, j):
        return lax.ppermute(value, "rows", [(i, (i + 2 * j) % rows_n) for i in range(rows_n)])

    def beside(value, j):
        return lax.ppermute(value, "rows", [(i, i ^ 2 * j) for i in range(rows_n)])

    def across(value, j):
        return lax.ppermute(value, "cols", [(i, i ^ j) for i in range(parts)])

    fast = cols % (TILE * rows_n) == 0
    with jax.named_scope("names"):
        flips = 1 - 2 * (sign_seed >> 29 & 1)
        names = jnp.concatenate([bucket_pair.T, flips[None]])
        kinds = jnp.stack([mixer_index, sign_seed])
        place = [part ^ j if parts == SLICES else j for j in range(SLICES)]
        order = [who * SLICES + c for who in (core, 1 - core) for c in place]
        order = jnp.stack([jnp.asarray(v, jnp.int32) for v in order + [chip, core, part]])
    with jax.named_scope("panel_mix"):
        tiles = mix_panel(matrix, mixers, kinds, order, order, 0)
        tiles = tiles + mix_panel(matrix, mixers, kinds, order, tiles[0], 1)
    with jax.named_scope("names"):
        carried = jnp.pad(names.astype(BF16), ((0, WIDTH - 3), (0, TILE - names.shape[1])))

    def before(values, *others):
        return lax.optimization_barrier((values, others))[0]

    def scatter(h):
        with jax.named_scope("panel_spread"):
            slices = tiles[h * SLICES : (h + 1) * SLICES]
            return [slices[0]] + [lax.ppermute(slices[j], "cols", [(0, j)]) for j in range(1, SLICES)]

    def spread(got, after, *extra):
        with jax.named_scope("panel_spread"):
            keep, give = pick(order, after, extra, got)
            return jnp.concatenate([keep, swap(give)])

    def gather_rows(held, *after):
        with jax.named_scope("panel_rows"):
            if chips != 4:
                return [held] + [shift(held, j) for j in range(1, chips)]
            far, near = beside(held, 2), beside(held, 1)
            return [held, far, near, beside(before(far, *after) if after else far, 1)]

    def gather_cols(summed):
        with jax.named_scope("panel_cols"):
            sent = summed.astype(F16)
            if parts == SLICES:
                return [sent] + [across(sent, j) for j in range(1, parts)]
            return list(lax.all_gather(sent, "cols")[:SLICES])

    def both_cores(mine):
        with jax.named_scope("panel_cores"):
            return [v.astype(F32) for v in mine + [swap(v) for v in mine]]

    mixed = []

    def mix_next(after, count):
        for _ in range(count):
            with jax.named_scope("mix"):
                more, after = mix_tiles(matrix, mixers, kinds, after, len(mixed) * STEP, STEP)
            mixed.append(more)
        return after

    early = names.shape[1] // STEP // 2
    token = mix_next(tiles[0], early)
    held0 = spread(scatter(0), token, carried)
    arrived0 = gather_rows(held0)
    held1 = spread(scatter(1), arrived0[1])
    token = mix_next(held1, names.shape[1] // STEP - early)
    with jax.named_scope("panel_sum"):
        summed0, all_names = first_sum(token, arrived0)
    arrived1 = gather_rows(held1, summed0)
    mine0 = gather_cols(summed0)
    with jax.named_scope("panel_sum"):
        summed1 = next_sum(all_names, summed0, arrived1)
    mine1 = gather_cols(summed1)
    pieces0 = both_cores(mine0[:-1] + list(before(mine0[-1:], summed1)))
    with jax.named_scope("cross0"):
        panel0, *crossed0 = cross_parts(names, order, summed1, mixed, pieces0, [], chips, fast)
    with jax.named_scope("factor0"):
        inverse0 = first_factor(first_gram(crossed0[0], panel0))
    pieces1 = both_cores(before(mine1, inverse0, crossed0[0]))
    with jax.named_scope("cross1"):
        panel1, *crossed = cross_parts(names, order, inverse0, mixed, pieces1, crossed0, chips, fast)
    with jax.named_scope("gram1"):
        side, block = second_gram(crossed[0], panel0, panel1)

    if not fast:
        inverse = second_factor(side, side, block, inverse0)
        total = lax.psum(crossed[0], "rows")
        share = P_SIZE // rows_n
        return lax.dynamic_slice_in_dim(nn(inverse, total), row * share, share, 0)
    with jax.named_scope("cross_sum"):
        keep, give = crossed
        on_chip = keep + swap(give)
    with jax.named_scope("factor1"):
        inverse = second_factor(on_chip, side, block, inverse0)
    with jax.named_scope("cross_sum"):
        total = on_chip[0]
        for j in range(1, chips):
            total = total + shift(on_chip[j], j)
    with jax.named_scope("solve"):
        solved = nn(inverse, total)
        return lax.all_to_all(solved, "rows", split_axis=0, concat_axis=1, tiled=True)


def solution(mesh):
    in_specs = (P("rows", "cols"), P(), P("rows", None), P("rows"), P("rows"))
    out_specs = P("rows", "cols")
    return jax.shard_map(local, mesh=mesh, in_specs=in_specs, out_specs=out_specs, check_vma=False)
```
